256 devices in a mesh: dp: 64 (over z, y, core), mp: 4 (over x).
Axes of the slice: x: 4, y: 4, z: 8, core: 2. Of those that a mesh axis runs over, the one named last changes fastest.
Arguments:
- tokens: bfloat16 [131072, 1024], P('dp'), may hold values from -96 to 96
- doc_ids: int32 [131072], P('dp'), may hold values from 0 to 2047, as said below
- ln_gain: float32 [1024], replicated, may hold values from 0.1 to 1.9
- w_query: bfloat16 [1024, 1024], P(None, 'mp'), may hold values from -16 to 16
- w_key: bfloat16 [1024, 1024], P(None, 'mp'), may hold values from -0.5 to 0.5
- w_value: bfloat16 [1024, 1024], P(None, 'mp'), may hold values from -0.1875 to 0.1875
- w_out: bfloat16 [1024, 1024], P('mp'), may hold values from -0.1875 to 0.1875
- centroids: float32 [65536, 1024], P('dp', 'mp'), may hold values from -6 to 6
- cluster_mass: float32 [65536], P('dp'), may hold values from 0.5 to 4
- assigned: int32 [2048], P('dp'), may hold values from 0 to 65535, as said below
Outputs:
- doc_vectors: float32 [2048, 1024], P('dp', 'mp')
- new_centroids: float32 [65536, 1024], P('dp', 'mp')
The draws below stay inside these ranges and needn't reach their ends.
Inputs may be any that keep to these rules, and one draw needn't show every extreme that they name: `doc_ids`: never falls along the positions. The documents that begin in row r (positions r * 2048 onward) have the ids r * 32 upward without gaps, from 24 to 32 of them, and some row has 32; ids of slots that no document takes never occur. A row begins with its own first document or with the rest of the last document begun in the row before, and row 0 begins with document 0; every document lies within the row where it begins and the next one. `assigned`: centroid c belongs to dp index c // 1024. Among the 32 slots of one row at most 2 name centroids of one dp index; in every row exactly 2 slots that hold documents name centroids of one dp index common to all rows.
All inputs are finite; a program needn't handle non-finite values.
Results may differ from the reference program's by a relative error of at most 0.0024.
Values sent between devices are 32-bit elements; how exact they have to be, the bound alone decides.
A program may use at most 128 MiB of HBM per device.

```python
import math
import jax
import jax.numpy as jnp
from jax import lax

D = 1024
HEADS = 16
HEAD_DIM = 64
ROW_LEN = 2048
DOCS_ROW = 32
CENT_DEV = 1024
TOKENS = 131072
NDOCS = 2048
CENTROIDS = 65536
CAP = 2


def draw_tokens(key, part):
    key_base, key_column, key_row = jax.random.split(jax.random.fold_in(key, 5), 3)
    base = jax.random.truncated_normal(key_base, -4.0, 4.0, (TOKENS, D), jnp.float32)
    row_scale = jnp.exp(jax.random.uniform(key_row, (TOKENS, 1), jnp.float32, math.log(0.5), math.log(2.0)))
    rising = jnp.exp(math.log(10.0) * jnp.arange(D, dtype=jnp.float32) / D)
    jiggle = jnp.exp(jax.random.uniform(key_column, (D,), jnp.float32, -0.35, 0.35))
    column_scale = 0.3 * rising * jiggle
    return (base * column_scale[None, :] * row_scale).astype(jnp.bfloat16)


def projection_pair(key):
    key_first, key_second = jax.random.split(jax.random.fold_in(key, 7), 2)
    w_key = jax.random.truncated_normal(key_first, -6.0, 6.0, (D, D), jnp.float32) / math.sqrt(D)
    w_key = jnp.clip(w_key, -0.5, 0.5)
    noise = jax.random.truncated_normal(key_second, -6.0, 6.0, (D, D), jnp.float32) / math.sqrt(D)
    w_query = noise
    w_query = jnp.clip(w_query, -16.0, 16.0)
    return (w_query, w_key)


def draw_w_query(key, part):
    return projection_pair(key)[0].astype(jnp.bfloat16)


def draw_w_key(key, part):
    return projection_pair(key)[1].astype(jnp.bfloat16)


def draw_doc_ids(key, part):
    row_count = TOKENS // ROW_LEN
    key_used, key_carry, key_jitter = jax.random.split(jax.random.fold_in(key, 11), 3)
    used_docs = jax.random.randint(key_used, (row_count,), 3 * DOCS_ROW // 4, DOCS_ROW + 1).at[0].set(DOCS_ROW)
    carry_len = jax.random.randint(key_carry, (row_count,), 0, ROW_LEN // 4).at[0].set(0)
    stride = (ROW_LEN - carry_len) // used_docs
    slot_index = jnp.arange(DOCS_ROW, dtype=jnp.int32)
    jitter = jax.random.randint(key_jitter, (row_count, DOCS_ROW), 0, jnp.maximum(stride // 2, 1)[:, None])
    jitter = jnp.where(slot_index[None, :] == 0, 0, jitter)
    starts = carry_len[:, None] + slot_index[None, :] * stride[:, None] + jitter
    starts = jnp.where(slot_index[None, :] < used_docs[:, None], starts, ROW_LEN)
    position = jnp.arange(ROW_LEN, dtype=jnp.int32)
    started = jnp.sum((position[None, :, None] >= starts[:, None, :]).astype(jnp.int32), axis=2)
    row_index = jnp.arange(row_count, dtype=jnp.int32)
    own_ids = row_index[:, None] * DOCS_ROW + started - 1
    prior_used = jnp.concatenate([used_docs[:1], used_docs[:-1]])
    previous = (row_index - 1) * DOCS_ROW + prior_used - 1
    ids_all = jnp.where(position[None, :] < carry_len[:, None], previous[:, None], own_ids)
    return ids_all.reshape(-1).astype(jnp.int32)


def draw_assigned(key, part):
    row_count = NDOCS // DOCS_ROW
    key_hot, key_order, key_offset, key_pick = jax.random.split(jax.random.fold_in(key, 23), 4)
    hot_owner = jax.random.randint(key_hot, (), 0, row_count)
    front = 3 * DOCS_ROW // 4
    order_keys = jax.random.split(key_order, row_count)
    orders = jax.vmap(lambda single: jax.random.permutation(single, front))(order_keys)
    slot_index = jnp.arange(DOCS_ROW, dtype=jnp.int32)
    chosen = jnp.sum((orders[:, :CAP][:, :, None] == slot_index[None, None, :]).astype(jnp.int32), axis=1) > 0
    others = jnp.cumsum(1 - chosen.astype(jnp.int32), axis=1) - 1
    offsets = jax.random.randint(key_offset, (row_count, 1), 0, row_count - 1)
    spread_owner = (hot_owner + 1 + (offsets + others) % (row_count - 1)) % row_count
    owners = jnp.where(chosen, hot_owner, spread_owner)
    picks = jax.random.randint(key_pick, (row_count, DOCS_ROW), 0, CENT_DEV)
    return (owners * CENT_DEV + picks).reshape(-1).astype(jnp.int32)


def block_levels(own_key, dims, cuts, least, top_value):
    def one(dim, parts):
        steps = jax.random.uniform(jax.random.fold_in(jax.random.fold_in(own_key, 6), dim), (parts,), jnp.float32, least / len(cuts), top_value / len(cuts))
        return jnp.repeat(jnp.exp(steps), dims[dim] // parts).reshape((-1,) + (1,) * (len(dims) - dim - 1))

    factor_of = one(*cuts[0])
    for cut in cuts[1:]:
        factor_of = factor_of * one(*cut)
    return factor_of


def bell_draw(own_key, extent, width, reach, pieces=(), held_as=jnp.bfloat16):
    drawn = jax.random.normal(own_key, extent, jnp.float32) * width
    if len(pieces) > 0:
        drawn = block_levels(own_key, extent, pieces, -0.22, 0.18) * drawn
    return jnp.clip(drawn, min=-reach, max=reach).astype(held_as)


def setup_inputs(seed: int = 0) -> dict:
    arg_keys = jax.random.split(jax.random.key(seed), 11)
    return {
        "tokens": draw_tokens(jax.random.fold_in(arg_keys[10], 71), 0),
        "doc_ids": draw_doc_ids(jax.random.fold_in(arg_keys[10], 71), 0),
        "ln_gain": jnp.clip(1.0 + 0.18 * jax.random.normal(arg_keys[2], (D,), jnp.float32), 0.1, 1.9),
        "w_query": draw_w_query(jax.random.fold_in(arg_keys[10], 71), 0),
        "w_key": draw_w_key(jax.random.fold_in(arg_keys[10], 71), 0),
        "w_value": bell_draw(arg_keys[5], (D, D), D ** -0.5, 0.1875, ((1, 4),)),
        "w_out": bell_draw(arg_keys[6], (D, D), D ** -0.5, 0.1875, ((0, 4),)),
        "centroids": bell_draw(arg_keys[7], (CENTROIDS, D), 1.0, 6.0, ((0, 64), (1, 4)), jnp.float32),
        "cluster_mass": jnp.clip(jnp.exp(math.log(4.0) - 2.0794415 * jax.random.uniform(arg_keys[8], (CENTROIDS,), jnp.float32) ** block_levels(arg_keys[8], (CENTROIDS,), ((0, 64),), -0.2, 0.2)), 0.5, 4.0),
        "assigned": draw_assigned(jax.random.fold_in(arg_keys[10], 71), 0),
    }


def layer_norm(tokens, ln_gain):
    widened = tokens.astype(jnp.float32)
    average = lax.optimization_barrier(jnp.mean(widened, axis=-1, keepdims=True))
    centered = widened - average
    variance = lax.optimization_barrier(jnp.mean(centered * centered, axis=-1, keepdims=True))
    return (centered * lax.rsqrt(variance + 1e-05) * ln_gain).astype(jnp.bfloat16)

def attend_block(queries, keys_all, values_all, query_ids, row_ids):
    scores = jnp.einsum('qhd,khd->hqk', queries.astype(jnp.float32), keys_all.astype(jnp.float32)) * (1.0 / math.sqrt(HEAD_DIM))
    same_doc = query_ids[:, None] == row_ids[None, :]
    scores = jnp.where(same_doc[None], scores, -1e+30)
    top_score = lax.optimization_barrier(jnp.max(scores, axis=-1, keepdims=True))
    raised = jnp.exp(scores - top_score)
    weights = (raised / lax.optimization_barrier(jnp.sum(raised, axis=-1, keepdims=True))).astype(jnp.bfloat16)
    return jnp.einsum('hqk,khd->qhd', weights.astype(jnp.float32), values_all.astype(jnp.float32)).astype(jnp.bfloat16)

def self_attention(normed, w_query, w_key, w_value, row_ids):
    length = normed.shape[0]

    def project(weight):
        return jnp.dot(normed, weight, preferred_element_type=jnp.float32).astype(jnp.bfloat16).reshape(length, HEADS, HEAD_DIM)
    queries = project(w_query)
    keys_all = project(w_key)
    values_all = project(w_value)
    block_rows = min(512, length)
    query_blocks = queries.reshape(length // block_rows, block_rows, HEADS, HEAD_DIM)
    id_blocks = row_ids.reshape(length // block_rows, block_rows)
    context = lax.map(lambda pair: attend_block(pair[0], keys_all, values_all, pair[1], row_ids), (query_blocks, id_blocks))
    return context.reshape(length, HEADS * HEAD_DIM)

def reference(tokens, doc_ids, ln_gain, w_query, w_key, w_value, w_out, centroids, cluster_mass, assigned):
    row_count = TOKENS // ROW_LEN
    token_rows = tokens.reshape(row_count, ROW_LEN, D)
    id_rows = doc_ids.reshape(row_count, ROW_LEN)

    def add_row(doc_sums, pair):
        row_tokens, row_ids = pair
        normed = layer_norm(row_tokens, ln_gain)
        context = self_attention(normed, w_query, w_key, w_value, row_ids)
        mixed = row_tokens.astype(jnp.float32) + jnp.dot(context, w_out, preferred_element_type=jnp.float32)
        return (doc_sums + jax.ops.segment_sum(mixed, row_ids, num_segments=NDOCS), jnp.float32(0.0))
    doc_sums, ignored = lax.scan(add_row, jnp.zeros((NDOCS, D), jnp.float32), (token_rows, id_rows))
    doc_counts = jax.ops.segment_sum(jnp.ones((TOKENS,), jnp.float32), doc_ids, num_segments=NDOCS)
    averages = doc_sums / jnp.maximum(doc_counts, 1.0)[:, None]
    doc_vectors = averages * lax.rsqrt(lax.optimization_barrier(jnp.mean(averages * averages, axis=1)) + 1e-06)[:, None]
    is_used = (doc_counts > 0).astype(jnp.float32)
    gained = jax.ops.segment_sum(doc_vectors * is_used[:, None], assigned, num_segments=CENTROIDS)
    members = jax.ops.segment_sum(is_used, assigned, num_segments=CENTROIDS)
    blended = cluster_mass[:, None] * centroids + gained
    scaled = blended * lax.rsqrt(lax.optimization_barrier(jnp.mean(blended * blended, axis=1)) + 1e-06)[:, None]
    new_centroids = jnp.where((members > 0)[:, None], scaled, centroids)
    return (doc_vectors, new_centroids)
```

```python
import functools
import math

import jax
import jax.numpy as jnp
from jax import lax
from jax.experimental import pallas as pl
from jax.experimental.pallas import tpu as pltpu
from jax.sharding import PartitionSpec as P

D = 1024
HEAD_DIM = 64
SEGS = 40
WIN = 128
LONG = 512
GROUP = 3
F32 = jnp.float32
BF16 = jnp.bfloat16
MESH = pl.DeviceIdType.MESH
NT = (((1,), (1,)), ((), ()))
NN = (((1,), (0,)), ((), ()))
EXP_SCALE = math.log2(math.e) / math.sqrt(HEAD_DIM)


def iota(shape, dim):
    return lax.broadcasted_iota(jnp.int32, shape, dim)


def halves(x):
    high = x.astype(BF16)
    return high, (x - high.astype(F32)).astype(BF16)


def to_column(row, n):
    full = jnp.broadcast_to(row, (n, n))
    return jnp.sum(jnp.where(iota((n, n), 0) == iota((n, n), 1), full, 0.0), axis=1, keepdims=True)


def to_row(column, n, width):
    full = jnp.broadcast_to(column, (n, width))
    return jnp.sum(jnp.where(iota((n, width), 0) == iota((n, width), 1), full, 0.0), axis=0, keepdims=True)


def pool_weights(p, inverse):
    n = inverse.shape[1]
    high = inverse.astype(BF16).astype(F32)
    low = inverse - high
    row = iota((16, n), 0)
    mine = (row < 4) & ((row & 1) == jnp.where(iota((16, n), 1) < n // 2, 0, 1))
    left = jnp.where(mine, jnp.where(row < 2, high, low), 0.0).astype(BF16)
    return lax.dot_general(left, p, NT, preferred_element_type=F32)


def weigh_values(sums, values):
    high, low = halves(sums)
    got = jnp.dot(high, values, preferred_element_type=F32) + jnp.dot(low, values, preferred_element_type=F32)
    row = iota((16, 128), 0)
    mine = (row & 1) == jnp.where(iota((16, 128), 1) < HEAD_DIM, 0, 1)
    return jnp.sum(jnp.where(mine, got, 0.0), axis=0, keepdims=True)


def rows_kernel(
    ids_ref, assigned_ref, tokens_ref, gain_ref, wq_ref, wk_ref, wv_ref, wo_ref,
    part_ref, carry_ref, cnt_ref, meta_ref, target_ref,
    q_s, k_s, v_s, tok_s, ctx_s, bound_v, bound_s, sc_s, p_s, sem,
):
    step = pl.program_id(0)
    last = pl.num_programs(0) - 1
    chunk = tokens_ref.shape[0]
    length = q_s.shape[0]
    width = wo_ref.shape[0]
    slots = 32
    r = lax.axis_index("dp")
    m = lax.axis_index("mp")

    @pl.when(step == 0)
    def _():
        local = ids_ref[...] - r * slots
        seg = iota((SEGS, length), 0)
        own = seg < slots
        carried = seg == slots
        starts = jnp.sum(jnp.where(own & (local < seg), 1.0, 0.0), axis=1, keepdims=True)
        ends = jnp.sum(
            jnp.where((own & (local <= seg)) | (carried & (local < 0)), 1.0, 0.0), axis=1, keepdims=True
        )
        lane = iota((SEGS, 128), 1)
        bound_v[...] = jnp.where(lane == 0, starts, ends).astype(jnp.int32)
        pltpu.make_async_copy(bound_v, bound_s, sem).start()
        counts = ends - starts
        picks = jnp.where((ends == float(length)) & (starts < float(length)), 1.0, 0.0)
        cnt_ref[...] = jnp.where(lane < 64, counts, picks)
        a_row = assigned_ref[...]
        used_row = to_row(counts[:slots], slots, slots) > 0
        d_row = jnp.where(used_row, ((a_row >> 10) - r) & 63, -1)
        d_col = to_column(d_row.astype(F32), slots)
        before = iota((slots, slots), 0) < iota((slots, slots), 1)
        same = d_col == d_row.astype(F32)
        rank_row = jnp.sum(jnp.where(before & same, 1.0, 0.0), axis=0, keepdims=True)
        spot = iota((64, slots), 0)
        local_row = ((a_row & 1023) + 1).astype(F32)
        here = spot == d_row
        first = jnp.sum(jnp.where(here & (rank_row == 0.0), local_row, 0.0), axis=1, keepdims=True)
        second = jnp.sum(jnp.where(here & (rank_row == 1.0), local_row, 0.0), axis=1, keepdims=True)
        place = (64 - iota((64, 128), 0)) & 63
        lane64 = iota((64, 128), 1)
        target_ref[...] = jnp.where(lane64 == place, first, 0.0) + jnp.where(lane64 == place + 64, second, 0.0)
        pick = (iota((slots, 128), 1) & 31) == iota((slots, 128), 0)
        rank_col = to_column(rank_row, slots)
        d_wide = jnp.sum(jnp.where(pick, d_col, 0.0), axis=0, keepdims=True)
        rank_wide = jnp.sum(jnp.where(pick, rank_col, 0.0), axis=0, keepdims=True)
        meta_ref[...] = jnp.where(iota((8, 128), 0) == 0, d_wide, rank_wide)

    sub = 128
    gain = gain_ref[...]
    low_half = (iota((sub, width), 1) & 127) < HEAD_DIM
    for j in range(chunk // sub):
        x = tokens_ref[j * sub : (j + 1) * sub, :].astype(F32)
        centered = x - jnp.mean(x, axis=1, keepdims=True)
        variance = jnp.mean(centered * centered, axis=1, keepdims=True)
        normed = (centered * lax.rsqrt(variance + 1e-05) * gain).astype(BF16)
        rows = pl.ds(pl.multiple_of(step * chunk + j * sub, sub), sub)
        q = jnp.dot(normed, wq_ref[...], preferred_element_type=F32)
        q_s[rows, 0:width] = jnp.where(low_half, q, 0.0).astype(BF16)
        q_s[rows, width : 2 * width] = jnp.where(low_half, 0.0, q).astype(BF16)
        k_s[rows, :] = jnp.dot(normed, wk_ref[...], preferred_element_type=F32).astype(BF16)
        v_s[rows, :] = jnp.dot(normed, wv_ref[...], preferred_element_type=F32).astype(BF16)

    local = ids_ref[:, pl.ds(pl.multiple_of(step * chunk, chunk), chunk)] - r * slots
    seg_of = jnp.where(local < 0, slots, local)
    member = jnp.where(iota((SEGS, chunk), 0) == seg_of, 1.0, 0.0).astype(BF16)
    columns = pl.ds(pl.multiple_of(m * width, width), width)
    got = jnp.dot(member, tokens_ref[:, columns], preferred_element_type=F32)
    tok_s[...] = jnp.where(step == 0, 0.0, tok_s[...]) + got

    @pl.when(step == last)
    def _():
        pltpu.make_async_copy(bound_v, bound_s, sem).wait()
        ctx_s[slots + 1 :] = jnp.zeros((SEGS - slots - 1, 1, width), F32)
        krow = iota((WIN, 1), 0)
        qlane = iota((1, 2 * WIN), 1) & (WIN - 1)

        def short(seg):
            start = bound_s[seg, 0]
            end = bound_s[seg, 1]
            base = pl.multiple_of(jnp.minimum((start // 16) * 16, length - WIN), 16)
            fits = end - base <= WIN
            stop = jnp.where(fits, end, start)
            bias = jnp.where((krow >= start - base) & (krow < stop - base), 0.0, -1e30)
            valid = (qlane >= start - base) & (qlane < stop - base)
            rows = pl.ds(base, WIN)
            for pair in range(width // 128):
                c0 = pair * 128
                q2 = jnp.concatenate(
                    [q_s[rows, c0 : c0 + 128], q_s[rows, width + c0 : width + c0 + 128]], axis=0
                )
                s = lax.dot_general(k_s[rows, c0 : c0 + 128], q2, NT, preferred_element_type=F32) + bias
                top = jnp.max(s, axis=0, keepdims=True)
                p = jnp.exp2((s - top) * EXP_SCALE)
                total = jnp.sum(p, axis=0, keepdims=True)
                inverse = jnp.where(valid, 1.0 / total, 0.0)
                sums = pool_weights(p.astype(BF16), inverse)
                ctx_s[seg, :, c0 : c0 + 128] = weigh_values(sums, v_s[rows, c0 : c0 + 128])

        @pl.loop(0, (slots + 1) // GROUP)
        def _(group):
            for j in range(GROUP):
                short(group * GROUP + j)

        lrow = iota((LONG, 1), 0)

        @pl.loop(0, slots + 1)
        def _(seg):
            start = bound_s[seg, 0]
            end = bound_s[seg, 1]
            base0 = jnp.minimum((start // 16) * 16, length - WIN)

            @pl.when(end - base0 > WIN)
            def _():
                base = (start // 16) * 16
                n_k = (end - base + LONG - 1) // LONG
                n_q = (end - base + WIN - 1) // WIN

                def k_rows(i):
                    at = pl.multiple_of(jnp.minimum(base + i * LONG, length - LONG), 16)
                    low = jnp.maximum(start, base + i * LONG) - at
                    bias = jnp.where((lrow >= low) & (lrow < end - at), 0.0, -1e30)
                    return pl.ds(at, LONG), pl.ds(pl.multiple_of(i * LONG, LONG), LONG), bias

                @pl.loop(0, n_q)
                def _(iq):
                    qs = base + iq * WIN
                    qat = pl.multiple_of(jnp.minimum(qs, length - WIN), 16)
                    valid = (qlane >= jnp.maximum(start, qs) - qat) & (qlane < end - qat)
                    qrows = pl.ds(qat, WIN)
                    for pair in range(width // 128):
                        c0 = pair * 128
                        q2 = jnp.concatenate(
                            [q_s[qrows, c0 : c0 + 128], q_s[qrows, width + c0 : width + c0 + 128]], axis=0
                        )

                        def scores(i, top):
                            krows, held, bias = k_rows(i)
                            s = lax.dot_general(
                                k_s[krows, c0 : c0 + 128], q2, NT, preferred_element_type=F32
                            ) + bias
                            sc_s[held, :] = s
                            return jnp.maximum(top, jnp.max(s, axis=0, keepdims=True))

                        top = lax.fori_loop(0, n_k, scores, jnp.full((1, 2 * WIN), -2e30, F32))

                        def raise_all(i, total):
                            krows, held, bias = k_rows(i)
                            p = jnp.exp2((sc_s[held, :] - top) * EXP_SCALE)
                            p_s[held, :] = p.astype(BF16)
                            return total + jnp.sum(p, axis=0, keepdims=True)

                        total = lax.fori_loop(0, n_k, raise_all, jnp.zeros((1, 2 * WIN), F32))
                        inverse = jnp.where(valid, 1.0 / total, 0.0)

                        def weigh(i, acc):
                            krows, held, bias = k_rows(i)
                            sums = pool_weights(p_s[held, :], inverse)
                            return acc + weigh_values(sums, v_s[krows, c0 : c0 + 128])

                        acc = lax.fori_loop(0, n_k, weigh, jnp.zeros((1, 128), F32))
                        ctx_s[seg, :, c0 : c0 + 128] += acc

        high, low = halves(ctx_s[...].reshape(SEGS, width))
        out = jnp.dot(high, wo_ref[...], preferred_element_type=F32) + jnp.dot(
            low, wo_ref[...], preferred_element_type=F32
        )
        carried_count = jnp.broadcast_to(bound_s[slots, 1].astype(F32), (8, width))
        row8 = iota((8, width), 0)
        for mm in range(part_ref.shape[0]):
            block = out[:, mm * width : (mm + 1) * width] + jnp.where(m == mm, tok_s[...], 0.0)
            part_ref[mm] = block[:slots]
            carry_ref[mm] = jnp.where(row8 == 1, carried_count, block[slots : slots + 8])


def exchange_kernel(
    dp, mp, part_ref, carry_ref, cnt_ref, meta_ref, target_ref, mass_ref, cent_ref,
    docs_ref, rows_ref, tgt_ref,
    got_part, got_carry, tsend, tgot, ss_send, ss_got, csend, cgot, n_send, n_got, cent_v,
    part_sems, carry_sems, t_sems, ss_sems, c_sems, n_sems, cent_sem,
):
    r = lax.axis_index("dp")
    m = lax.axis_index("mp")
    slots = 32
    cents = cent_v.shape[0]
    width = cent_v.shape[1]
    load = pltpu.make_async_copy(cent_ref, cent_v, cent_sem)
    load.start()

    barrier = pltpu.get_barrier_semaphore()
    nxt = lax.rem(r + 1, dp)
    prv = lax.rem(r + dp - 1, dp)
    for dm in range(1, mp):
        mm = lax.rem(m + dm, mp)
        pl.semaphore_signal(barrier, inc=1, device_id=(r, mm), device_id_type=MESH)
        pl.semaphore_signal(barrier, inc=1, device_id=(nxt, mm), device_id_type=MESH)

    @pl.loop(1, dp)
    def _(d):
        pl.semaphore_signal(barrier, inc=1, device_id=(lax.rem(r + d, dp), m), device_id_type=MESH)

    tsend[...] = target_ref[...].reshape(dp, 1, 128)
    tgot[0] = tsend[0]
    pl.semaphore_wait(barrier, dp - 1 + 2 * (mp - 1))

    def to_peer(src, dst, sems, dm):
        mm = lax.rem(m + dm, mp)
        return pltpu.make_async_remote_copy(
            src_ref=src, dst_ref=dst, send_sem=sems.at[0], recv_sem=sems.at[1],
            device_id=(r, mm), device_id_type=MESH,
        )

    for dm in range(1, mp):
        to_peer(part_ref.at[lax.rem(m + dm, mp)], got_part.at[mp - 1 - dm], part_sems, dm).start()
    for mm in range(mp):
        pltpu.make_async_remote_copy(
            src_ref=carry_ref.at[mm], dst_ref=got_carry.at[m], send_sem=carry_sems.at[0],
            recv_sem=carry_sems.at[1], device_id=(prv, mm), device_id_type=MESH,
        ).start()

    @pl.loop(1, dp)
    def _(d):
        pltpu.make_async_remote_copy(
            src_ref=tsend.at[d], dst_ref=tgot.at[dp - d], send_sem=t_sems.at[0], recv_sem=t_sems.at[1],
            device_id=(lax.rem(r + d, dp), m), device_id_type=MESH,
        ).start()

    d_wide = meta_ref[0:1, :]
    rank_wide = meta_ref[1:2, :]
    row = iota((8 * dp, 128), 0)
    col = iota((8 * dp, 128), 1)
    j = row & 7
    pick = (
        ((row >> 3).astype(F32) == d_wide)
        & ((j >> 1).astype(F32) == rank_wide)
        & ((j & 1) == ((col >> 5) & 1))
    )
    pick = jnp.where(pick, 1.0, 0.0).astype(BF16)

    def wait_all(buffer, sem):
        pltpu.make_async_copy(buffer, buffer, sem).wait()

    wait_all(got_part, part_sems.at[1])
    wait_all(got_carry, carry_sems.at[1])
    sums = part_ref[m]
    for i in range(mp - 1):
        sums = sums + got_part[i]
    carry = got_carry[0]
    for i in range(1, mp):
        carry = carry + got_carry[i]
    count_in = got_carry[0][1:2, :]
    counts = cnt_ref[0:slots, 0:1]
    picks = cnt_ref[0:slots, 64:65]
    sums = sums + picks * carry[0:1, :]
    totals = counts + picks * count_in
    averages = sums / jnp.maximum(totals, 1.0)
    squares = jnp.sum(averages * averages, axis=1, keepdims=True)
    square_row = to_row(squares, slots, 128)
    ss_send[...] = jnp.broadcast_to(square_row, (8, 128))
    for dm in range(1, mp):
        to_peer(ss_send, ss_got.at[mp - 1 - dm], ss_sems, dm).start()
    wait_all(ss_got, ss_sems.at[1])
    for i in range(mp - 1):
        square_row = square_row + ss_got[i][0:1, :]
    eye = iota((slots, 128), 0) == iota((slots, 128), 1)
    squares = jnp.sum(jnp.where(eye, square_row, 0.0), axis=1, keepdims=True)
    vectors = averages * lax.rsqrt(squares * (1.0 / D) + 1e-06)
    docs_ref[...] = vectors

    high, low = halves(vectors)
    high, low = high.astype(F32), low.astype(F32)
    stacked = jnp.concatenate([high[:, :128], high[:, 128:], low[:, :128], low[:, 128:]], axis=0).astype(BF16)
    outgoing = jnp.dot(pick, stacked, preferred_element_type=F32).reshape(dp, 8, 128)
    csend[...] = outgoing[:, :4, :]
    cgot[0] = csend[0]

    @pl.loop(1, dp)
    def _(d):
        pltpu.make_async_remote_copy(
            src_ref=csend.at[d], dst_ref=cgot.at[dp - d], send_sem=c_sems.at[0], recv_sem=c_sems.at[1],
            device_id=(lax.rem(r + d, dp), m), device_id_type=MESH,
        ).start()

    rest = pl.ds(1, dp - 1)
    wait_all(tgot.at[rest], t_sems.at[1])
    tgt_row = jnp.sum(tgot[...], axis=0)
    tgt_col = to_column(tgt_row, 128)
    tgt_ref[...] = jnp.broadcast_to(tgt_row, (8, 128))
    load.wait()
    hits = jnp.where(iota((128, cents), 1).astype(F32) == tgt_col - 1.0, 1.0, 0.0)
    mass = jnp.sum(hits * mass_ref[...], axis=1, keepdims=True)
    hits = hits.astype(BF16)
    cent_high, cent_low = halves(cent_v[...])
    picked = jnp.dot(hits, cent_high, preferred_element_type=F32) + jnp.dot(
        hits, cent_low, preferred_element_type=F32
    )
    start = mass * picked
    together = jnp.where((tgt_col == tgt_row) & (tgt_row > 0.0), 1.0, 0.0).astype(BF16)

    wait_all(cgot.at[rest], c_sems.at[1])
    arrived = jnp.concatenate(
        [
            jnp.concatenate([cgot[:, 2 * k, :], cgot[:, 2 * k + 1, :]], axis=1)
            for k in range(2)
        ],
        axis=0,
    )
    high, low = halves(arrived)
    blended = start + (
        jnp.dot(together, high, preferred_element_type=F32) + jnp.dot(together, low, preferred_element_type=F32)
    )
    norm_row = to_row(jnp.sum(blended * blended, axis=1, keepdims=True), 128, 128)
    n_send[...] = jnp.broadcast_to(norm_row, (8, 128))
    for dm in range(1, mp):
        to_peer(n_send, n_got.at[mp - 1 - dm], n_sems, dm).start()
    wait_all(n_got, n_sems.at[1])
    for i in range(mp - 1):
        norm_row = norm_row + n_got[i][0:1, :]
    norms = to_column(norm_row, 128)
    rows_ref[...] = blended * lax.rsqrt(norms * (1.0 / D) + 1e-06)

    wait_all(got_part, part_sems.at[0])
    wait_all(got_carry, carry_sems.at[0])
    wait_all(tsend.at[rest], t_sems.at[0])
    wait_all(ss_got, ss_sems.at[0])
    wait_all(csend.at[rest], c_sems.at[0])
    wait_all(n_got, n_sems.at[0])


def write_kernel(docs_ref, rows_ref, tgt_ref, cent_ref, docs_out, out_ref):
    step = pl.program_id(0)
    block = cent_ref.shape[0]

    @pl.when(step == 0)
    def _():
        docs_out[...] = docs_ref[...]

    tgt_row = tgt_ref[0:1, :]
    tgt_col = to_column(tgt_row, 128)
    earlier = iota((128, 128), 0) < iota((128, 128), 1)
    repeats = jnp.sum(jnp.where(earlier & (tgt_col == tgt_row), 1.0, 0.0), axis=0, keepdims=True)
    wanted = jnp.where(repeats == 0.0, tgt_row - 1.0, -1.0)
    index = (iota((block, 128), 0) + step * block).astype(F32)
    hits = jnp.where(index == wanted, 1.0, 0.0)
    touched = jnp.sum(hits, axis=1, keepdims=True) > 0.0
    hits = hits.astype(BF16)
    high, low = halves(rows_ref[...])
    new = jnp.dot(hits, high, preferred_element_type=F32) + jnp.dot(hits, low, preferred_element_type=F32)
    out_ref[...] = jnp.where(touched, new, cent_ref[...])


def shards(
    tokens, doc_ids, ln_gain, w_query, w_key, w_value, w_out, centroids, cluster_mass, assigned
):
    length = tokens.shape[0]
    width = w_out.shape[0]
    slots = assigned.shape[0]
    cents = centroids.shape[0]
    dp, mp = lax.axis_size("dp"), lax.axis_size("mp")
    chunk = 256

    def whole(*shape):
        return pl.BlockSpec(shape, lambda i: (0,) * len(shape))

    def shape(*dims):
        return jax.ShapeDtypeStruct(dims, F32)

    part, carry, cnt, meta, target = pl.pallas_call(
        rows_kernel,
        grid=(length // chunk,),
        in_specs=[
            whole(1, length), whole(1, slots), pl.BlockSpec((chunk, D), lambda i: (i, 0)), whole(1, D),
            whole(D, width), whole(D, width), whole(D, width), whole(width, D),
        ],
        out_specs=[whole(mp, slots, width), whole(mp, 8, width), whole(SEGS, 128), whole(8, 128), whole(dp, 128)],
        out_shape=[shape(mp, slots, width), shape(mp, 8, width), shape(SEGS, 128), shape(8, 128), shape(dp, 128)],
        scratch_shapes=[
            pltpu.VMEM((length, 2 * width), BF16),
            pltpu.VMEM((length, width), BF16),
            pltpu.VMEM((length, width), BF16),
            pltpu.VMEM((SEGS, width), F32),
            pltpu.VMEM((SEGS, 1, width), F32),
            pltpu.VMEM((SEGS, 128), jnp.int32),
            pltpu.SMEM((SEGS, 128), jnp.int32),
            pltpu.VMEM((length + LONG, 2 * WIN), F32),
            pltpu.VMEM((length + LONG, 2 * WIN), BF16),
            pltpu.SemaphoreType.DMA,
        ],
        compiler_params=pltpu.CompilerParams(vmem_limit_bytes=48 << 20),
        name="rows",
    )(
        doc_ids.reshape(1, length), assigned.reshape(1, slots), tokens, ln_gain.reshape(1, D),
        w_query, w_key, w_value, w_out,
    )

    vmem = pl.BlockSpec(memory_space=pltpu.VMEM)
    pair = pltpu.SemaphoreType.DMA((2,))
    docs, rows, tgt = pl.pallas_call(
        functools.partial(exchange_kernel, dp, mp),
        in_specs=[vmem] * 6 + [pl.BlockSpec(memory_space=pl.ANY)],
        out_specs=[vmem] * 3,
        out_shape=[shape(slots, width), shape(128, width), shape(8, 128)],
        scratch_shapes=[
            pltpu.VMEM((mp - 1, slots, width), F32),
            pltpu.VMEM((mp, 8, width), F32),
            pltpu.VMEM((dp, 1, 128), F32),
            pltpu.VMEM((dp, 1, 128), F32),
            pltpu.VMEM((8, 128), F32),
            pltpu.VMEM((mp - 1, 8, 128), F32),
            pltpu.VMEM((dp, 4, 128), F32),
            pltpu.VMEM((dp, 4, 128), F32),
            pltpu.VMEM((8, 128), F32),
            pltpu.VMEM((mp - 1, 8, 128), F32),
            pltpu.VMEM((cents, width), F32),
            pair, pair, pair, pair, pair, pair,
            pltpu.SemaphoreType.DMA,
        ],
        compiler_params=pltpu.CompilerParams(
            collective_id=0, has_side_effects=True, vmem_limit_bytes=32 << 20
        ),
        name="exchange",
    )(part, carry, cnt, meta, target, cluster_mass.reshape(1, cents), centroids)

    block = 256
    docs_out, updated = pl.pallas_call(
        write_kernel,
        grid=(cents // block,),
        in_specs=[whole(slots, width), whole(128, width), whole(8, 128), pl.BlockSpec((block, width), lambda i: (i, 0))],
        out_specs=[whole(slots, width), pl.BlockSpec((block, width), lambda i: (i, 0))],
        out_shape=[shape(slots, width), shape(cents, width)],
        name="write",
    )(docs, rows, tgt, centroids)
    return (docs_out, updated)


def solution(mesh):
    placed = (
        P("dp", None),
        P("dp"),
        P(),
        P(None, "mp"),
        P(None, "mp"),
        P(None, "mp"),
        P("mp", None),
        P("dp", "mp"),
        P("dp"),
        P("dp"),
    )
    return jax.shard_map(
        shards,
        mesh=mesh,
        in_specs=placed,
        out_specs=(P("dp", "mp"), P("dp", "mp")),
        check_vma=False,
    )
```

```python
import functools
import math

import jax
import jax.numpy as jnp
from jax import lax
from jax.experimental import pallas as pl
from jax.experimental.pallas import tpu as pltpu
from jax.sharding import PartitionSpec as P

D = 1024
HEAD_DIM = 64
SEGS = 40
WIN = 128
LONG = 512
GROUP = 11
F32 = jnp.float32
BF16 = jnp.bfloat16
MESH = pl.DeviceIdType.MESH
NT = (((1,), (1,)), ((), ()))
NN = (((1,), (0,)), ((), ()))
EXP_SCALE = math.log2(math.e) / math.sqrt(HEAD_DIM)


def iota(shape, dim):
    return lax.broadcasted_iota(jnp.int32, shape, dim)


def halves(x):
    high = x.astype(BF16)
    return high, (x - high.astype(F32)).astype(BF16)


def to_column(row, n):
    full = jnp.broadcast_to(row, (n, n))
    return jnp.sum(jnp.where(iota((n, n), 0) == iota((n, n), 1), full, 0.0), axis=1, keepdims=True)


def to_row(column, n, width):
    full = jnp.broadcast_to(column, (n, width))
    return jnp.sum(jnp.where(iota((n, width), 0) == iota((n, width), 1), full, 0.0), axis=0, keepdims=True)


def block_sums(k, q2, v, bias, valid):
    s = lax.dot_general(k, q2, NT, preferred_element_type=F32) + bias
    top = jnp.max(s, axis=0, keepdims=True)
    p = jnp.exp2((s - top) * EXP_SCALE)
    total = jnp.sum(p, axis=0, keepdims=True)
    weighted = p * jnp.where(valid, 1.0 / total, 0.0)
    first = jnp.sum(weighted[:, :WIN], axis=1, keepdims=True)
    second = jnp.sum(weighted[:, WIN:], axis=1, keepdims=True)
    sums = jnp.where(iota((1, 128), 1) < HEAD_DIM, first, second)
    return jnp.sum(sums * v.astype(F32), axis=0, keepdims=True)


def rows_kernel(
    ids_hbm, assigned_hbm, gain_hbm, tokens_hbm, wq_hbm, wk_hbm, wv_hbm,
    q_ref, k_ref, v_ref, ctx_ref, tok_ref, bound_ref, meta_ref, target_ref,
    ids_v, assigned_v, gain_v, tokens_v, w_v, normed_v, bound_s, sc_s, sems, token_sems, bound_sem,
):
    length = q_ref.shape[0] * 16
    width = k_ref.shape[2]
    slots = 32
    parts = token_sems.shape[0]
    piece = length // parts
    r = lax.axis_index("dp")
    m = lax.axis_index("mp")

    small = [
        pltpu.make_async_copy(src, dst, sems.at[i])
        for i, (src, dst) in enumerate(((ids_hbm, ids_v), (assigned_hbm, assigned_v), (gain_hbm, gain_v)))
    ]
    weights = [
        pltpu.make_async_copy(src, w_v.at[:, i * width : (i + 1) * width], sems.at[3 + i])
        for i, src in enumerate((wq_hbm, wk_hbm, wv_hbm))
    ]
    pieces = [
        pltpu.make_async_copy(
            tokens_hbm.at[pl.ds(i * piece, piece)], tokens_v.at[pl.ds(i * piece, piece)], token_sems.at[i]
        )
        for i in range(parts)
    ]
    for copy in small + pieces[:2] + weights + pieces[2:]:
        copy.start()
    for copy in small:
        copy.wait()

    local = ids_v[...] - r * slots
    seg = iota((SEGS, length), 0)
    own = seg < slots
    carried = seg == slots
    starts = jnp.sum(jnp.where(own & (local < seg), 1.0, 0.0), axis=1, keepdims=True)
    ends = jnp.sum(jnp.where((own & (local <= seg)) | (carried & (local < 0)), 1.0, 0.0), axis=1, keepdims=True)
    lane = iota((SEGS, 128), 1)
    at_row = jnp.minimum(jnp.floor(starts * (1.0 / 16.0)) * 16.0, float(length - WIN))
    fits = ends - at_row <= float(WIN)
    bound_ref[...] = jnp.where(
        lane == 0,
        starts,
        jnp.where(lane == 1, ends, jnp.where(lane == 2, at_row * (1.0 / 16.0), jnp.where(lane == 3, starts - at_row, jnp.where(fits, ends, starts) - at_row))),
    ).astype(jnp.int32)
    to_scalars = pltpu.make_async_copy(bound_ref, bound_s, bound_sem)
    to_scalars.start()
    counts = ends - starts
    picks = jnp.where((ends == float(length)) & (starts < float(length)), 1.0, 0.0)
    meta_ref[8:, :] = jnp.where(lane < 64, counts, picks)
    a_row = assigned_v[...]
    used_row = to_row(counts[:slots], slots, slots) > 0
    d_row = jnp.where(used_row, ((a_row >> 10) - r) & 63, -1)
    d_col = to_column(d_row.astype(F32), slots)
    before = iota((slots, slots), 0) < iota((slots, slots), 1)
    same = d_col == d_row.astype(F32)
    rank_row = jnp.sum(jnp.where(before & same, 1.0, 0.0), axis=0, keepdims=True)
    spot = iota((64, slots), 0)
    local_row = ((a_row & 1023) + 1).astype(F32)
    here = spot == d_row
    first = jnp.sum(jnp.where(here & (rank_row == 0.0), local_row, 0.0), axis=1, keepdims=True)
    second = jnp.sum(jnp.where(here & (rank_row == 1.0), local_row, 0.0), axis=1, keepdims=True)
    place = (64 - iota((64, 128), 0)) & 63
    lane64 = iota((64, 128), 1)
    target_ref[...] = jnp.where(lane64 == place, first, 0.0) + jnp.where(lane64 == place + 64, second, 0.0)
    pick = (iota((slots, 128), 1) & 31) == iota((slots, 128), 0)
    rank_col = to_column(rank_row, slots)
    d_wide = jnp.sum(jnp.where(pick, d_col, 0.0), axis=0, keepdims=True)
    rank_wide = jnp.sum(jnp.where(pick, rank_col, 0.0), axis=0, keepdims=True)
    meta_ref[:8, :] = jnp.where(iota((8, 128), 0) == 0, d_wide, rank_wide)
    ctx_ref[...] = jnp.zeros_like(ctx_ref)

    half = length // 2
    gain = gain_v[...]
    low_half = (iota((half, width), 1) & 127) < HEAD_DIM

    def norm(i):
        rows = slice(i * piece, (i + 1) * piece)
        x = tokens_v[rows, :].astype(F32)
        centered = x - jnp.mean(x, axis=1, keepdims=True)
        variance = jnp.mean(centered * centered, axis=1, keepdims=True)
        normed_v[rows, :] = (centered * lax.rsqrt(variance + 1e-05) * gain).astype(BF16)

    def project(i):
        rows = slice(i * half, (i + 1) * half)
        blocks = slice(i * half // 16, (i + 1) * half // 16)
        out = jnp.dot(normed_v[rows, :], w_v[...], preferred_element_type=F32)
        q = out[:, :width]
        q_ref[blocks, :, 0:width] = jnp.where(low_half, q, 0.0).astype(BF16).reshape(half // 16, 16, width)
        q_ref[blocks, :, width : 2 * width] = jnp.where(low_half, 0.0, q).astype(BF16).reshape(half // 16, 16, width)
        k_ref[blocks] = out[:, width : 2 * width].astype(BF16).reshape(half // 16, 16, width)
        v_ref[blocks] = out[:, 2 * width :].astype(BF16).reshape(half // 16, 16, width)

    for i in range(parts // 2):
        pieces[i].wait()
        norm(i)
    for copy in weights + pieces[parts // 2 :]:
        copy.wait()
    project(0)
    for i in range(parts // 2, parts):
        norm(i)
    project(1)

    seg_of = jnp.where(local < 0, slots, local)
    member = jnp.where(seg == seg_of, 1.0, 0.0).astype(BF16)
    columns = pl.ds(pl.multiple_of(m * width, width), width)
    tok_ref[...] = jnp.dot(member, tokens_v[:, columns], preferred_element_type=F32)

    to_scalars.wait()
    qlane = iota((1, 2 * WIN), 1) & (WIN - 1)

    def taken(ref, at, n, c0):
        return ref[pl.ds(at // 16, n // 16), :, c0 : c0 + 128].reshape(n, 128)

    def queries(at, c0):
        return jnp.concatenate([taken(q_ref, at, WIN, c0), taken(q_ref, at, WIN, width + c0)], axis=0)

    def long(seg, start, end, reach):
        first = (start // 16) * 16
        base = pl.multiple_of(jnp.minimum(first, length - reach), 16)
        row = iota((reach, 1), 0)
        bias = jnp.where((row >= start - base) & (row < end - base), 0.0, -1e30)

        @pl.loop(0, (end - first + WIN - 1) // WIN)
        def _(i):
            qs = first + i * WIN
            at = pl.multiple_of(jnp.minimum(qs, length - WIN), 16)
            valid = (qlane >= jnp.maximum(start, qs) - at) & (qlane < end - at)
            for pair in range(width // 128):
                c0 = pair * 128
                ctx_ref[seg, :, c0 : c0 + 128] += block_sums(
                    taken(k_ref, base, reach, c0), queries(at, c0), taken(v_ref, base, reach, c0), bias, valid
                )

    def longest(seg, start, end):
        first = (start // 16) * 16
        n_k = (end - first + LONG - 1) // LONG
        row = iota((LONG, 1), 0)

        def k_rows(i):
            at = pl.multiple_of(jnp.minimum(first + i * LONG, length - LONG), 16)
            low = jnp.maximum(start, first + i * LONG) - at
            bias = jnp.where((row >= low) & (row < end - at), 0.0, -1e30)
            return at, pl.ds(pl.multiple_of(i * LONG, LONG), LONG), bias

        @pl.loop(0, (end - first + WIN - 1) // WIN)
        def _(iq):
            qs = first + iq * WIN
            qat = pl.multiple_of(jnp.minimum(qs, length - WIN), 16)
            valid = (qlane >= jnp.maximum(start, qs) - qat) & (qlane < end - qat)
            for pair in range(width // 128):
                c0 = pair * 128
                q2 = queries(qat, c0)

                def scores(i, top):
                    krows, held, bias = k_rows(i)
                    s = lax.dot_general(taken(k_ref, krows, LONG, c0), q2, NT, preferred_element_type=F32) + bias
                    sc_s[held, :] = s
                    return jnp.maximum(top, jnp.max(s, axis=0, keepdims=True))

                top = lax.fori_loop(0, n_k, scores, jnp.full((1, 2 * WIN), -2e30, F32))

                def raise_all(i, total):
                    krows, held, bias = k_rows(i)
                    p = jnp.exp2((sc_s[held, :] - top) * EXP_SCALE)
                    sc_s[held, :] = p
                    return total + jnp.sum(p, axis=0, keepdims=True)

                total = lax.fori_loop(0, n_k, raise_all, jnp.zeros((1, 2 * WIN), F32))
                inverse = jnp.where(valid, 1.0 / total, 0.0)

                def weigh(i, acc):
                    krows, held, bias = k_rows(i)
                    weighted = sc_s[held, :] * inverse
                    one = jnp.sum(weighted[:, :WIN], axis=1, keepdims=True)
                    two = jnp.sum(weighted[:, WIN:], axis=1, keepdims=True)
                    sums = jnp.where(iota((1, 128), 1) < HEAD_DIM, one, two)
                    return acc + jnp.sum(sums * taken(v_ref, krows, LONG, c0).astype(F32), axis=0, keepdims=True)

                ctx_ref[seg, :, c0 : c0 + 128] += lax.fori_loop(0, n_k, weigh, jnp.zeros((1, 128), F32))

    @pl.loop(0, slots + 1)
    def _(seg):
        start = bound_s[seg, 0]
        end = bound_s[seg, 1]
        first = (start // 16) * 16

        @pl.when(end - jnp.minimum(first, length - WIN) > WIN)
        def _():
            @pl.when(end - first <= 256)
            def _():
                long(seg, start, end, 256)

            @pl.when((end - first > 256) & (end - first <= 512))
            def _():
                long(seg, start, end, 512)

            @pl.when(end - first > 512)
            def _():
                longest(seg, start, end)


def exchange_kernel(
    dp, mp, q_ref, k_ref, v_ref, ctx_ref, tok_ref, bound_ref, meta_ref, target_ref, mass_ref, wo_ref, cent_ref,
    docs_ref, out_ref,
    bound_s, ctx_s, part_s, carry_s, got_part, got_carry, tsend, tgot, ss_send, ss_got, csend, cgot, n_send, n_got,
    bound_sem, part_sems, carry_sems, t_sems, ss_sems, c_sems, n_sems,
):
    r = lax.axis_index("dp")
    m = lax.axis_index("mp")
    slots = 32
    cents, width = cent_ref.shape
    to_scalars = pltpu.make_async_copy(bound_ref, bound_s, bound_sem)
    to_scalars.start()

    barrier = pltpu.get_barrier_semaphore()
    nxt = lax.rem(r + 1, dp)
    prv = lax.rem(r + dp - 1, dp)
    for dm in range(1, mp):
        mm = lax.rem(m + dm, mp)
        pl.semaphore_signal(barrier, inc=1, device_id=(r, mm), device_id_type=MESH)
        pl.semaphore_signal(barrier, inc=1, device_id=(nxt, mm), device_id_type=MESH)

    @pl.loop(1, dp)
    def _(d):
        pl.semaphore_signal(barrier, inc=1, device_id=(lax.rem(r + d, dp), m), device_id_type=MESH)

    tsend[...] = target_ref[...].reshape(dp, 1, 128)
    tgot[0] = tsend[0]
    ctx_s[slots + 1 :] = jnp.zeros((SEGS - slots - 1, 1, width), F32)
    to_scalars.wait()
    krow = iota((WIN, 1), 0)
    qlane = iota((1, 2 * WIN), 1) & (WIN - 1)

    def short(seg):
        block = bound_s[seg, 2]
        low = bound_s[seg, 3]
        high = bound_s[seg, 4]
        bias = jnp.where((krow >= low) & (krow < high), 0.0, -1e30)
        valid = (qlane >= low) & (qlane < high)
        q = jnp.concatenate([q_ref[block + i] for i in range(WIN // 16)], axis=0)
        k = jnp.concatenate([k_ref[block + i] for i in range(WIN // 16)], axis=0)
        v = jnp.concatenate([v_ref[block + i] for i in range(WIN // 16)], axis=0)
        for pair in range(width // 128):
            c0 = pair * 128
            q2 = jnp.concatenate([q[:, c0 : c0 + 128], q[:, width + c0 : width + c0 + 128]], axis=0)
            ctx_s[seg, :, c0 : c0 + 128] = ctx_ref[seg, :, c0 : c0 + 128] + block_sums(
                k[:, c0 : c0 + 128], q2, v[:, c0 : c0 + 128], bias, valid
            )

    def to_peer(src, dst, sems, dm):
        mm = lax.rem(m + dm, mp)
        return pltpu.make_async_remote_copy(
            src_ref=src, dst_ref=dst, send_sem=sems.at[0], recv_sem=sems.at[1],
            device_id=(r, mm), device_id_type=MESH,
        )

    def wait_all(buffer, sem):
        pltpu.make_async_copy(buffer, buffer, sem).wait()

    def out_project(rows):
        high, low = halves(rows)
        return jnp.dot(high, wo_ref[...], preferred_element_type=F32) + jnp.dot(
            low, wo_ref[...], preferred_element_type=F32
        )

    groups = (slots + 1) // GROUP

    @pl.loop(0, groups - 1)
    def _(group):
        for j in range(GROUP):
            short(slots - group * GROUP - j)

    carried = out_project(ctx_s[slots:].reshape(SEGS - slots, width))
    row8 = iota((8, width), 0)
    carried_count = meta_ref[8 + slots : 9 + slots, 0:1]
    for mm in range(mp):
        block = carried[:, mm * width : (mm + 1) * width] + jnp.where(m == mm, tok_ref[slots:, :], 0.0)
        carry_s[mm] = jnp.where(row8 == 1, carried_count, block)

    pl.semaphore_wait(barrier, dp - 1 + 2 * (mp - 1))
    for mm in range(mp):
        pltpu.make_async_remote_copy(
            src_ref=carry_s.at[mm], dst_ref=got_carry.at[m], send_sem=carry_sems.at[0],
            recv_sem=carry_sems.at[1], device_id=(prv, mm), device_id_type=MESH,
        ).start()

    @pl.loop(1, dp)
    def _(d):
        pltpu.make_async_remote_copy(
            src_ref=tsend.at[d], dst_ref=tgot.at[dp - d], send_sem=t_sems.at[0], recv_sem=t_sems.at[1],
            device_id=(lax.rem(r + d, dp), m), device_id_type=MESH,
        ).start()

    for j in range(GROUP):
        short(GROUP - 1 - j)

    projected = out_project(ctx_s[:slots].reshape(slots, width))
    for mm in range(mp):
        part_s[mm] = projected[:, mm * width : (mm + 1) * width] + jnp.where(m == mm, tok_ref[:slots, :], 0.0)
    for dm in range(1, mp):
        to_peer(part_s.at[lax.rem(m + dm, mp)], got_part.at[mp - 1 - dm], part_sems, dm).start()

    d_wide = meta_ref[0:1, :]
    rank_wide = meta_ref[1:2, :]
    row = iota((8 * dp, 128), 0)
    col = iota((8 * dp, 128), 1)
    j = row & 7
    pick = (
        ((row >> 3).astype(F32) == d_wide)
        & ((j >> 1).astype(F32) == rank_wide)
        & ((j & 1) == ((col >> 5) & 1))
    )
    pick = jnp.where(pick, 1.0, 0.0).astype(BF16)

    wait_all(got_carry, carry_sems.at[1])
    carry = got_carry[0]
    for i in range(1, mp):
        carry = carry + got_carry[i]
    count_in = got_carry[0][1:2, :]
    counts = meta_ref[8 : 8 + slots, 0:1]
    picks = meta_ref[8 : 8 + slots, 64:65]
    sums = part_s[m] + picks * carry[0:1, :]
    inverse = 1.0 / jnp.maximum(counts + picks * count_in, 1.0)
    wait_all(got_part, part_sems.at[1])
    for i in range(mp - 1):
        sums = sums + got_part[i]
    averages = sums * inverse
    squares = jnp.sum(averages * averages, axis=1, keepdims=True)
    square_row = to_row(squares, slots, 128)
    ss_send[...] = jnp.broadcast_to(square_row, (8, 128))
    for dm in range(1, mp):
        to_peer(ss_send, ss_got.at[mp - 1 - dm], ss_sems, dm).start()
    wait_all(ss_got, ss_sems.at[1])
    for i in range(mp - 1):
        square_row = square_row + ss_got[i][0:1, :]
    eye = iota((slots, 128), 0) == iota((slots, 128), 1)
    squares = jnp.sum(jnp.where(eye, square_row, 0.0), axis=1, keepdims=True)
    vectors = averages * lax.rsqrt(squares * (1.0 / D) + 1e-06)

    high, low = halves(vectors)
    high, low = high.astype(F32), low.astype(F32)
    stacked = jnp.concatenate([high[:, :128], high[:, 128:], low[:, :128], low[:, 128:]], axis=0).astype(BF16)
    outgoing = jnp.dot(pick, stacked, preferred_element_type=F32).reshape(dp, 8, 128)
    csend[...] = outgoing[:, :4, :]
    cgot[0] = csend[0]

    @pl.loop(1, dp)
    def _(d):
        pltpu.make_async_remote_copy(
            src_ref=csend.at[d], dst_ref=cgot.at[dp - d], send_sem=c_sems.at[0], recv_sem=c_sems.at[1],
            device_id=(lax.rem(r + d, dp), m), device_id_type=MESH,
        ).start()

    docs_ref[...] = vectors

    rest = pl.ds(1, dp - 1)
    wait_all(tgot.at[rest], t_sems.at[1])
    tgt_row = jnp.sum(tgot[...], axis=0)
    tgt_col = to_column(tgt_row, 128)
    hits = jnp.where(iota((128, cents), 1).astype(F32) == tgt_col - 1.0, 1.0, 0.0)
    mass = jnp.sum(hits * mass_ref[...], axis=1, keepdims=True)
    hits = hits.astype(BF16)
    cent_high, cent_low = halves(cent_ref[...])
    picked = jnp.dot(hits, cent_high, preferred_element_type=F32) + jnp.dot(
        hits, cent_low, preferred_element_type=F32
    )
    start = mass * picked
    together = jnp.where((tgt_col == tgt_row) & (tgt_row > 0.0), 1.0, 0.0).astype(BF16)
    earlier = iota((128, 128), 0) < iota((128, 128), 1)
    repeats = jnp.sum(jnp.where(earlier & (tgt_col == tgt_row), 1.0, 0.0), axis=0, keepdims=True)
    wanted = jnp.where(repeats == 0.0, tgt_row - 1.0, -1.0)
    writes = jnp.where(iota((cents, 128), 0).astype(F32) == wanted, 1.0, 0.0)
    out_ref[...] = jnp.where(jnp.sum(writes, axis=1, keepdims=True) > 0.0, 0.0, cent_ref[...])
    writes = writes.astype(BF16)

    wait_all(cgot.at[rest], c_sems.at[1])
    arrived = jnp.concatenate(
        [jnp.concatenate([cgot[:, 2 * k, :], cgot[:, 2 * k + 1, :]], axis=1) for k in range(2)], axis=0
    )
    high, low = halves(arrived)
    blended = start + (
        jnp.dot(together, high, preferred_element_type=F32) + jnp.dot(together, low, preferred_element_type=F32)
    )
    norm_row = to_row(jnp.sum(blended * blended, axis=1, keepdims=True), 128, 128)
    n_send[...] = jnp.broadcast_to(norm_row, (8, 128))
    for dm in range(1, mp):
        to_peer(n_send, n_got.at[mp - 1 - dm], n_sems, dm).start()
    wait_all(n_got, n_sems.at[1])
    for i in range(mp - 1):
        norm_row = norm_row + n_got[i][0:1, :]
    norms = to_column(norm_row, 128)
    high, low = halves(blended * lax.rsqrt(norms * (1.0 / D) + 1e-06))
    out_ref[...] += jnp.dot(writes, high, preferred_element_type=F32) + jnp.dot(
        writes, low, preferred_element_type=F32
    )

    wait_all(got_part, part_sems.at[0])
    wait_all(carry_s, carry_sems.at[0])
    wait_all(tsend.at[rest], t_sems.at[0])
    wait_all(ss_got, ss_sems.at[0])
    wait_all(csend.at[rest], c_sems.at[0])
    wait_all(n_got, n_sems.at[0])


def shards(
    tokens, doc_ids, ln_gain, w_query, w_key, w_value, w_out, centroids, cluster_mass, assigned
):
    length = tokens.shape[0]
    width = w_out.shape[0]
    slots = assigned.shape[0]
    cents = centroids.shape[0]
    dp, mp = lax.axis_size("dp"), lax.axis_size("mp")

    def shape(*dims, dtype=F32):
        return jax.ShapeDtypeStruct(dims, dtype)

    vmem = pl.BlockSpec(memory_space=pltpu.VMEM)
    held = pl.pallas_call(
        rows_kernel,
        in_specs=[pl.BlockSpec(memory_space=pltpu.HBM)] * 7,
        out_specs=[vmem] * 8,
        out_shape=[
            shape(length // 16, 16, 2 * width, dtype=BF16),
            shape(length // 16, 16, width, dtype=BF16),
            shape(length // 16, 16, width, dtype=BF16),
            shape(SEGS, 1, width),
            shape(SEGS, width),
            shape(SEGS, 128, dtype=jnp.int32),
            shape(8 + SEGS, 128),
            shape(dp, 128),
        ],
        scratch_shapes=[
            pltpu.VMEM((1, length), jnp.int32),
            pltpu.VMEM((1, slots), jnp.int32),
            pltpu.VMEM((1, D), F32),
            pltpu.VMEM((length, D), BF16),
            pltpu.VMEM((D, 3 * width), BF16),
            pltpu.VMEM((length, D), BF16),
            pltpu.SMEM((SEGS, 128), jnp.int32),
            pltpu.VMEM((length + LONG, 2 * WIN), F32),
            pltpu.SemaphoreType.DMA((6,)),
            pltpu.SemaphoreType.DMA((8,)),
            pltpu.SemaphoreType.DMA,
        ],
        compiler_params=pltpu.CompilerParams(vmem_limit_bytes=40 << 20),
        name="rows",
    )(
        *[pltpu.with_memory_space_constraint(x, pltpu.HBM) for x in (
            doc_ids.reshape(1, length), assigned.reshape(1, slots), ln_gain.reshape(1, D), tokens,
            w_query, w_key, w_value)]
    )

    pair = pltpu.SemaphoreType.DMA((2,))
    return pl.pallas_call(
        functools.partial(exchange_kernel, dp, mp),
        in_specs=[vmem] * 11,
        out_specs=[vmem] * 2,
        out_shape=[shape(slots, width), shape(cents, width)],
        scratch_shapes=[
            pltpu.SMEM((SEGS, 128), jnp.int32),
            pltpu.VMEM((SEGS, 1, width), F32),
            pltpu.VMEM((mp, slots, width), F32),
            pltpu.VMEM((mp, 8, width), F32),
            pltpu.VMEM((mp - 1, slots, width), F32),
            pltpu.VMEM((mp, 8, width), F32),
            pltpu.VMEM((dp, 1, 128), F32),
            pltpu.VMEM((dp, 1, 128), F32),
            pltpu.VMEM((8, 128), F32),
            pltpu.VMEM((mp - 1, 8, 128), F32),
            pltpu.VMEM((dp, 4, 128), F32),
            pltpu.VMEM((dp, 4, 128), F32),
            pltpu.VMEM((8, 128), F32),
            pltpu.VMEM((mp - 1, 8, 128), F32),
            pltpu.SemaphoreType.DMA,
            pair, pair, pair, pair, pair, pair,
        ],
        compiler_params=pltpu.CompilerParams(
            collective_id=0, has_side_effects=True, vmem_limit_bytes=24 << 20
        ),
        name="exchange",
    )(*held, cluster_mass.reshape(1, cents), w_out, centroids)


def solution(mesh):
    placed = (
        P("dp", None),
        P("dp"),
        P(),
        P(None, "mp"),
        P(None, "mp"),
        P(None, "mp"),
        P("mp", None),
        P("dp", "mp"),
        P("dp"),
        P("dp"),
    )
    return jax.shard_map(
        shards,
        mesh=mesh,
        in_specs=placed,
        out_specs=(P("dp", "mp"), P("dp", "mp")),
        check_vma=False,
    )
```

```python
import functools
import math

import jax
import jax.numpy as jnp
from jax import lax
from jax.experimental import pallas as pl
from jax.experimental.pallas import tpu as pltpu
from jax.sharding import PartitionSpec as P

D = 1024
HEAD_DIM = 64
SEGS = 40
WIN = 128
LONG = 512
GROUP = 8
F32 = jnp.float32
BF16 = jnp.bfloat16
MESH = pl.DeviceIdType.MESH
NT = (((1,), (1,)), ((), ()))
NN = (((1,), (0,)), ((), ()))
EXP_SCALE = math.log2(math.e) / math.sqrt(HEAD_DIM)


def iota(shape, dim):
    return lax.broadcasted_iota(jnp.int32, shape, dim)


def halves(x):
    high = x.astype(BF16)
    return high, (x - high.astype(F32)).astype(BF16)


def to_column(row, n):
    full = jnp.broadcast_to(row, (n, n))
    return jnp.sum(jnp.where(iota((n, n), 0) == iota((n, n), 1), full, 0.0), axis=1, keepdims=True)


def to_row(column, n, width):
    full = jnp.broadcast_to(column, (n, width))
    return jnp.sum(jnp.where(iota((n, width), 0) == iota((n, width), 1), full, 0.0), axis=0, keepdims=True)


def block_sums(k, q2, v, bias, valid):
    s = lax.dot_general(k, q2, NT, preferred_element_type=F32) + bias
    top = jnp.max(s, axis=0, keepdims=True)
    p = jnp.exp2((s - top) * EXP_SCALE)
    total = jnp.sum(p, axis=0, keepdims=True)
    weighted = p * jnp.where(valid, 1.0 / total, 0.0)
    first = jnp.sum(weighted[:, :WIN], axis=1, keepdims=True)
    second = jnp.sum(weighted[:, WIN:], axis=1, keepdims=True)
    sums = jnp.where(iota((1, 128), 1) < HEAD_DIM, first, second)
    return jnp.sum(sums * v.astype(F32), axis=0, keepdims=True)


def rows_kernel(
    ids_hbm, assigned_hbm, gain_hbm, tokens_hbm, wq_hbm, wk_hbm, wv_hbm,
    q_ref, k_ref, v_ref, ctx_ref, tok_ref, bound_ref, meta_ref, target_ref,
    ids_v, assigned_v, gain_v, tokens_v, w_v, normed_v, bound_s, sc_s, sems, token_sems, bound_sem,
):
    length = q_ref.shape[0] * 16
    width = k_ref.shape[2]
    slots = 32
    parts = token_sems.shape[0]
    piece = length // parts
    r = lax.axis_index("dp")
    m = lax.axis_index("mp")

    small = [
        pltpu.make_async_copy(src, dst, sems.at[i])
        for i, (src, dst) in enumerate(((ids_hbm, ids_v), (assigned_hbm, assigned_v), (gain_hbm, gain_v)))
    ]
    weights = [
        pltpu.make_async_copy(src, w_v.at[:, i * width : (i + 1) * width], sems.at[3 + i])
        for i, src in enumerate((wq_hbm, wk_hbm, wv_hbm))
    ]
    pieces = [
        pltpu.make_async_copy(
            tokens_hbm.at[pl.ds(i * piece, piece)], tokens_v.at[pl.ds(i * piece, piece)], token_sems.at[i]
        )
        for i in range(parts)
    ]
    for copy in small + pieces[:2] + weights + pieces[2:]:
        copy.start()
    small[2].wait()

    gain = gain_v[...]
    low_half = (iota((1, width), 1) & 127) < HEAD_DIM

    def norm(i):
        rows = slice(i * piece, (i + 1) * piece)
        x = tokens_v[rows, :].astype(F32)
        centered = x - jnp.mean(x, axis=1, keepdims=True)
        variance = jnp.mean(centered * centered, axis=1, keepdims=True)
        normed_v[rows, :] = (centered * lax.rsqrt(variance + 1e-05) * gain).astype(BF16)

    def project(at, half):
        rows = slice(at, at + half)
        blocks = slice(at // 16, (at + half) // 16)
        out = jnp.dot(normed_v[rows, :], w_v[...], preferred_element_type=F32)
        q = out[:, :width]
        q_ref[blocks, :, 0:width] = jnp.where(low_half, q, 0.0).astype(BF16).reshape(half // 16, 16, width)
        q_ref[blocks, :, width : 2 * width] = jnp.where(low_half, 0.0, q).astype(BF16).reshape(half // 16, 16, width)
        k_ref[blocks] = out[:, width : 2 * width].astype(BF16).reshape(half // 16, 16, width)
        v_ref[blocks] = out[:, 2 * width :].astype(BF16).reshape(half // 16, 16, width)

    qlane = iota((1, 2 * WIN), 1) & (WIN - 1)

    def taken(ref, at, n, c0):
        return ref[pl.ds(at // 16, n // 16), :, c0 : c0 + 128].reshape(n, 128)

    def queries(at, c0):
        return jnp.concatenate([taken(q_ref, at, WIN, c0), taken(q_ref, at, WIN, width + c0)], axis=0)

    for copy in small[:2]:
        copy.wait()

    local = ids_v[...] - r * slots
    seg = iota((SEGS, length), 0)
    own = seg < slots
    carried = seg == slots
    starts = jnp.sum(jnp.where(own & (local < seg), 1.0, 0.0), axis=1, keepdims=True)
    ends = jnp.sum(jnp.where((own & (local <= seg)) | (carried & (local < 0)), 1.0, 0.0), axis=1, keepdims=True)
    lane = iota((SEGS, 128), 1)
    at_row = jnp.minimum(jnp.floor(starts * (1.0 / 16.0)) * 16.0, float(length - WIN))
    fits = (ends - at_row <= float(WIN)) & (iota((SEGS, 1), 0) < slots)
    far = jnp.where(fits | ((iota((SEGS, 1), 0) >= slots) & (ends <= float(LONG))), 0.0, 1.0)
    far = jnp.max(far, axis=0, keepdims=True)
    bound_ref[...] = jnp.where(
        lane == 0,
        starts,
        jnp.where(lane == 1, ends, jnp.where(lane == 2, at_row * (1.0 / 16.0), jnp.where(lane == 3, starts - at_row, jnp.where(lane == 4, jnp.where(fits, ends, starts) - at_row, far)))),
    ).astype(jnp.int32)
    to_scalars = pltpu.make_async_copy(bound_ref, bound_s, bound_sem)
    to_scalars.start()
    ctx_ref[...] = jnp.zeros_like(ctx_ref)

    for i in range(parts // 2):
        pieces[i].wait()
        norm(i)
    for copy in weights + pieces[parts // 2 :]:
        copy.wait()
    project(0, length // 2)
    for i in range(parts // 2, parts):
        norm(i)
    counts = ends - starts
    picks = jnp.where((ends == float(length)) & (starts < float(length)), 1.0, 0.0)
    meta_ref[8:, :] = jnp.where(lane < 64, counts, picks)
    a_row = assigned_v[...]
    used_row = to_row(counts[:slots], slots, slots) > 0
    d_row = jnp.where(used_row, ((a_row >> 10) - r) & 63, -1)
    d_col = to_column(d_row.astype(F32), slots)
    before = iota((slots, slots), 0) < iota((slots, slots), 1)
    same = d_col == d_row.astype(F32)
    rank_row = jnp.sum(jnp.where(before & same, 1.0, 0.0), axis=0, keepdims=True)
    spot = iota((64, slots), 0)
    local_row = ((a_row & 1023) + 1).astype(F32)
    here = spot == d_row
    first = jnp.sum(jnp.where(here & (rank_row == 0.0), local_row, 0.0), axis=1, keepdims=True)
    second = jnp.sum(jnp.where(here & (rank_row == 1.0), local_row, 0.0), axis=1, keepdims=True)
    place = (64 - iota((64, 128), 0)) & 63
    lane64 = iota((64, 128), 1)
    target_ref[...] = jnp.where(lane64 == place, first, 0.0) + jnp.where(lane64 == place + 64, second, 0.0)
    pick = (iota((slots, 128), 1) & 31) == iota((slots, 128), 0)
    rank_col = to_column(rank_row, slots)
    d_wide = jnp.sum(jnp.where(pick, d_col, 0.0), axis=0, keepdims=True)
    rank_wide = jnp.sum(jnp.where(pick, rank_col, 0.0), axis=0, keepdims=True)
    meta_ref[:8, :] = jnp.where(iota((8, 128), 0) == 0, d_wide, rank_wide)
    carried_end = jnp.where(ends[slots:slots + 1] <= float(LONG), ends[slots:slots + 1], 0.0).astype(jnp.int32)
    carried_bias = jnp.where(iota((LONG, 1), 0) < carried_end, 0.0, -1e30)
    for pair in range(width // 128):
        c0 = pair * 128
        total = jnp.zeros((1, 128), F32)
        for i in range(LONG // WIN):
            total = total + block_sums(
                taken(k_ref, 0, LONG, c0), queries(i * WIN, c0), taken(v_ref, 0, LONG, c0),
                carried_bias, qlane < carried_end - i * WIN,
            )
        ctx_ref[slots, :, c0 : c0 + 128] = total

    project(length // 2, length // 2)

    seg_of = jnp.where(local < 0, slots, local)
    member = jnp.where(seg == seg_of, 1.0, 0.0).astype(BF16)
    columns = pl.ds(pl.multiple_of(m * width, width), width)
    tok_ref[...] = jnp.dot(member, tokens_v[:, columns], preferred_element_type=F32)

    to_scalars.wait()
    def long(seg, start, end, reach):
        first = (start // 16) * 16
        base = pl.multiple_of(jnp.minimum(first, length - reach), 16)
        row = iota((reach, 1), 0)
        bias = jnp.where((row >= start - base) & (row < end - base), 0.0, -1e30)

        @pl.loop(0, (end - first + WIN - 1) // WIN)
        def _(i):
            qs = first + i * WIN
            at = pl.multiple_of(jnp.minimum(qs, length - WIN), 16)
            valid = (qlane >= jnp.maximum(start, qs) - at) & (qlane < end - at)
            for pair in range(width // 128):
                c0 = pair * 128
                ctx_ref[seg, :, c0 : c0 + 128] += block_sums(
                    taken(k_ref, base, reach, c0), queries(at, c0), taken(v_ref, base, reach, c0), bias, valid
                )

    def longest(seg, start, end):
        first = (start // 16) * 16
        n_k = (end - first + LONG - 1) // LONG
        row = iota((LONG, 1), 0)

        def k_rows(i):
            at = pl.multiple_of(jnp.minimum(first + i * LONG, length - LONG), 16)
            low = jnp.maximum(start, first + i * LONG) - at
            bias = jnp.where((row >= low) & (row < end - at), 0.0, -1e30)
            return at, pl.ds(pl.multiple_of(i * LONG, LONG), LONG), bias

        @pl.loop(0, (end - first + WIN - 1) // WIN)
        def _(iq):
            qs = first + iq * WIN
            qat = pl.multiple_of(jnp.minimum(qs, length - WIN), 16)
            valid = (qlane >= jnp.maximum(start, qs) - qat) & (qlane < end - qat)
            for pair in range(width // 128):
                c0 = pair * 128
                q2 = queries(qat, c0)

                def scores(i, top):
                    krows, held, bias = k_rows(i)
                    s = lax.dot_general(taken(k_ref, krows, LONG, c0), q2, NT, preferred_element_type=F32) + bias
                    sc_s[held, :] = s
                    return jnp.maximum(top, jnp.max(s, axis=0, keepdims=True))

                top = lax.fori_loop(0, n_k, scores, jnp.full((1, 2 * WIN), -2e30, F32))

                def raise_all(i, total):
                    krows, held, bias = k_rows(i)
                    p = jnp.exp2((sc_s[held, :] - top) * EXP_SCALE)
                    sc_s[held, :] = p
                    return total + jnp.sum(p, axis=0, keepdims=True)

                total = lax.fori_loop(0, n_k, raise_all, jnp.zeros((1, 2 * WIN), F32))
                inverse = jnp.where(valid, 1.0 / total, 0.0)

                def weigh(i, acc):
                    krows, held, bias = k_rows(i)
                    weighted = sc_s[held, :] * inverse
                    one = jnp.sum(weighted[:, :WIN], axis=1, keepdims=True)
                    two = jnp.sum(weighted[:, WIN:], axis=1, keepdims=True)
                    sums = jnp.where(iota((1, 128), 1) < HEAD_DIM, one, two)
                    return acc + jnp.sum(sums * taken(v_ref, krows, LONG, c0).astype(F32), axis=0, keepdims=True)

                ctx_ref[seg, :, c0 : c0 + 128] += lax.fori_loop(0, n_k, weigh, jnp.zeros((1, 128), F32))

    @pl.when(bound_s[0, 5] > 0)
    def _():
        @pl.loop(0, slots + 1)
        def _(seg):
            start = bound_s[seg, 0]
            end = bound_s[seg, 1]
            first = (start // 16) * 16

            @pl.when((end - jnp.minimum(first, length - WIN) > WIN) & ((seg < slots) | (end > LONG)))
            def _():
                @pl.when(end - first <= 256)
                def _():
                    long(seg, start, end, 256)

                @pl.when((end - first > 256) & (end - first <= 512))
                def _():
                    long(seg, start, end, 512)

                @pl.when(end - first > 512)
                def _():
                    longest(seg, start, end)


def exchange_kernel(
    dp, mp, q_ref, k_ref, v_ref, ctx_ref, tok_ref, bound_ref, meta_ref, target_ref, mass_ref, wo_ref, cent_ref,
    docs_ref, out_ref,
    bound_s, ctx_s, part_s, carry_s, got_part, got_carry, tsend, tgot, ss_send, ss_got, csend, cgot, n_send, n_got,
    bound_sem, part_sems, carry_sems, t_sems, ss_sems, c_sems, n_sems,
):
    r = lax.axis_index("dp")
    m = lax.axis_index("mp")
    slots = 32
    cents, width = cent_ref.shape
    to_scalars = pltpu.make_async_copy(bound_ref, bound_s, bound_sem)
    to_scalars.start()

    barrier = pltpu.get_barrier_semaphore()
    nxt = lax.rem(r + 1, dp)
    prv = lax.rem(r + dp - 1, dp)
    for dm in range(1, mp):
        mm = lax.rem(m + dm, mp)
        pl.semaphore_signal(barrier, inc=1, device_id=(r, mm), device_id_type=MESH)
        pl.semaphore_signal(barrier, inc=1, device_id=(nxt, mm), device_id_type=MESH)

    @pl.loop(1, dp)
    def _(d):
        pl.semaphore_signal(barrier, inc=1, device_id=(lax.rem(r + d, dp), m), device_id_type=MESH)

    tsend[...] = target_ref[...].reshape(dp, 1, 128)
    tgot[0] = tsend[0]
    ctx_s[slots + 1 :] = jnp.zeros((SEGS - slots - 1, 1, width), F32)
    to_scalars.wait()
    krow = iota((WIN, 1), 0)
    qlane = iota((1, 2 * WIN), 1) & (WIN - 1)

    def short(seg):
        block = bound_s[seg, 2]
        low = bound_s[seg, 3]
        high = bound_s[seg, 4]
        bias = jnp.where((krow >= low) & (krow < high), 0.0, -1e30)
        valid = (qlane >= low) & (qlane < high)
        q = jnp.concatenate([q_ref[block + i] for i in range(WIN // 16)], axis=0)
        k = jnp.concatenate([k_ref[block + i] for i in range(WIN // 16)], axis=0)
        v = jnp.concatenate([v_ref[block + i] for i in range(WIN // 16)], axis=0)
        for pair in range(width // 128):
            c0 = pair * 128
            q2 = jnp.concatenate([q[:, c0 : c0 + 128], q[:, width + c0 : width + c0 + 128]], axis=0)
            ctx_s[seg, :, c0 : c0 + 128] = ctx_ref[seg, :, c0 : c0 + 128] + block_sums(
                k[:, c0 : c0 + 128], q2, v[:, c0 : c0 + 128], bias, valid
            )

    def to_peer(src, dst, sems, dm):
        mm = lax.rem(m + dm, mp)
        return pltpu.make_async_remote_copy(
            src_ref=src, dst_ref=dst, send_sem=sems.at[0], recv_sem=sems.at[1],
            device_id=(r, mm), device_id_type=MESH,
        )

    def wait_all(buffer, sem):
        pltpu.make_async_copy(buffer, buffer, sem).wait()

    def out_project(rows):
        high, low = halves(rows)
        return jnp.dot(high, wo_ref[...], preferred_element_type=F32) + jnp.dot(
            low, wo_ref[...], preferred_element_type=F32
        )

    @pl.loop(0, slots // GROUP)
    def _(group):
        for j in range(GROUP):
            short(group * GROUP + j)

    ctx_s[slots] = ctx_ref[slots]
    projected = out_project(ctx_s[...].reshape(SEGS, width))
    row8 = iota((8, width), 0)
    carried_count = meta_ref[8 + slots : 9 + slots, 0:1]
    for mm in range(mp):
        block = projected[:, mm * width : (mm + 1) * width] + jnp.where(m == mm, tok_ref[...], 0.0)
        part_s[mm] = block[:slots]
        carry_s[mm] = jnp.where(row8 == 1, carried_count, block[slots:])

    pl.semaphore_wait(barrier, dp - 1 + 2 * (mp - 1))
    for mm in range(mp):
        pltpu.make_async_remote_copy(
            src_ref=carry_s.at[mm], dst_ref=got_carry.at[m], send_sem=carry_sems.at[0],
            recv_sem=carry_sems.at[1], device_id=(prv, mm), device_id_type=MESH,
        ).start()
    for dm in range(1, mp):
        to_peer(part_s.at[lax.rem(m + dm, mp)], got_part.at[mp - 1 - dm], part_sems, dm).start()

    @pl.loop(1, dp)
    def _(d):
        pltpu.make_async_remote_copy(
            src_ref=tsend.at[d], dst_ref=tgot.at[dp - d], send_sem=t_sems.at[0], recv_sem=t_sems.at[1],
            device_id=(lax.rem(r + d, dp), m), device_id_type=MESH,
        ).start()

    d_wide = meta_ref[0:1, :]
    rank_wide = meta_ref[1:2, :]
    row = iota((8 * dp, 128), 0)
    col = iota((8 * dp, 128), 1)
    j = row & 7
    pick = (
        ((row >> 3).astype(F32) == d_wide)
        & ((j >> 1).astype(F32) == rank_wide)
        & ((j & 1) == ((col >> 5) & 1))
    )
    pick = jnp.where(pick, 1.0, 0.0).astype(BF16)

    wait_all(got_carry, carry_sems.at[1])
    carry = got_carry[0]
    for i in range(1, mp):
        carry = carry + got_carry[i]
    count_in = got_carry[0][1:2, :]
    counts = meta_ref[8 : 8 + slots, 0:1]
    picks = meta_ref[8 : 8 + slots, 64:65]
    sums = part_s[m] + picks * carry[0:1, :]
    inverse = 1.0 / jnp.maximum(counts + picks * count_in, 1.0)
    wait_all(got_part, part_sems.at[1])
    for i in range(mp - 1):
        sums = sums + got_part[i]
    averages = sums * inverse
    squares = jnp.sum(averages * averages, axis=1, keepdims=True)
    square_row = to_row(squares, slots, 128)
    ss_send[...] = jnp.broadcast_to(square_row, (8, 128))
    for dm in range(1, mp):
        to_peer(ss_send, ss_got.at[mp - 1 - dm], ss_sems, dm).start()
    wait_all(ss_got, ss_sems.at[1])
    for i in range(mp - 1):
        square_row = square_row + ss_got[i][0:1, :]
    eye = iota((slots, 128), 0) == iota((slots, 128), 1)
    squares = jnp.sum(jnp.where(eye, square_row, 0.0), axis=1, keepdims=True)
    vectors = averages * lax.rsqrt(squares * (1.0 / D) + 1e-06)

    high, low = halves(vectors)
    high, low = high.astype(F32), low.astype(F32)
    stacked = jnp.concatenate([high[:, :128], high[:, 128:], low[:, :128], low[:, 128:]], axis=0).astype(BF16)
    outgoing = jnp.dot(pick, stacked, preferred_element_type=F32).reshape(dp, 8, 128)
    csend[...] = outgoing[:, :4, :]
    cgot[0] = csend[0]

    @pl.loop(1, dp)
    def _(d):
        pltpu.make_async_remote_copy(
            src_ref=csend.at[d], dst_ref=cgot.at[dp - d], send_sem=c_sems.at[0], recv_sem=c_sems.at[1],
            device_id=(lax.rem(r + d, dp), m), device_id_type=MESH,
        ).start()

    docs_ref[...] = vectors

    rest = pl.ds(1, dp - 1)
    wait_all(tgot.at[rest], t_sems.at[1])
    tgt_row = jnp.sum(tgot[...], axis=0)
    tgt_col = to_column(tgt_row, 128)
    hits = jnp.where(iota((128, cents), 1).astype(F32) == tgt_col - 1.0, 1.0, 0.0)
    mass = jnp.sum(hits * mass_ref[...], axis=1, keepdims=True)
    hits = hits.astype(BF16)
    cent_high, cent_low = halves(cent_ref[...])
    picked = jnp.dot(hits, cent_high, preferred_element_type=F32) + jnp.dot(
        hits, cent_low, preferred_element_type=F32
    )
    start = mass * picked
    together = jnp.where((tgt_col == tgt_row) & (tgt_row > 0.0), 1.0, 0.0).astype(BF16)
    earlier = iota((128, 128), 0) < iota((128, 128), 1)
    repeats = jnp.sum(jnp.where(earlier & (tgt_col == tgt_row), 1.0, 0.0), axis=0, keepdims=True)
    wanted = jnp.where(repeats == 0.0, tgt_row - 1.0, -1.0)
    writes = jnp.where(iota((cents, 128), 0).astype(F32) == wanted, 1.0, 0.0)
    out_ref[...] = jnp.where(jnp.sum(writes, axis=1, keepdims=True) > 0.0, 0.0, cent_ref[...])
    writes = writes.astype(BF16)

    wait_all(cgot.at[rest], c_sems.at[1])
    arrived = jnp.concatenate(
        [jnp.concatenate([cgot[:, 2 * k, :], cgot[:, 2 * k + 1, :]], axis=1) for k in range(2)], axis=0
    )
    high, low = halves(arrived)
    blended = start + (
        jnp.dot(together, high, preferred_element_type=F32) + jnp.dot(together, low, preferred_element_type=F32)
    )
    norm_row = to_row(jnp.sum(blended * blended, axis=1, keepdims=True), 128, 128)
    n_send[...] = jnp.broadcast_to(norm_row, (8, 128))
    for dm in range(1, mp):
        to_peer(n_send, n_got.at[mp - 1 - dm], n_sems, dm).start()
    wait_all(n_got, n_sems.at[1])
    for i in range(mp - 1):
        norm_row = norm_row + n_got[i][0:1, :]
    norms = to_column(norm_row, 128)
    high, low = halves(blended * lax.rsqrt(norms * (1.0 / D) + 1e-06))
    out_ref[...] += jnp.dot(writes, high, preferred_element_type=F32) + jnp.dot(
        writes, low, preferred_element_type=F32
    )

    wait_all(got_part, part_sems.at[0])
    wait_all(carry_s, carry_sems.at[0])
    wait_all(tsend.at[rest], t_sems.at[0])
    wait_all(ss_got, ss_sems.at[0])
    wait_all(csend.at[rest], c_sems.at[0])
    wait_all(n_got, n_sems.at[0])


def shards(
    tokens, doc_ids, ln_gain, w_query, w_key, w_value, w_out, centroids, cluster_mass, assigned
):
    length = tokens.shape[0]
    width = w_out.shape[0]
    slots = assigned.shape[0]
    cents = centroids.shape[0]
    dp, mp = lax.axis_size("dp"), lax.axis_size("mp")

    def shape(*dims, dtype=F32):
        return jax.ShapeDtypeStruct(dims, dtype)

    vmem = pl.BlockSpec(memory_space=pltpu.VMEM)
    held = pl.pallas_call(
        rows_kernel,
        in_specs=[pl.BlockSpec(memory_space=pltpu.HBM)] * 7,
        out_specs=[vmem] * 8,
        out_shape=[
            shape(length // 16, 16, 2 * width, dtype=BF16),
            shape(length // 16, 16, width, dtype=BF16),
            shape(length // 16, 16, width, dtype=BF16),
            shape(SEGS, 1, width),
            shape(SEGS, width),
            shape(SEGS, 128, dtype=jnp.int32),
            shape(8 + SEGS, 128),
            shape(dp, 128),
        ],
        scratch_shapes=[
            pltpu.VMEM((1, length), jnp.int32),
            pltpu.VMEM((1, slots), jnp.int32),
            pltpu.VMEM((1, D), F32),
            pltpu.VMEM((length, D), BF16),
            pltpu.VMEM((D, 3 * width), BF16),
            pltpu.VMEM((length, D), BF16),
            pltpu.SMEM((SEGS, 128), jnp.int32),
            pltpu.VMEM((length + LONG, 2 * WIN), F32),
            pltpu.SemaphoreType.DMA((6,)),
            pltpu.SemaphoreType.DMA((8,)),
            pltpu.SemaphoreType.DMA,
        ],
        compiler_params=pltpu.CompilerParams(vmem_limit_bytes=40 << 20),
        name="rows",
    )(
        *[pltpu.with_memory_space_constraint(x, pltpu.HBM) for x in (
            doc_ids.reshape(1, length), assigned.reshape(1, slots), ln_gain.reshape(1, D), tokens,
            w_query, w_key, w_value)]
    )

    pair = pltpu.SemaphoreType.DMA((2,))
    return pl.pallas_call(
        functools.partial(exchange_kernel, dp, mp),
        in_specs=[vmem] * 11,
        out_specs=[vmem] * 2,
        out_shape=[shape(slots, width), shape(cents, width)],
        scratch_shapes=[
            pltpu.SMEM((SEGS, 128), jnp.int32),
            pltpu.VMEM((SEGS, 1, width), F32),
            pltpu.VMEM((mp, slots, width), F32),
            pltpu.VMEM((mp, 8, width), F32),
            pltpu.VMEM((mp - 1, slots, width), F32),
            pltpu.VMEM((mp, 8, width), F32),
            pltpu.VMEM((dp, 1, 128), F32),
            pltpu.VMEM((dp, 1, 128), F32),
            pltpu.VMEM((8, 128), F32),
            pltpu.VMEM((mp - 1, 8, 128), F32),
            pltpu.VMEM((dp, 4, 128), F32),
            pltpu.VMEM((dp, 4, 128), F32),
            pltpu.VMEM((8, 128), F32),
            pltpu.VMEM((mp - 1, 8, 128), F32),
            pltpu.SemaphoreType.DMA,
            pair, pair, pair, pair, pair, pair,
        ],
        compiler_params=pltpu.CompilerParams(
            collective_id=0, has_side_effects=True, vmem_limit_bytes=24 << 20
        ),
        name="exchange",
    )(*held, cluster_mass.reshape(1, cents), w_out, centroids)


def solution(mesh):
    placed = (
        P("dp", None),
        P("dp"),
        P(),
        P(None, "mp"),
        P(None, "mp"),
        P(None, "mp"),
        P("mp", None),
        P("dp", "mp"),
        P("dp"),
        P("dp"),
    )
    return jax.shard_map(
        shards,
        mesh=mesh,
        in_specs=placed,
        out_specs=(P("dp", "mp"), P("dp", "mp")),
        check_vma=False,
    )
```

```python
import functools
import math

import jax
import jax.numpy as jnp
from jax import lax
from jax.experimental import pallas as pl
from jax.experimental.pallas import tpu as pltpu
from jax.sharding import PartitionSpec as P

D = 1024
HEAD_DIM = 64
SEGS = 40
WIN = 128
LONG = 512
GROUP = 8
F32 = jnp.float32
BF16 = jnp.bfloat16
MESH = pl.DeviceIdType.MESH
NT = (((1,), (1,)), ((), ()))
NN = (((1,), (0,)), ((), ()))
EXP_SCALE = math.log2(math.e) / math.sqrt(HEAD_DIM)


def iota(shape, dim):
    return lax.broadcasted_iota(jnp.int32, shape, dim)


def halves(x):
    high = x.astype(BF16)
    return high, (x - high.astype(F32)).astype(BF16)


def to_column(row, n):
    full = jnp.broadcast_to(row, (n, n))
    return jnp.sum(jnp.where(iota((n, n), 0) == iota((n, n), 1), full, 0.0), axis=1, keepdims=True)


def to_row(column, n, width):
    full = jnp.broadcast_to(column, (n, width))
    return jnp.sum(jnp.where(iota((n, width), 0) == iota((n, width), 1), full, 0.0), axis=0, keepdims=True)


def block_sums(k, q2, v, bias, valid):
    s = lax.dot_general(k, q2, NT, preferred_element_type=F32) + bias
    top = jnp.max(s, axis=0, keepdims=True)
    p = jnp.exp2((s - top) * EXP_SCALE)
    total = jnp.sum(p, axis=0, keepdims=True)
    weighted = p * jnp.where(valid, 1.0 / total, 0.0)
    first = jnp.sum(weighted[:, :WIN], axis=1, keepdims=True)
    second = jnp.sum(weighted[:, WIN:], axis=1, keepdims=True)
    sums = jnp.where(iota((1, 128), 1) < HEAD_DIM, first, second)
    return jnp.sum(sums * v.astype(F32), axis=0, keepdims=True)


def rows_kernel(
    ids_hbm, assigned_hbm, gain_hbm, tokens_hbm, wq_hbm, wk_hbm, wv_hbm,
    q_ref, k_ref, v_ref, ctx_ref, tok_ref, bound_ref, meta_ref, target_ref,
    ids_v, assigned_v, gain_v, tokens_v, w_v, normed_v, bound_s, sc_s, sems, token_sems, bound_sem,
):
    length = q_ref.shape[0] * 16
    width = k_ref.shape[2]
    slots = 32
    parts = token_sems.shape[0]
    piece = length // parts
    r = lax.axis_index("dp")
    m = lax.axis_index("mp")

    small = [
        pltpu.make_async_copy(src, dst, sems.at[i])
        for i, (src, dst) in enumerate(((ids_hbm, ids_v), (assigned_hbm, assigned_v), (gain_hbm, gain_v)))
    ]
    weights = [
        pltpu.make_async_copy(src, w_v.at[:, i * width : (i + 1) * width], sems.at[3 + i])
        for i, src in enumerate((wq_hbm, wk_hbm, wv_hbm))
    ]
    pieces = [
        pltpu.make_async_copy(
            tokens_hbm.at[pl.ds(i * piece, piece)], tokens_v.at[pl.ds(i * piece, piece)], token_sems.at[i]
        )
        for i in range(parts)
    ]
    for copy in small + pieces[:2] + weights + pieces[2:]:
        copy.start()
    small[2].wait()

    gain = gain_v[...]
    low_half = (iota((1, width), 1) & 127) < HEAD_DIM

    def norm(i):
        rows = slice(i * piece, (i + 1) * piece)
        x = tokens_v[rows, :].astype(F32)
        centered = x - jnp.mean(x, axis=1, keepdims=True)
        variance = jnp.mean(centered * centered, axis=1, keepdims=True)
        normed_v[rows, :] = (centered * lax.rsqrt(variance + 1e-05) * gain).astype(BF16)

    def project(at, half):
        rows = slice(at, at + half)
        blocks = slice(at // 16, (at + half) // 16)
        out = jnp.dot(normed_v[rows, :], w_v[...], preferred_element_type=F32)
        q = out[:, :width]
        q_ref[blocks, :, 0:width] = jnp.where(low_half, q, 0.0).astype(BF16).reshape(half // 16, 16, width)
        q_ref[blocks, :, width : 2 * width] = jnp.where(low_half, 0.0, q).astype(BF16).reshape(half // 16, 16, width)
        k_ref[blocks] = out[:, width : 2 * width].astype(BF16).reshape(half // 16, 16, width)
        v_ref[blocks] = out[:, 2 * width :].astype(BF16).reshape(half // 16, 16, width)

    qlane = iota((1, 2 * WIN), 1) & (WIN - 1)

    def taken(ref, at, n, c0):
        return ref[pl.ds(at // 16, n // 16), :, c0 : c0 + 128].reshape(n, 128)

    def queries(at, c0):
        return jnp.concatenate([taken(q_ref, at, WIN, c0), taken(q_ref, at, WIN, width + c0)], axis=0)

    for copy in small[:2]:
        copy.wait()

    local = ids_v[...] - r * slots
    seg = iota((SEGS, length), 0)
    own = seg < slots
    carried = seg == slots
    starts = jnp.sum(jnp.where(own & (local < seg), 1.0, 0.0), axis=1, keepdims=True)
    ends = jnp.sum(jnp.where((own & (local <= seg)) | (carried & (local < 0)), 1.0, 0.0), axis=1, keepdims=True)
    lane = iota((SEGS, 128), 1)
    at_row = jnp.minimum(jnp.floor(starts * (1.0 / 16.0)) * 16.0, float(length - WIN))
    fits = (ends - at_row <= float(WIN)) & (iota((SEGS, 1), 0) < slots)
    far = jnp.where(fits | ((iota((SEGS, 1), 0) >= slots) & (ends <= float(LONG))), 0.0, 1.0)
    far = jnp.max(far, axis=0, keepdims=True)
    bound_ref[...] = jnp.where(
        lane == 0,
        starts,
        jnp.where(lane == 1, ends, jnp.where(lane == 2, at_row * (1.0 / 16.0), jnp.where(lane == 3, starts - at_row, jnp.where(lane == 4, jnp.where(fits, ends, starts) - at_row, far)))),
    ).astype(jnp.int32)
    to_scalars = pltpu.make_async_copy(bound_ref, bound_s, bound_sem)
    to_scalars.start()
    ctx_ref[...] = jnp.zeros_like(ctx_ref)

    for i in range(parts // 2):
        pieces[i].wait()
        norm(i)
    for copy in weights + pieces[parts // 2 :]:
        copy.wait()
    project(0, length // 2)
    for i in range(parts // 2, parts):
        norm(i)
    counts = ends - starts
    picks = jnp.where((ends == float(length)) & (starts < float(length)), 1.0, 0.0)
    meta_ref[8:, :] = jnp.where(lane < 64, counts, picks)
    a_row = assigned_v[...]
    used_row = to_row(counts[:slots], slots, slots) > 0
    d_row = jnp.where(used_row, ((a_row >> 10) - r) & 63, -1)
    d_col = to_column(d_row.astype(F32), slots)
    before = iota((slots, slots), 0) < iota((slots, slots), 1)
    same = d_col == d_row.astype(F32)
    rank_row = jnp.sum(jnp.where(before & same, 1.0, 0.0), axis=0, keepdims=True)
    spot = iota((64, slots), 0)
    local_row = ((a_row & 1023) + 1).astype(F32)
    here = spot == d_row
    first = jnp.sum(jnp.where(here & (rank_row == 0.0), local_row, 0.0), axis=1, keepdims=True)
    second = jnp.sum(jnp.where(here & (rank_row == 1.0), local_row, 0.0), axis=1, keepdims=True)
    place = (64 - iota((64, 128), 0)) & 63
    lane64 = iota((64, 128), 1)
    target_ref[...] = jnp.where(lane64 == place, first, 0.0) + jnp.where(lane64 == place + 64, second, 0.0)
    pick = (iota((slots, 128), 1) & 31) == iota((slots, 128), 0)
    rank_col = to_column(rank_row, slots)
    d_wide = jnp.sum(jnp.where(pick, d_col, 0.0), axis=0, keepdims=True)
    rank_wide = jnp.sum(jnp.where(pick, rank_col, 0.0), axis=0, keepdims=True)
    meta_ref[:8, :] = jnp.where(iota((8, 128), 0) == 0, d_wide, rank_wide)
    carried_end = jnp.where(ends[slots:slots + 1] <= float(LONG), ends[slots:slots + 1], 0.0).astype(jnp.int32)
    carried_bias = jnp.where(iota((LONG, 1), 0) < carried_end, 0.0, -1e30)
    for pair in range(width // 128):
        c0 = pair * 128
        total = jnp.zeros((1, 128), F32)
        for i in range(LONG // WIN):
            total = total + block_sums(
                taken(k_ref, 0, LONG, c0), queries(i * WIN, c0), taken(v_ref, 0, LONG, c0),
                carried_bias, qlane < carried_end - i * WIN,
            )
        ctx_ref[slots, :, c0 : c0 + 128] = total

    project(length // 2, length // 2)

    seg_of = jnp.where(local < 0, slots, local)
    member = jnp.where(seg == seg_of, 1.0, 0.0).astype(BF16)
    columns = pl.ds(pl.multiple_of(m * width, width), width)
    tok_ref[...] = jnp.dot(member, tokens_v[:, columns], preferred_element_type=F32)

    to_scalars.wait()
    def long(seg, start, end, reach):
        first = (start // 16) * 16
        base = pl.multiple_of(jnp.minimum(first, length - reach), 16)
        row = iota((reach, 1), 0)
        bias = jnp.where((row >= start - base) & (row < end - base), 0.0, -1e30)

        @pl.loop(0, (end - first + WIN - 1) // WIN)
        def _(i):
            qs = first + i * WIN
            at = pl.multiple_of(jnp.minimum(qs, length - WIN), 16)
            valid = (qlane >= jnp.maximum(start, qs) - at) & (qlane < end - at)
            for pair in range(width // 128):
                c0 = pair * 128
                ctx_ref[seg, :, c0 : c0 + 128] += block_sums(
                    taken(k_ref, base, reach, c0), queries(at, c0), taken(v_ref, base, reach, c0), bias, valid
                )

    def longest(seg, start, end):
        first = (start // 16) * 16
        n_k = (end - first + LONG - 1) // LONG
        row = iota((LONG, 1), 0)

        def k_rows(i):
            at = pl.multiple_of(jnp.minimum(first + i * LONG, length - LONG), 16)
            low = jnp.maximum(start, first + i * LONG) - at
            bias = jnp.where((row >= low) & (row < end - at), 0.0, -1e30)
            return at, pl.ds(pl.multiple_of(i * LONG, LONG), LONG), bias

        @pl.loop(0, (end - first + WIN - 1) // WIN)
        def _(iq):
            qs = first + iq * WIN
            qat = pl.multiple_of(jnp.minimum(qs, length - WIN), 16)
            valid = (qlane >= jnp.maximum(start, qs) - qat) & (qlane < end - qat)
            for pair in range(width // 128):
                c0 = pair * 128
                q2 = queries(qat, c0)

                def scores(i, top):
                    krows, held, bias = k_rows(i)
                    s = lax.dot_general(taken(k_ref, krows, LONG, c0), q2, NT, preferred_element_type=F32) + bias
                    sc_s[held, :] = s
                    return jnp.maximum(top, jnp.max(s, axis=0, keepdims=True))

                top = lax.fori_loop(0, n_k, scores, jnp.full((1, 2 * WIN), -2e30, F32))

                def raise_all(i, total):
                    krows, held, bias = k_rows(i)
                    p = jnp.exp2((sc_s[held, :] - top) * EXP_SCALE)
                    sc_s[held, :] = p
                    return total + jnp.sum(p, axis=0, keepdims=True)

                total = lax.fori_loop(0, n_k, raise_all, jnp.zeros((1, 2 * WIN), F32))
                inverse = jnp.where(valid, 1.0 / total, 0.0)

                def weigh(i, acc):
                    krows, held, bias = k_rows(i)
                    weighted = sc_s[held, :] * inverse
                    one = jnp.sum(weighted[:, :WIN], axis=1, keepdims=True)
                    two = jnp.sum(weighted[:, WIN:], axis=1, keepdims=True)
                    sums = jnp.where(iota((1, 128), 1) < HEAD_DIM, one, two)
                    return acc + jnp.sum(sums * taken(v_ref, krows, LONG, c0).astype(F32), axis=0, keepdims=True)

                ctx_ref[seg, :, c0 : c0 + 128] += lax.fori_loop(0, n_k, weigh, jnp.zeros((1, 128), F32))

    @pl.when(bound_s[0, 5] > 0)
    def _():
        @pl.loop(0, slots + 1)
        def _(seg):
            start = bound_s[seg, 0]
            end = bound_s[seg, 1]
            first = (start // 16) * 16

            @pl.when((end - jnp.minimum(first, length - WIN) > WIN) & ((seg < slots) | (end > LONG)))
            def _():
                @pl.when(end - first <= 256)
                def _():
                    long(seg, start, end, 256)

                @pl.when((end - first > 256) & (end - first <= 512))
                def _():
                    long(seg, start, end, 512)

                @pl.when(end - first > 512)
                def _():
                    longest(seg, start, end)


def exchange_kernel(
    dp, mp, q_ref, k_ref, v_ref, ctx_ref, tok_ref, bound_ref, meta_ref, target_ref, mass_ref, wo_ref, cent_ref,
    docs_ref, rows_ref, writes_ref, keep_ref,
    bound_s, ctx_s, part_s, carry_s, got_part, got_carry, tsend, tgot, ss_send, ss_got, csend, cgot, n_send, n_got,
    ready, bound_sem, part_sems, carry_sems, t_sems, ss_sems, c_sems, n_sems,
):
    r = lax.axis_index("dp")
    m = lax.axis_index("mp")
    slots = 32
    cents, width = cent_ref.shape
    to_scalars = pltpu.make_async_copy(bound_ref, bound_s, bound_sem)
    to_scalars.start()

    barrier = pltpu.get_barrier_semaphore()
    nxt = lax.rem(r + 1, dp)
    prv = lax.rem(r + dp - 1, dp)
    plane = 8
    layers = dp // plane
    mine = lax.rem(r, plane)

    def along_z(i):
        return lax.rem(r + i * plane, dp)

    for dm in range(1, mp):
        pl.semaphore_signal(barrier, inc=1, device_id=(r, lax.rem(m + dm, mp)), device_id_type=MESH)
    for mm in range(mp):
        pl.semaphore_signal(barrier, inc=1, device_id=(nxt, mm), device_id_type=MESH)
    for i in range(1, layers):
        pl.semaphore_signal(barrier, inc=1, device_id=(along_z(i), m), device_id_type=MESH)
    for i in range(1, plane):
        peer = r - mine + lax.rem(mine + i, plane)
        pl.semaphore_signal(barrier, inc=1, device_id=(peer, m), device_id_type=MESH)

    tsend[...] = target_ref[...].reshape(dp, 1, 128)
    tgot[0] = tsend[0]
    ctx_s[slots + 1 :] = jnp.zeros((SEGS - slots - 1, 1, width), F32)
    to_scalars.wait()
    krow = iota((WIN, 1), 0)
    qlane = iota((1, 2 * WIN), 1) & (WIN - 1)

    def short(seg):
        block = bound_s[seg, 2]
        low = bound_s[seg, 3]
        high = bound_s[seg, 4]
        bias = jnp.where((krow >= low) & (krow < high), 0.0, -1e30)
        valid = (qlane >= low) & (qlane < high)
        q = jnp.concatenate([q_ref[block + i] for i in range(WIN // 16)], axis=0)
        k = jnp.concatenate([k_ref[block + i] for i in range(WIN // 16)], axis=0)
        v = jnp.concatenate([v_ref[block + i] for i in range(WIN // 16)], axis=0)
        for pair in range(width // 128):
            c0 = pair * 128
            q2 = jnp.concatenate([q[:, c0 : c0 + 128], q[:, width + c0 : width + c0 + 128]], axis=0)
            ctx_s[seg, :, c0 : c0 + 128] = ctx_ref[seg, :, c0 : c0 + 128] + block_sums(
                k[:, c0 : c0 + 128], q2, v[:, c0 : c0 + 128], bias, valid
            )

    def to_peer(src, dst, sems, dm):
        mm = lax.rem(m + dm, mp)
        return pltpu.make_async_remote_copy(
            src_ref=src, dst_ref=dst, send_sem=sems.at[0], recv_sem=sems.at[1],
            device_id=(r, mm), device_id_type=MESH,
        )

    def wait_all(buffer, sem):
        pltpu.make_async_copy(buffer, buffer, sem).wait()

    def out_project(rows):
        high, low = halves(rows)
        return jnp.dot(high, wo_ref[...], preferred_element_type=F32) + jnp.dot(
            low, wo_ref[...], preferred_element_type=F32
        )

    @pl.loop(0, slots // GROUP)
    def _(group):
        for j in range(GROUP):
            short(group * GROUP + j)

    ctx_s[slots] = ctx_ref[slots]
    projected = out_project(ctx_s[...].reshape(SEGS, width))
    row8 = iota((8, width), 0)
    carried_count = meta_ref[8 + slots : 9 + slots, 0:1]
    for mm in range(mp):
        block = projected[:, mm * width : (mm + 1) * width] + jnp.where(m == mm, tok_ref[...], 0.0)
        part_s[mm] = block[:slots]
        carry_s[mm] = jnp.where(row8 == 1, carried_count, block[slots:])

    pl.semaphore_wait(barrier, mp - 1 + mp + layers - 1 + plane - 1)
    for mm in range(mp):
        pltpu.make_async_remote_copy(
            src_ref=carry_s.at[mm], dst_ref=got_carry.at[m], send_sem=carry_sems.at[0],
            recv_sem=carry_sems.at[1], device_id=(prv, mm), device_id_type=MESH,
        ).start()
    for dm in range(1, mp):
        to_peer(part_s.at[lax.rem(m + dm, mp)], got_part.at[mp - 1 - dm], part_sems, dm).start()

    for i in range(1, layers):
        pl.semaphore_signal(ready, inc=1, device_id=(along_z(i), m), device_id_type=MESH)

    d_wide = meta_ref[0:1, :]
    rank_wide = meta_ref[1:2, :]
    row = iota((8 * dp, 128), 0)
    col = iota((8 * dp, 128), 1)
    j = row & 7
    pick = (
        ((row >> 3).astype(F32) == d_wide)
        & ((j >> 1).astype(F32) == rank_wide)
        & ((j & 1) == ((col >> 5) & 1))
    )
    pick = jnp.where(pick, 1.0, 0.0).astype(BF16)

    wait_all(got_carry, carry_sems.at[1])
    carry = got_carry[0]
    for i in range(1, mp):
        carry = carry + got_carry[i]
    count_in = got_carry[0][1:2, :]
    counts = meta_ref[8 : 8 + slots, 0:1]
    picks = meta_ref[8 : 8 + slots, 64:65]
    sums = part_s[m] + picks * carry[0:1, :]
    inverse = 1.0 / jnp.maximum(counts + picks * count_in, 1.0)
    wait_all(got_part, part_sems.at[1])
    for i in range(mp - 1):
        sums = sums + got_part[i]
    averages = sums * inverse
    squares = jnp.sum(averages * averages, axis=1, keepdims=True)
    square_row = to_row(squares, slots, 128)
    ss_send[...] = jnp.broadcast_to(square_row, (8, 128))
    for dm in range(1, mp):
        to_peer(ss_send, ss_got.at[mp - 1 - dm], ss_sems, dm).start()
    pl.semaphore_wait(ready, layers - 1)

    @pl.loop(1, dp)
    def _(d):
        pltpu.make_async_remote_copy(
            src_ref=tsend.at[d], dst_ref=tgot.at[dp - d], send_sem=t_sems.at[0], recv_sem=t_sems.at[1],
            device_id=(lax.rem(r + d, dp), m), device_id_type=MESH,
        ).start()

    wait_all(ss_got, ss_sems.at[1])
    for i in range(mp - 1):
        square_row = square_row + ss_got[i][0:1, :]
    eye = iota((slots, 128), 0) == iota((slots, 128), 1)
    squares = jnp.sum(jnp.where(eye, square_row, 0.0), axis=1, keepdims=True)
    vectors = averages * lax.rsqrt(squares * (1.0 / D) + 1e-06)

    high, low = halves(vectors)
    high, low = high.astype(F32), low.astype(F32)
    stacked = jnp.concatenate([high[:, :128], high[:, 128:], low[:, :128], low[:, 128:]], axis=0).astype(BF16)
    outgoing = jnp.dot(pick, stacked, preferred_element_type=F32).reshape(dp, 8, 128)
    csend[...] = outgoing[:, :4, :]
    cgot[0] = csend[0]

    @pl.loop(1, dp)
    def _(d):
        pltpu.make_async_remote_copy(
            src_ref=csend.at[d], dst_ref=cgot.at[dp - d], send_sem=c_sems.at[0], recv_sem=c_sems.at[1],
            device_id=(lax.rem(r + d, dp), m), device_id_type=MESH,
        ).start()

    docs_ref[...] = vectors

    rest = pl.ds(1, dp - 1)
    wait_all(tgot.at[rest], t_sems.at[1])
    tgt_row = jnp.sum(tgot[...], axis=0)
    tgt_col = to_column(tgt_row, 128)
    hits = jnp.where(iota((128, cents), 1).astype(F32) == tgt_col - 1.0, 1.0, 0.0)
    mass = jnp.sum(hits * mass_ref[...], axis=1, keepdims=True)
    hits = hits.astype(BF16)
    cent_high, cent_low = halves(cent_ref[...])
    picked = jnp.dot(hits, cent_high, preferred_element_type=F32) + jnp.dot(
        hits, cent_low, preferred_element_type=F32
    )
    start = mass * picked
    together = jnp.where((tgt_col == tgt_row) & (tgt_row > 0.0), 1.0, 0.0).astype(BF16)
    earlier = iota((128, 128), 0) < iota((128, 128), 1)
    repeats = jnp.sum(jnp.where(earlier & (tgt_col == tgt_row), 1.0, 0.0), axis=0, keepdims=True)
    wanted = jnp.where(repeats == 0.0, tgt_row - 1.0, -1.0)
    writes = jnp.where(iota((cents, 128), 0).astype(F32) == wanted, 1.0, 0.0)
    keep_ref[...] = jnp.where(jnp.sum(writes, axis=1, keepdims=True) > 0.0, 0.0, cent_ref[...])
    writes_ref[...] = writes.astype(BF16)

    wait_all(cgot.at[rest], c_sems.at[1])
    arrived = jnp.concatenate(
        [jnp.concatenate([cgot[:, 2 * k, :], cgot[:, 2 * k + 1, :]], axis=1) for k in range(2)], axis=0
    )
    high, low = halves(arrived)
    blended = start + (
        jnp.dot(together, high, preferred_element_type=F32) + jnp.dot(together, low, preferred_element_type=F32)
    )
    norm_row = to_row(jnp.sum(blended * blended, axis=1, keepdims=True), 128, 128)
    n_send[...] = jnp.broadcast_to(norm_row, (8, 128))
    for dm in range(1, mp):
        to_peer(n_send, n_got.at[mp - 1 - dm], n_sems, dm).start()
    wait_all(n_got, n_sems.at[1])
    for i in range(mp - 1):
        norm_row = norm_row + n_got[i][0:1, :]
    norms = to_column(norm_row, 128)
    rows_ref[...] = blended * lax.rsqrt(norms * (1.0 / D) + 1e-06)

    wait_all(got_part, part_sems.at[0])
    wait_all(carry_s, carry_sems.at[0])
    wait_all(tsend.at[rest], t_sems.at[0])
    wait_all(ss_got, ss_sems.at[0])
    wait_all(csend.at[rest], c_sems.at[0])
    wait_all(n_got, n_sems.at[0])


def write_kernel(docs_ref, rows_ref, writes_ref, keep_ref, docs_hbm, out_hbm, out_v, sems):
    parts = 4
    block = keep_ref.shape[0] // parts
    docs_copy = pltpu.make_async_copy(docs_ref, docs_hbm, sems.at[parts])
    docs_copy.start()
    high, low = halves(rows_ref[...])
    copies = []
    for i in range(parts):
        rows = pl.ds(i * block, block)
        writes = writes_ref[rows, :]
        out_v[rows, :] = (
            keep_ref[rows, :]
            + jnp.dot(writes, high, preferred_element_type=F32)
            + jnp.dot(writes, low, preferred_element_type=F32)
        )
        copies.append(pltpu.make_async_copy(out_v.at[rows], out_hbm.at[rows], sems.at[i]))
        copies[-1].start()
    docs_copy.wait()
    for copy in copies:
        copy.wait()


def shards(
    tokens, doc_ids, ln_gain, w_query, w_key, w_value, w_out, centroids, cluster_mass, assigned
):
    length = tokens.shape[0]
    width = w_out.shape[0]
    slots = assigned.shape[0]
    cents = centroids.shape[0]
    dp, mp = lax.axis_size("dp"), lax.axis_size("mp")

    def shape(*dims, dtype=F32):
        return jax.ShapeDtypeStruct(dims, dtype)

    vmem = pl.BlockSpec(memory_space=pltpu.VMEM)
    held = pl.pallas_call(
        rows_kernel,
        in_specs=[pl.BlockSpec(memory_space=pltpu.HBM)] * 7,
        out_specs=[vmem] * 8,
        out_shape=[
            shape(length // 16, 16, 2 * width, dtype=BF16),
            shape(length // 16, 16, width, dtype=BF16),
            shape(length // 16, 16, width, dtype=BF16),
            shape(SEGS, 1, width),
            shape(SEGS, width),
            shape(SEGS, 128, dtype=jnp.int32),
            shape(8 + SEGS, 128),
            shape(dp, 128),
        ],
        scratch_shapes=[
            pltpu.VMEM((1, length), jnp.int32),
            pltpu.VMEM((1, slots), jnp.int32),
            pltpu.VMEM((1, D), F32),
            pltpu.VMEM((length, D), BF16),
            pltpu.VMEM((D, 3 * width), BF16),
            pltpu.VMEM((length, D), BF16),
            pltpu.SMEM((SEGS, 128), jnp.int32),
            pltpu.VMEM((length + LONG, 2 * WIN), F32),
            pltpu.SemaphoreType.DMA((6,)),
            pltpu.SemaphoreType.DMA((8,)),
            pltpu.SemaphoreType.DMA,
        ],
        compiler_params=pltpu.CompilerParams(vmem_limit_bytes=40 << 20),
        name="rows",
    )(
        *[pltpu.with_memory_space_constraint(x, pltpu.HBM) for x in (
            doc_ids.reshape(1, length), assigned.reshape(1, slots), ln_gain.reshape(1, D), tokens,
            w_query, w_key, w_value)]
    )

    pair = pltpu.SemaphoreType.DMA((2,))
    new = pl.pallas_call(
        functools.partial(exchange_kernel, dp, mp),
        in_specs=[vmem] * 11,
        out_specs=[vmem] * 4,
        out_shape=[
            shape(slots, width),
            shape(128, width),
            shape(cents, 128, dtype=BF16),
            shape(cents, width),
        ],
        scratch_shapes=[
            pltpu.SMEM((SEGS, 128), jnp.int32),
            pltpu.VMEM((SEGS, 1, width), F32),
            pltpu.VMEM((mp, slots, width), F32),
            pltpu.VMEM((mp, 8, width), F32),
            pltpu.VMEM((mp - 1, slots, width), F32),
            pltpu.VMEM((mp, 8, width), F32),
            pltpu.VMEM((dp, 1, 128), F32),
            pltpu.VMEM((dp, 1, 128), F32),
            pltpu.VMEM((8, 128), F32),
            pltpu.VMEM((mp - 1, 8, 128), F32),
            pltpu.VMEM((dp, 4, 128), F32),
            pltpu.VMEM((dp, 4, 128), F32),
            pltpu.VMEM((8, 128), F32),
            pltpu.VMEM((mp - 1, 8, 128), F32),
            pltpu.SemaphoreType.REGULAR,
            pltpu.SemaphoreType.DMA,
            pair, pair, pair, pair, pair, pair,
        ],
        compiler_params=pltpu.CompilerParams(
            collective_id=0, has_side_effects=True, vmem_limit_bytes=24 << 20
        ),
        name="exchange",
    )(*held, cluster_mass.reshape(1, cents), w_out, centroids)

    anywhere = pl.BlockSpec(memory_space=pl.ANY)
    return pl.pallas_call(
        write_kernel,
        in_specs=[vmem] * 4,
        out_specs=[anywhere] * 2,
        out_shape=[shape(slots, width), shape(cents, width)],
        scratch_shapes=[pltpu.VMEM((cents, width), F32), pltpu.SemaphoreType.DMA((5,))],
        compiler_params=pltpu.CompilerParams(vmem_limit_bytes=16 << 20),
        name="write",
    )(*new)


def solution(mesh):
    placed = (
        P("dp", None),
        P("dp"),
        P(),
        P(None, "mp"),
        P(None, "mp"),
        P(None, "mp"),
        P("mp", None),
        P("dp", "mp"),
        P("dp"),
        P("dp"),
    )
    return jax.shard_map(
        shards,
        mesh=mesh,
        in_specs=placed,
        out_specs=(P("dp", "mp"), P("dp", "mp")),
        check_vma=False,
    )
```

```python
import functools
import math

import jax
import jax.numpy as jnp
from jax import lax
from jax.experimental import pallas as pl
from jax.experimental.pallas import tpu as pltpu
from jax.sharding import PartitionSpec as P

D = 1024
HEAD_DIM = 64
SEGS = 40
WIN = 128
LONG = 512
GROUP = 16
F32 = jnp.float32
BF16 = jnp.bfloat16
MESH = pl.DeviceIdType.MESH
NT = (((1,), (1,)), ((), ()))
NN = (((1,), (0,)), ((), ()))
EXP_SCALE = math.log2(math.e) / math.sqrt(HEAD_DIM)


def iota(shape, dim):
    return lax.broadcasted_iota(jnp.int32, shape, dim)


def halves(x):
    high = x.astype(BF16)
    return high, (x - high.astype(F32)).astype(BF16)


def to_column(row, n):
    full = jnp.broadcast_to(row, (n, n))
    return jnp.sum(jnp.where(iota((n, n), 0) == iota((n, n), 1), full, 0.0), axis=1, keepdims=True)


def to_row(column, n, width):
    full = jnp.broadcast_to(column, (n, width))
    return jnp.sum(jnp.where(iota((n, width), 0) == iota((n, width), 1), full, 0.0), axis=0, keepdims=True)


def block_sums(k, q2, v, bias, valid):
    s = lax.dot_general(k, q2, NT, preferred_element_type=F32) + bias
    top = jnp.max(s, axis=0, keepdims=True)
    p = jnp.exp2((s - top) * EXP_SCALE)
    total = jnp.sum(p, axis=0, keepdims=True)
    weighted = p * jnp.where(valid, 1.0 / total, 0.0)
    first = jnp.sum(weighted[:, :WIN], axis=1, keepdims=True)
    second = jnp.sum(weighted[:, WIN:], axis=1, keepdims=True)
    sums = jnp.where(iota((1, 128), 1) < HEAD_DIM, first, second)
    return jnp.sum(sums * v.astype(F32), axis=0, keepdims=True)


def rows_kernel(
    ids_hbm, assigned_hbm, gain_hbm, tokens_hbm, wq_hbm, wk_hbm, wv_hbm,
    q_ref, k_ref, v_ref, ctx_ref, tok_ref, bound_ref, meta_ref, target_ref,
    ids_v, assigned_v, gain_v, tokens_v, w_v, normed_v, bound_s, sc_s, sems, token_sems, bound_sem,
):
    length = q_ref.shape[0] * 16
    width = k_ref.shape[2]
    slots = 32
    parts = token_sems.shape[0]
    piece = length // parts
    r = lax.axis_index("dp")
    m = lax.axis_index("mp")

    small = [
        pltpu.make_async_copy(src, dst, sems.at[i])
        for i, (src, dst) in enumerate(((ids_hbm, ids_v), (assigned_hbm, assigned_v), (gain_hbm, gain_v)))
    ]
    weights = [
        pltpu.make_async_copy(src, w_v.at[:, i * width : (i + 1) * width], sems.at[3 + i])
        for i, src in enumerate((wq_hbm, wk_hbm, wv_hbm))
    ]
    pieces = [
        pltpu.make_async_copy(
            tokens_hbm.at[pl.ds(i * piece, piece)], tokens_v.at[pl.ds(i * piece, piece)], token_sems.at[i]
        )
        for i in range(parts)
    ]
    for copy in small + pieces[:2] + weights + pieces[2:]:
        copy.start()
    small[2].wait()

    gain = gain_v[...]
    low_half = (iota((1, width), 1) & 127) < HEAD_DIM

    def norm(i):
        rows = slice(i * piece, (i + 1) * piece)
        x = tokens_v[rows, :].astype(F32)
        centered = x - jnp.mean(x, axis=1, keepdims=True)
        variance = jnp.mean(centered * centered, axis=1, keepdims=True)
        normed_v[rows, :] = (centered * lax.rsqrt(variance + 1e-05) * gain).astype(BF16)

    def project(at, half):
        rows = slice(at, at + half)
        blocks = slice(at // 16, (at + half) // 16)
        out = jnp.dot(normed_v[rows, :], w_v[...], preferred_element_type=F32)
        q = out[:, :width]
        q_ref[blocks, :, 0:width] = jnp.where(low_half, q, 0.0).astype(BF16).reshape(half // 16, 16, width)
        q_ref[blocks, :, width : 2 * width] = jnp.where(low_half, 0.0, q).astype(BF16).reshape(half // 16, 16, width)
        k_ref[blocks] = out[:, width : 2 * width].astype(BF16).reshape(half // 16, 16, width)
        v_ref[blocks] = out[:, 2 * width :].astype(BF16).reshape(half // 16, 16, width)

    qlane = iota((1, 2 * WIN), 1) & (WIN - 1)

    def taken(ref, at, n, c0):
        return ref[pl.ds(at // 16, n // 16), :, c0 : c0 + 128].reshape(n, 128)

    def queries(at, c0):
        return jnp.concatenate([taken(q_ref, at, WIN, c0), taken(q_ref, at, WIN, width + c0)], axis=0)

    for copy in small[:2]:
        copy.wait()

    local = ids_v[...] - r * slots
    seg = iota((SEGS, length), 0)
    own = seg < slots
    carried = seg == slots
    starts = jnp.sum(jnp.where(own & (local < seg), 1.0, 0.0), axis=1, keepdims=True)
    ends = jnp.sum(jnp.where((own & (local <= seg)) | (carried & (local < 0)), 1.0, 0.0), axis=1, keepdims=True)
    lane = iota((SEGS, 128), 1)
    at_row = jnp.minimum(jnp.floor(starts * (1.0 / 16.0)) * 16.0, float(length - WIN))
    fits = (ends - at_row <= float(WIN)) & (iota((SEGS, 1), 0) < slots)
    far = jnp.where(fits | ((iota((SEGS, 1), 0) >= slots) & (ends <= float(LONG))), 0.0, 1.0)
    far = jnp.max(far, axis=0, keepdims=True)
    bound_ref[...] = jnp.where(
        lane == 0,
        starts,
        jnp.where(lane == 1, ends, jnp.where(lane == 2, at_row * (1.0 / 16.0), jnp.where(lane == 3, starts - at_row, jnp.where(lane == 4, jnp.where(fits, ends, starts) - at_row, far)))),
    ).astype(jnp.int32)
    to_scalars = pltpu.make_async_copy(bound_ref, bound_s, bound_sem)
    to_scalars.start()
    ctx_ref[...] = jnp.zeros_like(ctx_ref)

    for i in range(parts // 2):
        pieces[i].wait()
        norm(i)
    for copy in weights + pieces[parts // 2 :]:
        copy.wait()
    project(0, length // 2)
    for i in range(parts // 2, parts):
        norm(i)
    counts = ends - starts
    picks = jnp.where((ends == float(length)) & (starts < float(length)), 1.0, 0.0)
    meta_ref[8:, :] = jnp.where(lane < 64, counts, picks)
    a_row = assigned_v[...]
    used_row = to_row(counts[:slots], slots, slots) > 0
    d_row = jnp.where(used_row, ((a_row >> 10) - r) & 63, -1)
    d_col = to_column(d_row.astype(F32), slots)
    before = iota((slots, slots), 0) < iota((slots, slots), 1)
    same = d_col == d_row.astype(F32)
    rank_row = jnp.sum(jnp.where(before & same, 1.0, 0.0), axis=0, keepdims=True)
    spot = iota((64, slots), 0)
    local_row = ((a_row & 1023) + 1).astype(F32)
    here = spot == d_row
    first = jnp.sum(jnp.where(here & (rank_row == 0.0), local_row, 0.0), axis=1, keepdims=True)
    second = jnp.sum(jnp.where(here & (rank_row == 1.0), local_row, 0.0), axis=1, keepdims=True)
    place = (64 - iota((64, 128), 0)) & 63
    lane64 = iota((64, 128), 1)
    target_ref[...] = jnp.where(lane64 == place, first, 0.0) + jnp.where(lane64 == place + 64, second, 0.0)
    pick = (iota((slots, 128), 1) & 31) == iota((slots, 128), 0)
    rank_col = to_column(rank_row, slots)
    d_wide = jnp.sum(jnp.where(pick, d_col, 0.0), axis=0, keepdims=True)
    rank_wide = jnp.sum(jnp.where(pick, rank_col, 0.0), axis=0, keepdims=True)
    meta_ref[:8, :] = jnp.where(iota((8, 128), 0) == 0, d_wide, rank_wide)
    carried_end = jnp.where(ends[slots:slots + 1] <= float(LONG), ends[slots:slots + 1], 0.0).astype(jnp.int32)
    carried_bias = jnp.where(iota((LONG, 1), 0) < carried_end, 0.0, -1e30)
    for pair in range(width // 128):
        c0 = pair * 128
        total = jnp.zeros((1, 128), F32)
        for i in range(LONG // WIN):
            total = total + block_sums(
                taken(k_ref, 0, LONG, c0), queries(i * WIN, c0), taken(v_ref, 0, LONG, c0),
                carried_bias, qlane < carried_end - i * WIN,
            )
        ctx_ref[slots, :, c0 : c0 + 128] = total

    project(length // 2, length // 2)

    seg_of = jnp.where(local < 0, slots, local)
    member = jnp.where(seg == seg_of, 1.0, 0.0).astype(BF16)
    columns = pl.ds(pl.multiple_of(m * width, width), width)
    tok_ref[...] = jnp.dot(member, tokens_v[:, columns], preferred_element_type=F32)

    to_scalars.wait()
    def long(seg, start, end, reach):
        first = (start // 16) * 16
        base = pl.multiple_of(jnp.minimum(first, length - reach), 16)
        row = iota((reach, 1), 0)
        bias = jnp.where((row >= start - base) & (row < end - base), 0.0, -1e30)

        @pl.loop(0, (end - first + WIN - 1) // WIN)
        def _(i):
            qs = first + i * WIN
            at = pl.multiple_of(jnp.minimum(qs, length - WIN), 16)
            valid = (qlane >= jnp.maximum(start, qs) - at) & (qlane < end - at)
            for pair in range(width // 128):
                c0 = pair * 128
                ctx_ref[seg, :, c0 : c0 + 128] += block_sums(
                    taken(k_ref, base, reach, c0), queries(at, c0), taken(v_ref, base, reach, c0), bias, valid
                )

    def longest(seg, start, end):
        first = (start // 16) * 16
        n_k = (end - first + LONG - 1) // LONG
        row = iota((LONG, 1), 0)

        def k_rows(i):
            at = pl.multiple_of(jnp.minimum(first + i * LONG, length - LONG), 16)
            low = jnp.maximum(start, first + i * LONG) - at
            bias = jnp.where((row >= low) & (row < end - at), 0.0, -1e30)
            return at, pl.ds(pl.multiple_of(i * LONG, LONG), LONG), bias

        @pl.loop(0, (end - first + WIN - 1) // WIN)
        def _(iq):
            qs = first + iq * WIN
            qat = pl.multiple_of(jnp.minimum(qs, length - WIN), 16)
            valid = (qlane >= jnp.maximum(start, qs) - qat) & (qlane < end - qat)
            for pair in range(width // 128):
                c0 = pair * 128
                q2 = queries(qat, c0)

                def scores(i, top):
                    krows, held, bias = k_rows(i)
                    s = lax.dot_general(taken(k_ref, krows, LONG, c0), q2, NT, preferred_element_type=F32) + bias
                    sc_s[held, :] = s
                    return jnp.maximum(top, jnp.max(s, axis=0, keepdims=True))

                top = lax.fori_loop(0, n_k, scores, jnp.full((1, 2 * WIN), -2e30, F32))

                def raise_all(i, total):
                    krows, held, bias = k_rows(i)
                    p = jnp.exp2((sc_s[held, :] - top) * EXP_SCALE)
                    sc_s[held, :] = p
                    return total + jnp.sum(p, axis=0, keepdims=True)

                total = lax.fori_loop(0, n_k, raise_all, jnp.zeros((1, 2 * WIN), F32))
                inverse = jnp.where(valid, 1.0 / total, 0.0)

                def weigh(i, acc):
                    krows, held, bias = k_rows(i)
                    weighted = sc_s[held, :] * inverse
                    one = jnp.sum(weighted[:, :WIN], axis=1, keepdims=True)
                    two = jnp.sum(weighted[:, WIN:], axis=1, keepdims=True)
                    sums = jnp.where(iota((1, 128), 1) < HEAD_DIM, one, two)
                    return acc + jnp.sum(sums * taken(v_ref, krows, LONG, c0).astype(F32), axis=0, keepdims=True)

                ctx_ref[seg, :, c0 : c0 + 128] += lax.fori_loop(0, n_k, weigh, jnp.zeros((1, 128), F32))

    @pl.when(bound_s[0, 5] > 0)
    def _():
        @pl.loop(0, slots + 1)
        def _(seg):
            start = bound_s[seg, 0]
            end = bound_s[seg, 1]
            first = (start // 16) * 16

            @pl.when((end - jnp.minimum(first, length - WIN) > WIN) & ((seg < slots) | (end > LONG)))
            def _():
                @pl.when(end - first <= 256)
                def _():
                    long(seg, start, end, 256)

                @pl.when((end - first > 256) & (end - first <= 512))
                def _():
                    long(seg, start, end, 512)

                @pl.when(end - first > 512)
                def _():
                    longest(seg, start, end)


def exchange_kernel(
    dp, mp, q_ref, k_ref, v_ref, ctx_ref, tok_ref, bound_ref, meta_ref, target_ref, mass_ref, wo_hbm, cent_hbm,
    docs_ref, rows_ref, writes_ref, keep_ref,
    bound_s, ctx_s, part_s, carry_s, got_part, got_carry, tsend, tgot, ss_send, ss_got, csend, cgot, n_send, n_got,
    wo_ref, cent_ref, ready, late_sems, bound_sem, part_sems, carry_sems, t_sems, ss_sems, c_sems, n_sems,
):
    r = lax.axis_index("dp")
    m = lax.axis_index("mp")
    slots = 32
    cents, width = cent_ref.shape
    load_wo = pltpu.make_async_copy(wo_hbm, wo_ref, late_sems.at[0])
    load_cent = pltpu.make_async_copy(cent_hbm, cent_ref, late_sems.at[1])
    load_wo.start()
    load_cent.start()
    to_scalars = pltpu.make_async_copy(bound_ref, bound_s, bound_sem)
    to_scalars.start()

    barrier = pltpu.get_barrier_semaphore()
    nxt = lax.rem(r + 1, dp)
    prv = lax.rem(r + dp - 1, dp)
    plane = 8
    layers = dp // plane
    mine = lax.rem(r, plane)

    def along_z(i):
        return lax.rem(r + i * plane, dp)

    for dm in range(1, mp):
        pl.semaphore_signal(barrier, inc=1, device_id=(r, lax.rem(m + dm, mp)), device_id_type=MESH)
    for mm in range(mp):
        pl.semaphore_signal(barrier, inc=1, device_id=(nxt, mm), device_id_type=MESH)
    for i in range(1, layers):
        pl.semaphore_signal(barrier, inc=1, device_id=(along_z(i), m), device_id_type=MESH)
    for i in range(1, plane):
        peer = r - mine + lax.rem(mine + i, plane)
        pl.semaphore_signal(barrier, inc=1, device_id=(peer, m), device_id_type=MESH)

    tsend[...] = target_ref[...].reshape(dp, 1, 128)
    tgot[0] = tsend[0]
    ctx_s[slots + 1 :] = jnp.zeros((SEGS - slots - 1, 1, width), F32)
    to_scalars.wait()
    krow = iota((WIN, 1), 0)
    qlane = iota((1, 2 * WIN), 1) & (WIN - 1)

    def short(seg):
        block = bound_s[seg, 2]
        low = bound_s[seg, 3]
        high = bound_s[seg, 4]
        bias = jnp.where((krow >= low) & (krow < high), 0.0, -1e30)
        valid = (qlane >= low) & (qlane < high)
        q = jnp.concatenate([q_ref[block + i] for i in range(WIN // 16)], axis=0)
        k = jnp.concatenate([k_ref[block + i] for i in range(WIN // 16)], axis=0)
        v = jnp.concatenate([v_ref[block + i] for i in range(WIN // 16)], axis=0)
        for pair in range(width // 128):
            c0 = pair * 128
            q2 = jnp.concatenate([q[:, c0 : c0 + 128], q[:, width + c0 : width + c0 + 128]], axis=0)
            ctx_s[seg, :, c0 : c0 + 128] = ctx_ref[seg, :, c0 : c0 + 128] + block_sums(
                k[:, c0 : c0 + 128], q2, v[:, c0 : c0 + 128], bias, valid
            )

    def to_peer(src, dst, sems, dm):
        mm = lax.rem(m + dm, mp)
        return pltpu.make_async_remote_copy(
            src_ref=src, dst_ref=dst, send_sem=sems.at[0], recv_sem=sems.at[1],
            device_id=(r, mm), device_id_type=MESH,
        )

    def far_first(i):
        def order(k):
            odd = k % 2
            return 4 - odd * ((k + 1) // 2) + (1 - odd) * (k // 2)

        return order(i // 8) * 8 + order(i % 8)

    def wait_all(buffer, sem):
        pltpu.make_async_copy(buffer, buffer, sem).wait()

    def out_project(rows):
        high, low = halves(rows)
        return jnp.dot(high, wo_ref[...], preferred_element_type=F32) + jnp.dot(
            low, wo_ref[...], preferred_element_type=F32
        )

    @pl.loop(0, slots // GROUP)
    def _(group):
        for j in range(GROUP):
            short(group * GROUP + j)

    ctx_s[slots] = ctx_ref[slots]
    load_wo.wait()
    projected = out_project(ctx_s[...].reshape(SEGS, width))
    row8 = iota((8, width), 0)
    carried_count = meta_ref[8 + slots : 9 + slots, 0:1]
    for mm in range(mp):
        block = projected[:, mm * width : (mm + 1) * width] + jnp.where(m == mm, tok_ref[...], 0.0)
        part_s[mm] = block[:slots]
        carry_s[mm] = jnp.where(row8 == 1, carried_count, block[slots:])

    pl.semaphore_wait(barrier, mp - 1 + mp + layers - 1 + plane - 1)
    for mm in range(mp):
        pltpu.make_async_remote_copy(
            src_ref=carry_s.at[mm], dst_ref=got_carry.at[m], send_sem=carry_sems.at[0],
            recv_sem=carry_sems.at[1], device_id=(prv, mm), device_id_type=MESH,
        ).start()
    for dm in range(1, mp):
        to_peer(part_s.at[lax.rem(m + dm, mp)], got_part.at[mp - 1 - dm], part_sems, dm).start()

    for i in range(1, layers):
        pl.semaphore_signal(ready, inc=1, device_id=(along_z(i), m), device_id_type=MESH)

    d_wide = meta_ref[0:1, :]
    rank_wide = meta_ref[1:2, :]
    row = iota((8 * dp, 128), 0)
    col = iota((8 * dp, 128), 1)
    j = row & 7
    pick = (
        ((row >> 3).astype(F32) == d_wide)
        & ((j >> 1).astype(F32) == rank_wide)
        & ((j & 1) == ((col >> 5) & 1))
    )
    pick = jnp.where(pick, 1.0, 0.0).astype(BF16)

    wait_all(got_carry, carry_sems.at[1])
    carry = got_carry[0]
    for i in range(1, mp):
        carry = carry + got_carry[i]
    count_in = got_carry[0][1:2, :]
    counts = meta_ref[8 : 8 + slots, 0:1]
    picks = meta_ref[8 : 8 + slots, 64:65]
    sums = part_s[m] + picks * carry[0:1, :]
    inverse = 1.0 / jnp.maximum(counts + picks * count_in, 1.0)
    wait_all(got_part, part_sems.at[1])
    for i in range(mp - 1):
        sums = sums + got_part[i]
    averages = sums * inverse
    squares = jnp.sum(averages * averages, axis=1, keepdims=True)
    square_row = to_row(squares, slots, 128)
    ss_send[...] = jnp.broadcast_to(square_row, (8, 128))
    for dm in range(1, mp):
        to_peer(ss_send, ss_got.at[mp - 1 - dm], ss_sems, dm).start()
    pl.semaphore_wait(ready, layers - 1)

    @pl.loop(1, dp)
    def _(d):
        pltpu.make_async_remote_copy(
            src_ref=tsend.at[d], dst_ref=tgot.at[dp - d], send_sem=t_sems.at[0], recv_sem=t_sems.at[1],
            device_id=(lax.rem(r + d, dp), m), device_id_type=MESH,
        ).start()

    wait_all(ss_got, ss_sems.at[1])
    for i in range(mp - 1):
        square_row = square_row + ss_got[i][0:1, :]
    eye = iota((slots, 128), 0) == iota((slots, 128), 1)
    squares = jnp.sum(jnp.where(eye, square_row, 0.0), axis=1, keepdims=True)
    vectors = averages * lax.rsqrt(squares * (1.0 / D) + 1e-06)

    high, low = halves(vectors)
    high, low = high.astype(F32), low.astype(F32)
    stacked = jnp.concatenate([high[:, :128], high[:, 128:], low[:, :128], low[:, 128:]], axis=0).astype(BF16)
    outgoing = jnp.dot(pick, stacked, preferred_element_type=F32).reshape(dp, 8, 128)
    csend[...] = outgoing[:, :4, :]
    cgot[0] = csend[0]

    @pl.loop(0, dp - 1)
    def _(i):
        d = far_first(i)
        pltpu.make_async_remote_copy(
            src_ref=csend.at[d], dst_ref=cgot.at[dp - d], send_sem=c_sems.at[0], recv_sem=c_sems.at[1],
            device_id=(lax.rem(r + d, dp), m), device_id_type=MESH,
        ).start()

    docs_ref[...] = vectors

    rest = pl.ds(1, dp - 1)
    wait_all(tgot.at[rest], t_sems.at[1])
    tgt_row = jnp.sum(tgot[...], axis=0)
    tgt_col = to_column(tgt_row, 128)
    hits = jnp.where(iota((128, cents), 1).astype(F32) == tgt_col - 1.0, 1.0, 0.0)
    mass = jnp.sum(hits * mass_ref[...], axis=1, keepdims=True)
    hits = hits.astype(BF16)
    load_cent.wait()
    cent_high, cent_low = halves(cent_ref[...])
    picked = jnp.dot(hits, cent_high, preferred_element_type=F32) + jnp.dot(
        hits, cent_low, preferred_element_type=F32
    )
    start = mass * picked
    together = jnp.where((tgt_col == tgt_row) & (tgt_row > 0.0), 1.0, 0.0).astype(BF16)
    earlier = iota((128, 128), 0) < iota((128, 128), 1)
    repeats = jnp.sum(jnp.where(earlier & (tgt_col == tgt_row), 1.0, 0.0), axis=0, keepdims=True)
    wanted = jnp.where(repeats == 0.0, tgt_row - 1.0, -1.0)
    writes = jnp.where(iota((cents, 128), 0).astype(F32) == wanted, 1.0, 0.0)
    keep_ref[...] = jnp.where(jnp.sum(writes, axis=1, keepdims=True) > 0.0, 0.0, cent_ref[...])
    writes_ref[...] = writes.astype(BF16)

    wait_all(cgot.at[rest], c_sems.at[1])
    arrived = jnp.concatenate(
        [jnp.concatenate([cgot[:, 2 * k, :], cgot[:, 2 * k + 1, :]], axis=1) for k in range(2)], axis=0
    )
    high, low = halves(arrived)
    blended = start + (
        jnp.dot(together, high, preferred_element_type=F32) + jnp.dot(together, low, preferred_element_type=F32)
    )
    norm_row = to_row(jnp.sum(blended * blended, axis=1, keepdims=True), 128, 128)
    n_send[...] = jnp.broadcast_to(norm_row, (8, 128))
    for dm in range(1, mp):
        to_peer(n_send, n_got.at[mp - 1 - dm], n_sems, dm).start()
    wait_all(n_got, n_sems.at[1])
    for i in range(mp - 1):
        norm_row = norm_row + n_got[i][0:1, :]
    norms = to_column(norm_row, 128)
    rows_ref[...] = blended * lax.rsqrt(norms * (1.0 / D) + 1e-06)

    wait_all(got_part, part_sems.at[0])
    wait_all(carry_s, carry_sems.at[0])
    wait_all(tsend.at[rest], t_sems.at[0])
    wait_all(ss_got, ss_sems.at[0])
    wait_all(csend.at[rest], c_sems.at[0])
    wait_all(n_got, n_sems.at[0])


def write_kernel(docs_ref, rows_ref, writes_ref, keep_ref, docs_hbm, out_hbm, out_v, sems):
    parts = 4
    block = keep_ref.shape[0] // parts
    docs_copy = pltpu.make_async_copy(docs_ref, docs_hbm, sems.at[parts])
    docs_copy.start()
    high, low = halves(rows_ref[...])
    copies = []
    for i in range(parts):
        rows = pl.ds(i * block, block)
        writes = writes_ref[rows, :]
        out_v[rows, :] = (
            keep_ref[rows, :]
            + jnp.dot(writes, high, preferred_element_type=F32)
            + jnp.dot(writes, low, preferred_element_type=F32)
        )
        copies.append(pltpu.make_async_copy(out_v.at[rows], out_hbm.at[rows], sems.at[i]))
        copies[-1].start()
    docs_copy.wait()
    for copy in copies:
        copy.wait()


def shards(
    tokens, doc_ids, ln_gain, w_query, w_key, w_value, w_out, centroids, cluster_mass, assigned
):
    length = tokens.shape[0]
    width = w_out.shape[0]
    slots = assigned.shape[0]
    cents = centroids.shape[0]
    dp, mp = lax.axis_size("dp"), lax.axis_size("mp")

    def shape(*dims, dtype=F32):
        return jax.ShapeDtypeStruct(dims, dtype)

    vmem = pl.BlockSpec(memory_space=pltpu.VMEM)
    held = pl.pallas_call(
        rows_kernel,
        in_specs=[pl.BlockSpec(memory_space=pltpu.HBM)] * 7,
        out_specs=[vmem] * 8,
        out_shape=[
            shape(length // 16, 16, 2 * width, dtype=BF16),
            shape(length // 16, 16, width, dtype=BF16),
            shape(length // 16, 16, width, dtype=BF16),
            shape(SEGS, 1, width),
            shape(SEGS, width),
            shape(SEGS, 128, dtype=jnp.int32),
            shape(8 + SEGS, 128),
            shape(dp, 128),
        ],
        scratch_shapes=[
            pltpu.VMEM((1, length), jnp.int32),
            pltpu.VMEM((1, slots), jnp.int32),
            pltpu.VMEM((1, D), F32),
            pltpu.VMEM((length, D), BF16),
            pltpu.VMEM((D, 3 * width), BF16),
            pltpu.VMEM((length, D), BF16),
            pltpu.SMEM((SEGS, 128), jnp.int32),
            pltpu.VMEM((length + LONG, 2 * WIN), F32),
            pltpu.SemaphoreType.DMA((6,)),
            pltpu.SemaphoreType.DMA((8,)),
            pltpu.SemaphoreType.DMA,
        ],
        compiler_params=pltpu.CompilerParams(vmem_limit_bytes=40 << 20),
        name="rows",
    )(
        *[pltpu.with_memory_space_constraint(x, pltpu.HBM) for x in (
            doc_ids.reshape(1, length), assigned.reshape(1, slots), ln_gain.reshape(1, D), tokens,
            w_query, w_key, w_value)]
    )

    pair = pltpu.SemaphoreType.DMA((2,))
    new = pl.pallas_call(
        functools.partial(exchange_kernel, dp, mp),
        in_specs=[vmem] * 9 + [pl.BlockSpec(memory_space=pl.ANY)] * 2,
        out_specs=[vmem] * 4,
        out_shape=[
            shape(slots, width),
            shape(128, width),
            shape(cents, 128, dtype=BF16),
            shape(cents, width),
        ],
        scratch_shapes=[
            pltpu.SMEM((SEGS, 128), jnp.int32),
            pltpu.VMEM((SEGS, 1, width), F32),
            pltpu.VMEM((mp, slots, width), F32),
            pltpu.VMEM((mp, 8, width), F32),
            pltpu.VMEM((mp - 1, slots, width), F32),
            pltpu.VMEM((mp, 8, width), F32),
            pltpu.VMEM((dp, 1, 128), F32),
            pltpu.VMEM((dp, 1, 128), F32),
            pltpu.VMEM((8, 128), F32),
            pltpu.VMEM((mp - 1, 8, 128), F32),
            pltpu.VMEM((dp, 4, 128), F32),
            pltpu.VMEM((dp, 4, 128), F32),
            pltpu.VMEM((8, 128), F32),
            pltpu.VMEM((mp - 1, 8, 128), F32),
            pltpu.VMEM((width, D), BF16),
            pltpu.VMEM((cents, width), F32),
            pltpu.SemaphoreType.REGULAR,
            pltpu.SemaphoreType.DMA((2,)),
            pltpu.SemaphoreType.DMA,
            pair, pair, pair, pair, pair, pair,
        ],
        compiler_params=pltpu.CompilerParams(
            collective_id=0, has_side_effects=True, vmem_limit_bytes=24 << 20
        ),
        name="exchange",
    )(*held, cluster_mass.reshape(1, cents),
        *[pltpu.with_memory_space_constraint(x, pltpu.HBM) for x in (w_out, centroids)])

    anywhere = pl.BlockSpec(memory_space=pl.ANY)
    return pl.pallas_call(
        write_kernel,
        in_specs=[vmem] * 4,
        out_specs=[anywhere] * 2,
        out_shape=[shape(slots, width), shape(cents, width)],
        scratch_shapes=[pltpu.VMEM((cents, width), F32), pltpu.SemaphoreType.DMA((5,))],
        compiler_params=pltpu.CompilerParams(vmem_limit_bytes=16 << 20),
        name="write",
    )(*new)


def solution(mesh):
    placed = (
        P("dp", None),
        P("dp"),
        P(),
        P(None, "mp"),
        P(None, "mp"),
        P(None, "mp"),
        P("mp", None),
        P("dp", "mp"),
        P("dp"),
        P("dp"),
    )
    return jax.shard_map(
        shards,
        mesh=mesh,
        in_specs=placed,
        out_specs=(P("dp", "mp"), P("dp", "mp")),
        check_vma=False,
    )
```

```python
import functools
import math

import jax
import jax.numpy as jnp
from jax import lax
from jax.experimental import pallas as pl
from jax.experimental.pallas import tpu as pltpu
from jax.sharding import PartitionSpec as P

D = 1024
HEAD_DIM = 64
SEGS = 40
WIN = 128
LONG = 512
GROUP = 8
F32 = jnp.float32
BF16 = jnp.bfloat16
MESH = pl.DeviceIdType.MESH
NT = (((1,), (1,)), ((), ()))
NN = (((1,), (0,)), ((), ()))
EXP_SCALE = math.log2(math.e) / math.sqrt(HEAD_DIM)


def iota(shape, dim):
    return lax.broadcasted_iota(jnp.int32, shape, dim)


def halves(x):
    high = x.astype(BF16)
    return high, (x - high.astype(F32)).astype(BF16)


def to_column(row, n):
    full = jnp.broadcast_to(row, (n, n))
    return jnp.sum(jnp.where(iota((n, n), 0) == iota((n, n), 1), full, 0.0), axis=1, keepdims=True)


def to_row(column, n, width):
    full = jnp.broadcast_to(column, (n, width))
    return jnp.sum(jnp.where(iota((n, width), 0) == iota((n, width), 1), full, 0.0), axis=0, keepdims=True)


def block_sums(k, q2, v, bias, valid):
    s = lax.dot_general(k, q2, NT, preferred_element_type=F32) + bias
    top = jnp.max(s, axis=0, keepdims=True)
    p = jnp.exp2((s - top) * EXP_SCALE)
    total = jnp.sum(p, axis=0, keepdims=True)
    weighted = p * jnp.where(valid, 1.0 / total, 0.0)
    first = jnp.sum(weighted[:, :WIN], axis=1, keepdims=True)
    second = jnp.sum(weighted[:, WIN:], axis=1, keepdims=True)
    sums = jnp.where(iota((1, 128), 1) < HEAD_DIM, first, second)
    return jnp.sum(sums * v.astype(F32), axis=0, keepdims=True)


def rows_kernel(
    ids_hbm, assigned_hbm, gain_hbm, tokens_hbm, wq_hbm, wk_hbm, wv_hbm,
    q_ref, k_ref, v_ref, ctx_ref, bound_ref, meta_ref, target_ref,
    ids_v, assigned_v, gain_v, tokens_v, w_v, normed_v, bound_s, sc_s, sems, token_sems, bound_sem,
):
    length = q_ref.shape[0] * 16
    width = k_ref.shape[2]
    slots = 32
    parts = token_sems.shape[0]
    piece = length // parts
    r = lax.axis_index("dp")

    small = [
        pltpu.make_async_copy(src, dst, sems.at[i])
        for i, (src, dst) in enumerate(((ids_hbm, ids_v), (assigned_hbm, assigned_v), (gain_hbm, gain_v)))
    ]
    weights = [
        pltpu.make_async_copy(src, w_v.at[:, i * width : (i + 1) * width], sems.at[3 + i])
        for i, src in enumerate((wq_hbm, wk_hbm, wv_hbm))
    ]
    pieces = [
        pltpu.make_async_copy(
            tokens_hbm.at[pl.ds(i * piece, piece)], tokens_v.at[pl.ds(i * piece, piece)], token_sems.at[i]
        )
        for i in range(parts)
    ]
    for copy in small + pieces[:1] + weights + pieces[1:]:
        copy.start()
    small[2].wait()

    gain = gain_v[...]
    low_half = (iota((1, width), 1) & 127) < HEAD_DIM

    def norm(i):
        rows = slice(i * piece, (i + 1) * piece)
        x = tokens_v[rows, :].astype(F32)
        centered = x - jnp.mean(x, axis=1, keepdims=True)
        variance = jnp.mean(centered * centered, axis=1, keepdims=True)
        normed_v[rows, :] = (centered * lax.rsqrt(variance + 1e-05) * gain).astype(BF16)

    def project(at, half):
        rows = slice(at, at + half)
        blocks = slice(at // 16, (at + half) // 16)
        out = jnp.dot(normed_v[rows, :], w_v[...], preferred_element_type=F32)
        q = out[:, :width]
        q_ref[blocks, :, 0:width] = jnp.where(low_half, q, 0.0).astype(BF16).reshape(half // 16, 16, width)
        q_ref[blocks, :, width : 2 * width] = jnp.where(low_half, 0.0, q).astype(BF16).reshape(half // 16, 16, width)
        k_ref[blocks] = out[:, width : 2 * width].astype(BF16).reshape(half // 16, 16, width)
        v_ref[blocks] = out[:, 2 * width :].astype(BF16).reshape(half // 16, 16, width)

    qlane = iota((1, 2 * WIN), 1) & (WIN - 1)

    def taken(ref, at, n, c0):
        return ref[pl.ds(at // 16, n // 16), :, c0 : c0 + 128].reshape(n, 128)

    def queries(at, c0):
        return jnp.concatenate([taken(q_ref, at, WIN, c0), taken(q_ref, at, WIN, width + c0)], axis=0)

    for copy in small[:2]:
        copy.wait()

    local = ids_v[...] - r * slots
    seg = iota((SEGS, length), 0)
    own = seg < slots
    carried = seg == slots
    starts = jnp.sum(jnp.where(own & (local < seg), 1.0, 0.0), axis=1, keepdims=True)
    ends = jnp.sum(jnp.where((own & (local <= seg)) | (carried & (local < 0)), 1.0, 0.0), axis=1, keepdims=True)
    lane = iota((SEGS, 128), 1)
    at_row = jnp.minimum(jnp.floor(starts * (1.0 / 16.0)) * 16.0, float(length - WIN))
    fits = (ends - at_row <= float(WIN)) & (iota((SEGS, 1), 0) < slots)
    far = jnp.where(fits | ((iota((SEGS, 1), 0) >= slots) & (ends <= float(LONG))), 0.0, 1.0)
    far = jnp.max(far, axis=0, keepdims=True)
    bound_ref[...] = jnp.where(
        lane == 0,
        starts,
        jnp.where(lane == 1, ends, jnp.where(lane == 2, at_row * (1.0 / 16.0), jnp.where(lane == 3, starts - at_row, jnp.where(lane == 4, jnp.where(fits, ends, starts) - at_row, far)))),
    ).astype(jnp.int32)
    to_scalars = pltpu.make_async_copy(bound_ref, bound_s, bound_sem)
    to_scalars.start()
    ctx_ref[...] = jnp.zeros_like(ctx_ref)

    for i in range(parts // 2):
        pieces[i].wait()
        norm(i)
    for copy in weights + pieces[parts // 2 :]:
        copy.wait()
    project(0, length // 2)
    for i in range(parts // 2, parts):
        norm(i)
    counts = ends - starts
    picks = jnp.where((ends == float(length)) & (starts < float(length)), 1.0, 0.0)
    meta_ref[8:, :] = jnp.where(lane < 64, counts, picks)
    a_row = assigned_v[...]
    used_row = to_row(counts[:slots], slots, slots) > 0
    d_row = jnp.where(used_row, ((a_row >> 10) - r) & 63, -1)
    d_col = to_column(d_row.astype(F32), slots)
    before = iota((slots, slots), 0) < iota((slots, slots), 1)
    same = d_col == d_row.astype(F32)
    rank_row = jnp.sum(jnp.where(before & same, 1.0, 0.0), axis=0, keepdims=True)
    spot = iota((64, slots), 0)
    local_row = ((a_row & 1023) + 1).astype(F32)
    here = spot == d_row
    first = jnp.sum(jnp.where(here & (rank_row == 0.0), local_row, 0.0), axis=1, keepdims=True)
    second = jnp.sum(jnp.where(here & (rank_row == 1.0), local_row, 0.0), axis=1, keepdims=True)
    place = (64 - iota((64, 128), 0)) & 63
    lane64 = iota((64, 128), 1)
    target_ref[...] = jnp.where(lane64 == place, first, 0.0) + jnp.where(lane64 == place + 64, second, 0.0)
    pick = (iota((slots, 128), 1) & 31) == iota((slots, 128), 0)
    rank_col = to_column(rank_row, slots)
    d_wide = jnp.sum(jnp.where(pick, d_col, 0.0), axis=0, keepdims=True)
    rank_wide = jnp.sum(jnp.where(pick, rank_col, 0.0), axis=0, keepdims=True)
    meta_ref[:8, :] = jnp.where(iota((8, 128), 0) == 0, d_wide, rank_wide)
    carried_end = jnp.where(ends[slots:slots + 1] <= float(LONG), ends[slots:slots + 1], 0.0).astype(jnp.int32)
    carried_bias = jnp.where(iota((LONG, 1), 0) < carried_end, 0.0, -1e30)
    for pair in range(width // 128):
        c0 = pair * 128
        total = jnp.zeros((1, 128), F32)
        for i in range(LONG // WIN):
            total = total + block_sums(
                taken(k_ref, 0, LONG, c0), queries(i * WIN, c0), taken(v_ref, 0, LONG, c0),
                carried_bias, qlane < carried_end - i * WIN,
            )
        ctx_ref[slots, :, c0 : c0 + 128] = total

    project(length // 2, length // 2)

    to_scalars.wait()
    def long(seg, start, end, reach):
        first = (start // 16) * 16
        base = pl.multiple_of(jnp.minimum(first, length - reach), 16)
        row = iota((reach, 1), 0)
        bias = jnp.where((row >= start - base) & (row < end - base), 0.0, -1e30)

        @pl.loop(0, (end - first + WIN - 1) // WIN)
        def _(i):
            qs = first + i * WIN
            at = pl.multiple_of(jnp.minimum(qs, length - WIN), 16)
            valid = (qlane >= jnp.maximum(start, qs) - at) & (qlane < end - at)
            for pair in range(width // 128):
                c0 = pair * 128
                ctx_ref[seg, :, c0 : c0 + 128] += block_sums(
                    taken(k_ref, base, reach, c0), queries(at, c0), taken(v_ref, base, reach, c0), bias, valid
                )

    def longest(seg, start, end):
        first = (start // 16) * 16
        n_k = (end - first + LONG - 1) // LONG
        row = iota((LONG, 1), 0)

        def k_rows(i):
            at = pl.multiple_of(jnp.minimum(first + i * LONG, length - LONG), 16)
            low = jnp.maximum(start, first + i * LONG) - at
            bias = jnp.where((row >= low) & (row < end - at), 0.0, -1e30)
            return at, pl.ds(pl.multiple_of(i * LONG, LONG), LONG), bias

        @pl.loop(0, (end - first + WIN - 1) // WIN)
        def _(iq):
            qs = first + iq * WIN
            qat = pl.multiple_of(jnp.minimum(qs, length - WIN), 16)
            valid = (qlane >= jnp.maximum(start, qs) - qat) & (qlane < end - qat)
            for pair in range(width // 128):
                c0 = pair * 128
                q2 = queries(qat, c0)

                def scores(i, top):
                    krows, held, bias = k_rows(i)
                    s = lax.dot_general(taken(k_ref, krows, LONG, c0), q2, NT, preferred_element_type=F32) + bias
                    sc_s[held, :] = s
                    return jnp.maximum(top, jnp.max(s, axis=0, keepdims=True))

                top = lax.fori_loop(0, n_k, scores, jnp.full((1, 2 * WIN), -2e30, F32))

                def raise_all(i, total):
                    krows, held, bias = k_rows(i)
                    p = jnp.exp2((sc_s[held, :] - top) * EXP_SCALE)
                    sc_s[held, :] = p
                    return total + jnp.sum(p, axis=0, keepdims=True)

                total = lax.fori_loop(0, n_k, raise_all, jnp.zeros((1, 2 * WIN), F32))
                inverse = jnp.where(valid, 1.0 / total, 0.0)

                def weigh(i, acc):
                    krows, held, bias = k_rows(i)
                    weighted = sc_s[held, :] * inverse
                    one = jnp.sum(weighted[:, :WIN], axis=1, keepdims=True)
                    two = jnp.sum(weighted[:, WIN:], axis=1, keepdims=True)
                    sums = jnp.where(iota((1, 128), 1) < HEAD_DIM, one, two)
                    return acc + jnp.sum(sums * taken(v_ref, krows, LONG, c0).astype(F32), axis=0, keepdims=True)

                ctx_ref[seg, :, c0 : c0 + 128] += lax.fori_loop(0, n_k, weigh, jnp.zeros((1, 128), F32))

    @pl.when(bound_s[0, 5] > 0)
    def _():
        @pl.loop(0, slots + 1)
        def _(seg):
            start = bound_s[seg, 0]
            end = bound_s[seg, 1]
            first = (start // 16) * 16

            @pl.when((end - jnp.minimum(first, length - WIN) > WIN) & ((seg < slots) | (end > LONG)))
            def _():
                @pl.when(end - first <= 256)
                def _():
                    long(seg, start, end, 256)

                @pl.when((end - first > 256) & (end - first <= 512))
                def _():
                    long(seg, start, end, 512)

                @pl.when(end - first > 512)
                def _():
                    longest(seg, start, end)


def exchange_kernel(
    dp, mp, q_ref, k_ref, v_ref, ctx_ref, bound_ref, meta_ref, target_ref, mass_ref,
    wo_hbm, cent_hbm, tokens_hbm, ids_hbm,
    docs_ref, rows_ref, writes_ref, keep_ref,
    bound_s, ctx_s, part_s, carry_s, got_part, got_carry, tsend, tgot, ss_send, ss_got, csend, cgot, n_send, n_got,
    wo_ref, cent_ref, own_v, ids_v, ready, late_sems, bound_sem, part_sems, carry_sems, t_sems, ss_sems, c_sems, n_sems,
):
    r = lax.axis_index("dp")
    m = lax.axis_index("mp")
    slots = 32
    cents, width = cent_ref.shape
    length = own_v.shape[0]
    load_wo = pltpu.make_async_copy(wo_hbm, wo_ref, late_sems.at[0])
    load_cent = pltpu.make_async_copy(cent_hbm, cent_ref, late_sems.at[1])
    columns = pl.ds(pl.multiple_of(m * width, width), width)
    load_own = pltpu.make_async_copy(tokens_hbm.at[:, columns], own_v, late_sems.at[2])
    load_ids = pltpu.make_async_copy(ids_hbm, ids_v, late_sems.at[3])
    for load in (load_ids, load_own, load_wo, load_cent):
        load.start()
    to_scalars = pltpu.make_async_copy(bound_ref, bound_s, bound_sem)
    to_scalars.start()

    barrier = pltpu.get_barrier_semaphore()
    nxt = lax.rem(r + 1, dp)
    prv = lax.rem(r + dp - 1, dp)
    plane = 8
    layers = dp // plane
    mine = lax.rem(r, plane)

    def along_z(i):
        return lax.rem(r + i * plane, dp)

    for dm in range(1, mp):
        pl.semaphore_signal(barrier, inc=1, device_id=(r, lax.rem(m + dm, mp)), device_id_type=MESH)
    for mm in range(mp):
        pl.semaphore_signal(barrier, inc=1, device_id=(nxt, mm), device_id_type=MESH)
    for i in range(1, layers):
        pl.semaphore_signal(barrier, inc=1, device_id=(along_z(i), m), device_id_type=MESH)
    for i in range(1, plane):
        peer = r - mine + lax.rem(mine + i, plane)
        pl.semaphore_signal(barrier, inc=1, device_id=(peer, m), device_id_type=MESH)

    tsend[...] = target_ref[...].reshape(dp, 1, 128)
    tgot[0] = tsend[0]
    to_scalars.wait()
    krow = iota((WIN, 1), 0)
    qlane = iota((1, 2 * WIN), 1) & (WIN - 1)

    def short(seg):
        block = bound_s[seg, 2]
        low = bound_s[seg, 3]
        high = bound_s[seg, 4]
        bias = jnp.where((krow >= low) & (krow < high), 0.0, -1e30)
        valid = (qlane >= low) & (qlane < high)
        q = jnp.concatenate([q_ref[block + i] for i in range(WIN // 16)], axis=0)
        k = jnp.concatenate([k_ref[block + i] for i in range(WIN // 16)], axis=0)
        v = jnp.concatenate([v_ref[block + i] for i in range(WIN // 16)], axis=0)
        for pair in range(width // 128):
            c0 = pair * 128
            q2 = jnp.concatenate([q[:, c0 : c0 + 128], q[:, width + c0 : width + c0 + 128]], axis=0)
            ctx_s[seg, :, c0 : c0 + 128] = ctx_ref[seg, :, c0 : c0 + 128] + block_sums(
                k[:, c0 : c0 + 128], q2, v[:, c0 : c0 + 128], bias, valid
            )

    def to_peer(src, dst, sems, dm):
        mm = lax.rem(m + dm, mp)
        return pltpu.make_async_remote_copy(
            src_ref=src, dst_ref=dst, send_sem=sems.at[0], recv_sem=sems.at[1],
            device_id=(r, mm), device_id_type=MESH,
        )

    def far_first(i):
        def order(k):
            odd = k % 2
            return 4 - odd * ((k + 1) // 2) + (1 - odd) * (k // 2)

        return order(i // 8) * 8 + order(i % 8)

    def wait_all(buffer, sem):
        pltpu.make_async_copy(buffer, buffer, sem).wait()

    def out_project(rows):
        high, low = halves(rows)
        return jnp.dot(high, wo_ref[...], preferred_element_type=F32) + jnp.dot(
            low, wo_ref[...], preferred_element_type=F32
        )

    before = slots // GROUP - 1

    @pl.loop(0, before)
    def _(group):
        for j in range(GROUP):
            short(group * GROUP + j)

    load_ids.wait()
    load_own.wait()
    local = ids_v[...] - r * slots
    member = jnp.where(iota((SEGS, length), 0) == jnp.where(local < 0, slots, local), 1.0, 0.0).astype(BF16)
    tok = jnp.dot(member, own_v[...], preferred_element_type=F32)

    load_wo.wait()
    carried = out_project(ctx_ref[slots:].reshape(SEGS - slots, width))
    row8 = iota((8, width), 0)
    carried_count = meta_ref[8 + slots : 9 + slots, 0:1]
    for mm in range(mp):
        block = carried[:, mm * width : (mm + 1) * width] + jnp.where(m == mm, tok[slots:], 0.0)
        carry_s[mm] = jnp.where(row8 == 1, carried_count, block)

    pl.semaphore_wait(barrier, mp - 1 + mp + layers - 1 + plane - 1)
    for mm in range(mp):
        pltpu.make_async_remote_copy(
            src_ref=carry_s.at[mm], dst_ref=got_carry.at[m], send_sem=carry_sems.at[0],
            recv_sem=carry_sems.at[1], device_id=(prv, mm), device_id_type=MESH,
        ).start()
    for i in range(1, layers):
        pl.semaphore_signal(ready, inc=1, device_id=(along_z(i), m), device_id_type=MESH)

    for j in range(GROUP):
        short(before * GROUP + j)

    projected = out_project(ctx_s[:slots].reshape(slots, width))
    for mm in range(mp):
        part_s[mm] = projected[:, mm * width : (mm + 1) * width] + jnp.where(m == mm, tok[:slots], 0.0)
    for dm in range(1, mp):
        to_peer(part_s.at[lax.rem(m + dm, mp)], got_part.at[mp - 1 - dm], part_sems, dm).start()

    d_wide = meta_ref[0:1, :]
    rank_wide = meta_ref[1:2, :]
    row = iota((8 * dp, 128), 0)
    col = iota((8 * dp, 128), 1)
    j = row & 7
    pick = (
        ((row >> 3).astype(F32) == d_wide)
        & ((j >> 1).astype(F32) == rank_wide)
        & ((j & 1) == ((col >> 5) & 1))
    )
    pick = jnp.where(pick, 1.0, 0.0).astype(BF16)

    wait_all(got_carry, carry_sems.at[1])
    carry = got_carry[0]
    for i in range(1, mp):
        carry = carry + got_carry[i]
    count_in = got_carry[0][1:2, :]
    counts = meta_ref[8 : 8 + slots, 0:1]
    picks = meta_ref[8 : 8 + slots, 64:65]
    sums = part_s[m] + picks * carry[0:1, :]
    inverse = 1.0 / jnp.maximum(counts + picks * count_in, 1.0)
    wait_all(got_part, part_sems.at[1])
    for i in range(mp - 1):
        sums = sums + got_part[i]
    averages = sums * inverse
    squares = jnp.sum(averages * averages, axis=1, keepdims=True)
    square_row = to_row(squares, slots, 128)
    ss_send[...] = jnp.broadcast_to(square_row, (8, 128))
    for dm in range(1, mp):
        to_peer(ss_send, ss_got.at[mp - 1 - dm], ss_sems, dm).start()
    pl.semaphore_wait(ready, layers - 1)

    @pl.loop(1, dp)
    def _(d):
        pltpu.make_async_remote_copy(
            src_ref=tsend.at[d], dst_ref=tgot.at[dp - d], send_sem=t_sems.at[0], recv_sem=t_sems.at[1],
            device_id=(lax.rem(r + d, dp), m), device_id_type=MESH,
        ).start()

    wait_all(ss_got, ss_sems.at[1])
    for i in range(mp - 1):
        square_row = square_row + ss_got[i][0:1, :]
    eye = iota((slots, 128), 0) == iota((slots, 128), 1)
    squares = jnp.sum(jnp.where(eye, square_row, 0.0), axis=1, keepdims=True)
    vectors = averages * lax.rsqrt(squares * (1.0 / D) + 1e-06)

    high, low = halves(vectors)
    high, low = high.astype(F32), low.astype(F32)
    stacked = jnp.concatenate([high[:, :128], high[:, 128:], low[:, :128], low[:, 128:]], axis=0).astype(BF16)
    outgoing = jnp.dot(pick, stacked, preferred_element_type=F32).reshape(dp, 8, 128)
    csend[...] = outgoing[:, :4, :]
    cgot[0] = csend[0]

    @pl.loop(0, dp - 1)
    def _(i):
        d = far_first(i)
        pltpu.make_async_remote_copy(
            src_ref=csend.at[d], dst_ref=cgot.at[dp - d], send_sem=c_sems.at[0], recv_sem=c_sems.at[1],
            device_id=(lax.rem(r + d, dp), m), device_id_type=MESH,
        ).start()

    docs_ref[...] = vectors

    rest = pl.ds(1, dp - 1)
    wait_all(tgot.at[rest], t_sems.at[1])
    tgt_row = jnp.sum(tgot[...], axis=0)
    tgt_col = to_column(tgt_row, 128)
    hits = jnp.where(iota((128, cents), 1).astype(F32) == tgt_col - 1.0, 1.0, 0.0)
    mass = jnp.sum(hits * mass_ref[...], axis=1, keepdims=True)
    hits = hits.astype(BF16)
    load_cent.wait()
    cent_high, cent_low = halves(cent_ref[...])
    picked = jnp.dot(hits, cent_high, preferred_element_type=F32) + jnp.dot(
        hits, cent_low, preferred_element_type=F32
    )
    start = mass * picked
    together = jnp.where((tgt_col == tgt_row) & (tgt_row > 0.0), 1.0, 0.0).astype(BF16)
    earlier = iota((128, 128), 0) < iota((128, 128), 1)
    repeats = jnp.sum(jnp.where(earlier & (tgt_col == tgt_row), 1.0, 0.0), axis=0, keepdims=True)
    wanted = jnp.where(repeats == 0.0, tgt_row - 1.0, -1.0)
    writes = jnp.where(iota((cents, 128), 0).astype(F32) == wanted, 1.0, 0.0)
    keep_ref[...] = jnp.where(jnp.sum(writes, axis=1, keepdims=True) > 0.0, 0.0, cent_ref[...])
    writes_ref[...] = writes.astype(BF16)

    wait_all(cgot.at[rest], c_sems.at[1])
    arrived = jnp.concatenate(
        [jnp.concatenate([cgot[:, 2 * k, :], cgot[:, 2 * k + 1, :]], axis=1) for k in range(2)], axis=0
    )
    high, low = halves(arrived)
    blended = start + (
        jnp.dot(together, high, preferred_element_type=F32) + jnp.dot(together, low, preferred_element_type=F32)
    )
    norm_row = to_row(jnp.sum(blended * blended, axis=1, keepdims=True), 128, 128)
    n_send[...] = jnp.broadcast_to(norm_row, (8, 128))
    for dm in range(1, mp):
        to_peer(n_send, n_got.at[mp - 1 - dm], n_sems, dm).start()
    wait_all(n_got, n_sems.at[1])
    for i in range(mp - 1):
        norm_row = norm_row + n_got[i][0:1, :]
    norms = to_column(norm_row, 128)
    rows_ref[...] = blended * lax.rsqrt(norms * (1.0 / D) + 1e-06)

    wait_all(got_part, part_sems.at[0])
    wait_all(carry_s, carry_sems.at[0])
    wait_all(tsend.at[rest], t_sems.at[0])
    wait_all(ss_got, ss_sems.at[0])
    wait_all(csend.at[rest], c_sems.at[0])
    wait_all(n_got, n_sems.at[0])


def write_kernel(docs_ref, rows_ref, writes_ref, keep_ref, docs_hbm, out_hbm, out_v, sems):
    parts = 4
    block = keep_ref.shape[0] // parts
    docs_copy = pltpu.make_async_copy(docs_ref, docs_hbm, sems.at[parts])
    docs_copy.start()
    high, low = halves(rows_ref[...])
    copies = []
    for i in range(parts):
        rows = pl.ds(i * block, block)
        writes = writes_ref[rows, :]
        out_v[rows, :] = (
            keep_ref[rows, :]
            + jnp.dot(writes, high, preferred_element_type=F32)
            + jnp.dot(writes, low, preferred_element_type=F32)
        )
        copies.append(pltpu.make_async_copy(out_v.at[rows], out_hbm.at[rows], sems.at[i]))
        copies[-1].start()
    docs_copy.wait()
    for copy in copies:
        copy.wait()


def shards(
    tokens, doc_ids, ln_gain, w_query, w_key, w_value, w_out, centroids, cluster_mass, assigned
):
    length = tokens.shape[0]
    width = w_out.shape[0]
    slots = assigned.shape[0]
    cents = centroids.shape[0]
    dp, mp = lax.axis_size("dp"), lax.axis_size("mp")

    def shape(*dims, dtype=F32):
        return jax.ShapeDtypeStruct(dims, dtype)

    vmem = pl.BlockSpec(memory_space=pltpu.VMEM)
    held = pl.pallas_call(
        rows_kernel,
        in_specs=[pl.BlockSpec(memory_space=pltpu.HBM)] * 7,
        out_specs=[vmem] * 7,
        out_shape=[
            shape(length // 16, 16, 2 * width, dtype=BF16),
            shape(length // 16, 16, width, dtype=BF16),
            shape(length // 16, 16, width, dtype=BF16),
            shape(SEGS, 1, width),
            shape(SEGS, 128, dtype=jnp.int32),
            shape(8 + SEGS, 128),
            shape(dp, 128),
        ],
        scratch_shapes=[
            pltpu.VMEM((1, length), jnp.int32),
            pltpu.VMEM((1, slots), jnp.int32),
            pltpu.VMEM((1, D), F32),
            pltpu.VMEM((length, D), BF16),
            pltpu.VMEM((D, 3 * width), BF16),
            pltpu.VMEM((length, D), BF16),
            pltpu.SMEM((SEGS, 128), jnp.int32),
            pltpu.VMEM((length + LONG, 2 * WIN), F32),
            pltpu.SemaphoreType.DMA((6,)),
            pltpu.SemaphoreType.DMA((4,)),
            pltpu.SemaphoreType.DMA,
        ],
        compiler_params=pltpu.CompilerParams(vmem_limit_bytes=40 << 20),
        name="rows",
    )(
        *[pltpu.with_memory_space_constraint(x, pltpu.HBM) for x in (
            doc_ids.reshape(1, length), assigned.reshape(1, slots), ln_gain.reshape(1, D), tokens,
            w_query, w_key, w_value)]
    )

    pair = pltpu.SemaphoreType.DMA((2,))
    new = pl.pallas_call(
        functools.partial(exchange_kernel, dp, mp),
        in_specs=[vmem] * 8 + [pl.BlockSpec(memory_space=pl.ANY)] * 4,
        out_specs=[vmem] * 4,
        out_shape=[
            shape(slots, width),
            shape(128, width),
            shape(cents, 128, dtype=BF16),
            shape(cents, width),
        ],
        scratch_shapes=[
            pltpu.SMEM((SEGS, 128), jnp.int32),
            pltpu.VMEM((slots, 1, width), F32),
            pltpu.VMEM((mp, slots, width), F32),
            pltpu.VMEM((mp, 8, width), F32),
            pltpu.VMEM((mp - 1, slots, width), F32),
            pltpu.VMEM((mp, 8, width), F32),
            pltpu.VMEM((dp, 1, 128), F32),
            pltpu.VMEM((dp, 1, 128), F32),
            pltpu.VMEM((8, 128), F32),
            pltpu.VMEM((mp - 1, 8, 128), F32),
            pltpu.VMEM((dp, 4, 128), F32),
            pltpu.VMEM((dp, 4, 128), F32),
            pltpu.VMEM((8, 128), F32),
            pltpu.VMEM((mp - 1, 8, 128), F32),
            pltpu.VMEM((width, D), BF16),
            pltpu.VMEM((cents, width), F32),
            pltpu.VMEM((length, width), BF16),
            pltpu.VMEM((1, length), jnp.int32),
            pltpu.SemaphoreType.REGULAR,
            pltpu.SemaphoreType.DMA((4,)),
            pltpu.SemaphoreType.DMA,
            pair, pair, pair, pair, pair, pair,
        ],
        compiler_params=pltpu.CompilerParams(
            collective_id=0, has_side_effects=True, vmem_limit_bytes=24 << 20
        ),
        name="exchange",
    )(*held, cluster_mass.reshape(1, cents),
        *[pltpu.with_memory_space_constraint(x, pltpu.HBM)
          for x in (w_out, centroids, tokens, doc_ids.reshape(1, length))])

    anywhere = pl.BlockSpec(memory_space=pl.ANY)
    return pl.pallas_call(
        write_kernel,
        in_specs=[vmem] * 4,
        out_specs=[anywhere] * 2,
        out_shape=[shape(slots, width), shape(cents, width)],
        scratch_shapes=[pltpu.VMEM((cents, width), F32), pltpu.SemaphoreType.DMA((5,))],
        compiler_params=pltpu.CompilerParams(vmem_limit_bytes=16 << 20),
        name="write",
    )(*new)


def solution(mesh):
    placed = (
        P("dp", None),
        P("dp"),
        P(),
        P(None, "mp"),
        P(None, "mp"),
        P(None, "mp"),
        P("mp", None),
        P("dp", "mp"),
        P("dp"),
        P("dp"),
    )
    return jax.shard_map(
        shards,
        mesh=mesh,
        in_specs=placed,
        out_specs=(P("dp", "mp"), P("dp", "mp")),
        check_vma=False,
    )
```

```python
import functools
import math

import jax
import jax.numpy as jnp
from jax import lax
from jax.experimental import pallas as pl
from jax.experimental.pallas import tpu as pltpu
from jax.sharding import PartitionSpec as P

D = 1024
HEAD_DIM = 64
SEGS = 40
WIN = 128
LONG = 512
GROUP = 32
F32 = jnp.float32
BF16 = jnp.bfloat16
MESH = pl.DeviceIdType.MESH
NT = (((1,), (1,)), ((), ()))
NN = (((1,), (0,)), ((), ()))
EXP_SCALE = math.log2(math.e) / math.sqrt(HEAD_DIM)


def iota(shape, dim):
    return lax.broadcasted_iota(jnp.int32, shape, dim)


def halves(x):
    high = x.astype(BF16)
    return high, (x - high.astype(F32)).astype(BF16)


def to_column(row, n):
    full = jnp.broadcast_to(row, (n, n))
    return jnp.sum(jnp.where(iota((n, n), 0) == iota((n, n), 1), full, 0.0), axis=1, keepdims=True)


def to_row(column, n, width):
    full = jnp.broadcast_to(column, (n, width))
    return jnp.sum(jnp.where(iota((n, width), 0) == iota((n, width), 1), full, 0.0), axis=0, keepdims=True)


def block_sums(k, q2, v, bias, valid):
    s = lax.dot_general(k, q2, NT, preferred_element_type=F32) + bias
    top = jnp.max(s, axis=0, keepdims=True)
    p = jnp.exp2((s - top) * EXP_SCALE)
    total = jnp.sum(p, axis=0, keepdims=True)
    weighted = p * jnp.where(valid, 1.0 / total, 0.0)
    first = jnp.sum(weighted[:, :WIN], axis=1, keepdims=True)
    second = jnp.sum(weighted[:, WIN:], axis=1, keepdims=True)
    sums = jnp.where(iota((1, 128), 1) < HEAD_DIM, first, second)
    return jnp.sum(sums * v.astype(F32), axis=0, keepdims=True)


def rows_kernel(
    ids_hbm, assigned_hbm, gain_hbm, tokens_hbm, wq_hbm, wk_hbm, wv_hbm,
    q_ref, k_ref, v_ref, ctx_ref, tok_ref, bound_ref, meta_ref, target_ref,
    ids_v, assigned_v, gain_v, tokens_v, w_v, normed_v, bound_s, sc_s, sems, token_sems, bound_sem,
):
    length = q_ref.shape[0] * 16
    width = k_ref.shape[2]
    slots = 32
    parts = token_sems.shape[0]
    piece = length // parts
    r = lax.axis_index("dp")
    m = lax.axis_index("mp")

    small = [
        pltpu.make_async_copy(src, dst, sems.at[i])
        for i, (src, dst) in enumerate(((ids_hbm, ids_v), (assigned_hbm, assigned_v), (gain_hbm, gain_v)))
    ]
    weights = [
        pltpu.make_async_copy(src, w_v.at[:, i * width : (i + 1) * width], sems.at[3 + i])
        for i, src in enumerate((wq_hbm, wk_hbm, wv_hbm))
    ]
    pieces = [
        pltpu.make_async_copy(
            tokens_hbm.at[pl.ds(i * piece, piece)], tokens_v.at[pl.ds(i * piece, piece)], token_sems.at[i]
        )
        for i in range(parts)
    ]
    for copy in small + pieces[:1] + weights + pieces[1:]:
        copy.start()
    small[2].wait()

    gain = gain_v[...]
    low_half = (iota((1, width), 1) & 127) < HEAD_DIM

    def norm(i):
        rows = slice(i * piece, (i + 1) * piece)
        x = tokens_v[rows, :].astype(F32)
        centered = x - jnp.mean(x, axis=1, keepdims=True)
        variance = jnp.mean(centered * centered, axis=1, keepdims=True)
        normed_v[rows, :] = (centered * lax.rsqrt(variance + 1e-05) * gain).astype(BF16)

    def project(at, half):
        rows = slice(at, at + half)
        blocks = slice(at // 16, (at + half) // 16)
        out = jnp.dot(normed_v[rows, :], w_v[...], preferred_element_type=F32)
        q = out[:, :width]
        q_ref[blocks, :, 0:width] = jnp.where(low_half, q, 0.0).astype(BF16).reshape(half // 16, 16, width)
        q_ref[blocks, :, width : 2 * width] = jnp.where(low_half, 0.0, q).astype(BF16).reshape(half // 16, 16, width)
        k_ref[blocks] = out[:, width : 2 * width].astype(BF16).reshape(half // 16, 16, width)
        v_ref[blocks] = out[:, 2 * width :].astype(BF16).reshape(half // 16, 16, width)

    qlane = iota((1, 2 * WIN), 1) & (WIN - 1)

    def taken(ref, at, n, c0):
        return ref[pl.ds(at // 16, n // 16), :, c0 : c0 + 128].reshape(n, 128)

    def queries(at, c0):
        return jnp.concatenate([taken(q_ref, at, WIN, c0), taken(q_ref, at, WIN, width + c0)], axis=0)

    for copy in small[:2]:
        copy.wait()

    local = ids_v[...] - r * slots
    seg = iota((SEGS, length), 0)
    own = seg < slots
    carried = seg == slots
    starts = jnp.sum(jnp.where(own & (local < seg), 1.0, 0.0), axis=1, keepdims=True)
    ends = jnp.sum(jnp.where((own & (local <= seg)) | (carried & (local < 0)), 1.0, 0.0), axis=1, keepdims=True)
    lane = iota((SEGS, 128), 1)
    at_row = jnp.minimum(jnp.floor(starts * (1.0 / 16.0)) * 16.0, float(length - WIN))
    fits = (ends - at_row <= float(WIN)) & (iota((SEGS, 1), 0) < slots)
    far = jnp.where(fits | ((iota((SEGS, 1), 0) >= slots) & (ends <= float(LONG))), 0.0, 1.0)
    far = jnp.max(far, axis=0, keepdims=True)
    bound_ref[...] = jnp.where(
        lane == 0,
        starts,
        jnp.where(lane == 1, ends, jnp.where(lane == 2, at_row * (1.0 / 16.0), jnp.where(lane == 3, starts - at_row, jnp.where(lane == 4, jnp.where(fits, ends, starts) - at_row, far)))),
    ).astype(jnp.int32)
    to_scalars = pltpu.make_async_copy(bound_ref, bound_s, bound_sem)
    to_scalars.start()
    ctx_ref[...] = jnp.zeros_like(ctx_ref)

    for i in range(parts // 2):
        pieces[i].wait()
        norm(i)
    for copy in weights + pieces[parts // 2 :]:
        copy.wait()
    project(0, length // 2)
    for i in range(parts // 2, parts):
        norm(i)
    counts = ends - starts
    picks = jnp.where((ends == float(length)) & (starts < float(length)), 1.0, 0.0)
    meta_ref[8:, :] = jnp.where(lane < 64, counts, picks)
    a_row = assigned_v[...]
    used_row = to_row(counts[:slots], slots, slots) > 0
    d_row = jnp.where(used_row, ((a_row >> 10) - r) & 63, -1)
    d_col = to_column(d_row.astype(F32), slots)
    before = iota((slots, slots), 0) < iota((slots, slots), 1)
    same = d_col == d_row.astype(F32)
    rank_row = jnp.sum(jnp.where(before & same, 1.0, 0.0), axis=0, keepdims=True)
    spot = iota((64, slots), 0)
    local_row = ((a_row & 1023) + 1).astype(F32)
    here = spot == d_row
    first = jnp.sum(jnp.where(here & (rank_row == 0.0), local_row, 0.0), axis=1, keepdims=True)
    second = jnp.sum(jnp.where(here & (rank_row == 1.0), local_row, 0.0), axis=1, keepdims=True)
    place = (64 - iota((64, 128), 0)) & 63
    lane64 = iota((64, 128), 1)
    target_ref[...] = jnp.where(lane64 == place, first, 0.0) + jnp.where(lane64 == place + 64, second, 0.0)
    pick = (iota((slots, 128), 1) & 31) == iota((slots, 128), 0)
    rank_col = to_column(rank_row, slots)
    d_wide = jnp.sum(jnp.where(pick, d_col, 0.0), axis=0, keepdims=True)
    rank_wide = jnp.sum(jnp.where(pick, rank_col, 0.0), axis=0, keepdims=True)
    meta_ref[:8, :] = jnp.where(iota((8, 128), 0) == 0, d_wide, rank_wide)
    carried_end = jnp.where(ends[slots:slots + 1] <= float(LONG), ends[slots:slots + 1], 0.0).astype(jnp.int32)
    carried_bias = jnp.where(iota((LONG, 1), 0) < carried_end, 0.0, -1e30)
    for pair in range(width // 128):
        c0 = pair * 128
        total = jnp.zeros((1, 128), F32)
        for i in range(LONG // WIN):
            total = total + block_sums(
                taken(k_ref, 0, LONG, c0), queries(i * WIN, c0), taken(v_ref, 0, LONG, c0),
                carried_bias, qlane < carried_end - i * WIN,
            )
        ctx_ref[slots, :, c0 : c0 + 128] = total

    project(length // 2, length // 2)

    seg_of = jnp.where(local < 0, slots, local)
    member = jnp.where(seg == seg_of, 1.0, 0.0).astype(BF16)
    columns = pl.ds(pl.multiple_of(m * width, width), width)
    tok_ref[...] = jnp.dot(member, tokens_v[:, columns], preferred_element_type=F32)

    to_scalars.wait()
    def long(seg, start, end, reach):
        first = (start // 16) * 16
        base = pl.multiple_of(jnp.minimum(first, length - reach), 16)
        row = iota((reach, 1), 0)
        bias = jnp.where((row >= start - base) & (row < end - base), 0.0, -1e30)

        @pl.loop(0, (end - first + WIN - 1) // WIN)
        def _(i):
            qs = first + i * WIN
            at = pl.multiple_of(jnp.minimum(qs, length - WIN), 16)
            valid = (qlane >= jnp.maximum(start, qs) - at) & (qlane < end - at)
            for pair in range(width // 128):
                c0 = pair * 128
                ctx_ref[seg, :, c0 : c0 + 128] += block_sums(
                    taken(k_ref, base, reach, c0), queries(at, c0), taken(v_ref, base, reach, c0), bias, valid
                )

    def longest(seg, start, end):
        first = (start // 16) * 16
        n_k = (end - first + LONG - 1) // LONG
        row = iota((LONG, 1), 0)

        def k_rows(i):
            at = pl.multiple_of(jnp.minimum(first + i * LONG, length - LONG), 16)
            low = jnp.maximum(start, first + i * LONG) - at
            bias = jnp.where((row >= low) & (row < end - at), 0.0, -1e30)
            return at, pl.ds(pl.multiple_of(i * LONG, LONG), LONG), bias

        @pl.loop(0, (end - first + WIN - 1) // WIN)
        def _(iq):
            qs = first + iq * WIN
            qat = pl.multiple_of(jnp.minimum(qs, length - WIN), 16)
            valid = (qlane >= jnp.maximum(start, qs) - qat) & (qlane < end - qat)
            for pair in range(width // 128):
                c0 = pair * 128
                q2 = queries(qat, c0)

                def scores(i, top):
                    krows, held, bias = k_rows(i)
                    s = lax.dot_general(taken(k_ref, krows, LONG, c0), q2, NT, preferred_element_type=F32) + bias
                    sc_s[held, :] = s
                    return jnp.maximum(top, jnp.max(s, axis=0, keepdims=True))

                top = lax.fori_loop(0, n_k, scores, jnp.full((1, 2 * WIN), -2e30, F32))

                def raise_all(i, total):
                    krows, held, bias = k_rows(i)
                    p = jnp.exp2((sc_s[held, :] - top) * EXP_SCALE)
                    sc_s[held, :] = p
                    return total + jnp.sum(p, axis=0, keepdims=True)

                total = lax.fori_loop(0, n_k, raise_all, jnp.zeros((1, 2 * WIN), F32))
                inverse = jnp.where(valid, 1.0 / total, 0.0)

                def weigh(i, acc):
                    krows, held, bias = k_rows(i)
                    weighted = sc_s[held, :] * inverse
                    one = jnp.sum(weighted[:, :WIN], axis=1, keepdims=True)
                    two = jnp.sum(weighted[:, WIN:], axis=1, keepdims=True)
                    sums = jnp.where(iota((1, 128), 1) < HEAD_DIM, one, two)
                    return acc + jnp.sum(sums * taken(v_ref, krows, LONG, c0).astype(F32), axis=0, keepdims=True)

                ctx_ref[seg, :, c0 : c0 + 128] += lax.fori_loop(0, n_k, weigh, jnp.zeros((1, 128), F32))

    @pl.when(bound_s[0, 5] > 0)
    def _():
        @pl.loop(0, slots + 1)
        def _(seg):
            start = bound_s[seg, 0]
            end = bound_s[seg, 1]
            first = (start // 16) * 16

            @pl.when((end - jnp.minimum(first, length - WIN) > WIN) & ((seg < slots) | (end > LONG)))
            def _():
                @pl.when(end - first <= 256)
                def _():
                    long(seg, start, end, 256)

                @pl.when((end - first > 256) & (end - first <= 512))
                def _():
                    long(seg, start, end, 512)

                @pl.when(end - first > 512)
                def _():
                    longest(seg, start, end)


def exchange_kernel(
    dp, mp, q_ref, k_ref, v_ref, ctx_ref, tok_ref, bound_ref, meta_ref, target_ref, mass_ref, wo_hbm, cent_hbm,
    docs_ref, rows_ref, writes_ref, keep_ref,
    bound_s, ctx_s, part_s, carry_s, got_part, got_carry, tsend, tgot, ss_send, ss_got, csend, cgot, n_send, n_got,
    wo_ref, cent_ref, ready, late_sems, bound_sem, part_sems, carry_sems, t_sems, ss_sems, c_sems, n_sems,
):
    r = lax.axis_index("dp")
    m = lax.axis_index("mp")
    slots = 32
    cents, width = cent_ref.shape
    load_wo = pltpu.make_async_copy(wo_hbm, wo_ref, late_sems.at[0])
    load_cent = pltpu.make_async_copy(cent_hbm, cent_ref, late_sems.at[1])
    load_wo.start()
    load_cent.start()
    to_scalars = pltpu.make_async_copy(bound_ref, bound_s, bound_sem)
    to_scalars.start()

    barrier = pltpu.get_barrier_semaphore()
    nxt = lax.rem(r + 1, dp)
    prv = lax.rem(r + dp - 1, dp)
    plane = 8
    layers = dp // plane
    mine = lax.rem(r, plane)

    def along_z(i):
        return lax.rem(r + i * plane, dp)

    for dm in range(1, mp):
        pl.semaphore_signal(barrier, inc=1, device_id=(r, lax.rem(m + dm, mp)), device_id_type=MESH)
    for mm in range(mp):
        pl.semaphore_signal(barrier, inc=1, device_id=(nxt, mm), device_id_type=MESH)
    for i in range(1, layers):
        pl.semaphore_signal(barrier, inc=1, device_id=(along_z(i), m), device_id_type=MESH)
    for i in range(1, plane):
        peer = r - mine + lax.rem(mine + i, plane)
        pl.semaphore_signal(barrier, inc=1, device_id=(peer, m), device_id_type=MESH)

    tsend[...] = target_ref[...].reshape(dp, 1, 128)
    tgot[0] = tsend[0]
    ctx_s[slots + 1 :] = jnp.zeros((SEGS - slots - 1, 1, width), F32)
    to_scalars.wait()
    krow = iota((WIN, 1), 0)
    qlane = iota((1, 2 * WIN), 1) & (WIN - 1)

    def short(seg):
        block = bound_s[seg, 2]
        low = bound_s[seg, 3]
        high = bound_s[seg, 4]
        bias = jnp.where((krow >= low) & (krow < high), 0.0, -1e30)
        valid = (qlane >= low) & (qlane < high)
        q = jnp.concatenate([q_ref[block + i] for i in range(WIN // 16)], axis=0)
        k = jnp.concatenate([k_ref[block + i] for i in range(WIN // 16)], axis=0)
        v = jnp.concatenate([v_ref[block + i] for i in range(WIN // 16)], axis=0)
        for pair in range(width // 128):
            c0 = pair * 128
            q2 = jnp.concatenate([q[:, c0 : c0 + 128], q[:, width + c0 : width + c0 + 128]], axis=0)
            ctx_s[seg, :, c0 : c0 + 128] = ctx_ref[seg, :, c0 : c0 + 128] + block_sums(
                k[:, c0 : c0 + 128], q2, v[:, c0 : c0 + 128], bias, valid
            )

    def to_peer(src, dst, sems, dm):
        mm = lax.rem(m + dm, mp)
        return pltpu.make_async_remote_copy(
            src_ref=src, dst_ref=dst, send_sem=sems.at[0], recv_sem=sems.at[1],
            device_id=(r, mm), device_id_type=MESH,
        )

    def far_first(i):
        def order(k):
            odd = k % 2
            return 4 - odd * ((k + 1) // 2) + (1 - odd) * (k // 2)

        return order(i // 8) * 8 + order(i % 8)

    def wait_all(buffer, sem):
        pltpu.make_async_copy(buffer, buffer, sem).wait()

    def out_project(rows):
        high, low = halves(rows)
        return jnp.dot(high, wo_ref[...], preferred_element_type=F32) + jnp.dot(
            low, wo_ref[...], preferred_element_type=F32
        )

    @pl.loop(0, slots // GROUP)
    def _(group):
        for j in range(GROUP):
            short(group * GROUP + j)

    ctx_s[slots] = ctx_ref[slots]
    load_wo.wait()
    projected = out_project(ctx_s[...].reshape(SEGS, width))
    row8 = iota((8, width), 0)
    carried_count = meta_ref[8 + slots : 9 + slots, 0:1]
    for mm in range(mp):
        block = projected[:, mm * width : (mm + 1) * width] + jnp.where(m == mm, tok_ref[...], 0.0)
        part_s[mm] = block[:slots]
        carry_s[mm] = jnp.where(row8 == 1, carried_count, block[slots:])

    pl.semaphore_wait(barrier, mp - 1 + mp + layers - 1 + plane - 1)
    for mm in range(mp):
        pltpu.make_async_remote_copy(
            src_ref=carry_s.at[mm], dst_ref=got_carry.at[m], send_sem=carry_sems.at[0],
            recv_sem=carry_sems.at[1], device_id=(prv, mm), device_id_type=MESH,
        ).start()
    for dm in range(1, mp):
        to_peer(part_s.at[lax.rem(m + dm, mp)], got_part.at[mp - 1 - dm], part_sems, dm).start()

    for i in range(1, layers):
        pl.semaphore_signal(ready, inc=1, device_id=(along_z(i), m), device_id_type=MESH)

    d_wide = meta_ref[0:1, :]
    rank_wide = meta_ref[1:2, :]
    row = iota((8 * dp, 128), 0)
    col = iota((8 * dp, 128), 1)
    j = row & 7
    pick = (
        ((row >> 3).astype(F32) == d_wide)
        & ((j >> 1).astype(F32) == rank_wide)
        & ((j & 1) == ((col >> 5) & 1))
    )
    pick = jnp.where(pick, 1.0, 0.0).astype(BF16)

    wait_all(got_carry, carry_sems.at[1])
    carry = got_carry[0]
    for i in range(1, mp):
        carry = carry + got_carry[i]
    count_in = got_carry[0][1:2, :]
    counts = meta_ref[8 : 8 + slots, 0:1]
    picks = meta_ref[8 : 8 + slots, 64:65]
    sums = part_s[m] + picks * carry[0:1, :]
    inverse = 1.0 / jnp.maximum(counts + picks * count_in, 1.0)
    wait_all(got_part, part_sems.at[1])
    for i in range(mp - 1):
        sums = sums + got_part[i]
    averages = sums * inverse
    squares = jnp.sum(averages * averages, axis=1, keepdims=True)
    square_row = to_row(squares, slots, 128)
    ss_send[...] = jnp.broadcast_to(square_row, (8, 128))
    for dm in range(1, mp):
        to_peer(ss_send, ss_got.at[mp - 1 - dm], ss_sems, dm).start()
    pl.semaphore_wait(ready, layers - 1)

    @pl.loop(1, dp)
    def _(d):
        pltpu.make_async_remote_copy(
            src_ref=tsend.at[d], dst_ref=tgot.at[dp - d], send_sem=t_sems.at[0], recv_sem=t_sems.at[1],
            device_id=(lax.rem(r + d, dp), m), device_id_type=MESH,
        ).start()

    wait_all(ss_got, ss_sems.at[1])
    for i in range(mp - 1):
        square_row = square_row + ss_got[i][0:1, :]
    eye = iota((slots, 128), 0) == iota((slots, 128), 1)
    squares = jnp.sum(jnp.where(eye, square_row, 0.0), axis=1, keepdims=True)
    vectors = averages * lax.rsqrt(squares * (1.0 / D) + 1e-06)

    high, low = halves(vectors)
    high, low = high.astype(F32), low.astype(F32)
    stacked = jnp.concatenate([high[:, :128], high[:, 128:], low[:, :128], low[:, 128:]], axis=0).astype(BF16)
    outgoing = jnp.dot(pick, stacked, preferred_element_type=F32).reshape(dp, 8, 128)
    csend[...] = outgoing[:, :4, :]
    cgot[0] = csend[0]

    @pl.loop(0, dp - 1)
    def _(i):
        d = far_first(i)
        pltpu.make_async_remote_copy(
            src_ref=csend.at[d], dst_ref=cgot.at[dp - d], send_sem=c_sems.at[0], recv_sem=c_sems.at[1],
            device_id=(lax.rem(r + d, dp), m), device_id_type=MESH,
        ).start()

    docs_ref[...] = vectors

    rest = pl.ds(1, dp - 1)
    wait_all(tgot.at[rest], t_sems.at[1])
    tgt_row = jnp.sum(tgot[...], axis=0)
    tgt_col = to_column(tgt_row, 128)
    hits = jnp.where(iota((128, cents), 1).astype(F32) == tgt_col - 1.0, 1.0, 0.0)
    mass = jnp.sum(hits * mass_ref[...], axis=1, keepdims=True)
    hits = hits.astype(BF16)
    load_cent.wait()
    cent_high, cent_low = halves(cent_ref[...])
    picked = jnp.dot(hits, cent_high, preferred_element_type=F32) + jnp.dot(
        hits, cent_low, preferred_element_type=F32
    )
    start = mass * picked
    together = jnp.where((tgt_col == tgt_row) & (tgt_row > 0.0), 1.0, 0.0).astype(BF16)
    earlier = iota((128, 128), 0) < iota((128, 128), 1)
    repeats = jnp.sum(jnp.where(earlier & (tgt_col == tgt_row), 1.0, 0.0), axis=0, keepdims=True)
    wanted = jnp.where(repeats == 0.0, tgt_row - 1.0, -1.0)
    writes = jnp.where(iota((cents, 128), 0).astype(F32) == wanted, 1.0, 0.0)
    keep_ref[...] = jnp.where(jnp.sum(writes, axis=1, keepdims=True) > 0.0, 0.0, cent_ref[...])
    writes_ref[...] = writes.astype(BF16)

    wait_all(cgot.at[rest], c_sems.at[1])
    arrived = jnp.concatenate(
        [jnp.concatenate([cgot[:, 2 * k, :], cgot[:, 2 * k + 1, :]], axis=1) for k in range(2)], axis=0
    )
    high, low = halves(arrived)
    blended = start + (
        jnp.dot(together, high, preferred_element_type=F32) + jnp.dot(together, low, preferred_element_type=F32)
    )
    norm_row = to_row(jnp.sum(blended * blended, axis=1, keepdims=True), 128, 128)
    n_send[...] = jnp.broadcast_to(norm_row, (8, 128))
    for dm in range(1, mp):
        to_peer(n_send, n_got.at[mp - 1 - dm], n_sems, dm).start()
    wait_all(n_got, n_sems.at[1])
    for i in range(mp - 1):
        norm_row = norm_row + n_got[i][0:1, :]
    norms = to_column(norm_row, 128)
    rows_ref[...] = blended * lax.rsqrt(norms * (1.0 / D) + 1e-06)

    wait_all(got_part, part_sems.at[0])
    wait_all(carry_s, carry_sems.at[0])
    wait_all(tsend.at[rest], t_sems.at[0])
    wait_all(ss_got, ss_sems.at[0])
    wait_all(csend.at[rest], c_sems.at[0])
    wait_all(n_got, n_sems.at[0])


def write_kernel(docs_ref, rows_ref, writes_ref, keep_ref, docs_hbm, out_hbm, out_v, sems):
    parts = 4
    block = keep_ref.shape[0] // parts
    docs_copy = pltpu.make_async_copy(docs_ref, docs_hbm, sems.at[parts])
    docs_copy.start()
    high, low = halves(rows_ref[...])
    copies = []
    for i in range(parts):
        rows = pl.ds(i * block, block)
        writes = writes_ref[rows, :]
        out_v[rows, :] = (
            keep_ref[rows, :]
            + jnp.dot(writes, high, preferred_element_type=F32)
            + jnp.dot(writes, low, preferred_element_type=F32)
        )
        copies.append(pltpu.make_async_copy(out_v.at[rows], out_hbm.at[rows], sems.at[i]))
        copies[-1].start()
    docs_copy.wait()
    for copy in copies:
        copy.wait()


def shards(
    tokens, doc_ids, ln_gain, w_query, w_key, w_value, w_out, centroids, cluster_mass, assigned
):
    length = tokens.shape[0]
    width = w_out.shape[0]
    slots = assigned.shape[0]
    cents = centroids.shape[0]
    dp, mp = lax.axis_size("dp"), lax.axis_size("mp")

    def shape(*dims, dtype=F32):
        return jax.ShapeDtypeStruct(dims, dtype)

    vmem = pl.BlockSpec(memory_space=pltpu.VMEM)
    held = pl.pallas_call(
        rows_kernel,
        in_specs=[pl.BlockSpec(memory_space=pltpu.HBM)] * 7,
        out_specs=[vmem] * 8,
        out_shape=[
            shape(length // 16, 16, 2 * width, dtype=BF16),
            shape(length // 16, 16, width, dtype=BF16),
            shape(length // 16, 16, width, dtype=BF16),
            shape(SEGS, 1, width),
            shape(SEGS, width),
            shape(SEGS, 128, dtype=jnp.int32),
            shape(8 + SEGS, 128),
            shape(dp, 128),
        ],
        scratch_shapes=[
            pltpu.VMEM((1, length), jnp.int32),
            pltpu.VMEM((1, slots), jnp.int32),
            pltpu.VMEM((1, D), F32),
            pltpu.VMEM((length, D), BF16),
            pltpu.VMEM((D, 3 * width), BF16),
            pltpu.VMEM((length, D), BF16),
            pltpu.SMEM((SEGS, 128), jnp.int32),
            pltpu.VMEM((length + LONG, 2 * WIN), F32),
            pltpu.SemaphoreType.DMA((6,)),
            pltpu.SemaphoreType.DMA((4,)),
            pltpu.SemaphoreType.DMA,
        ],
        compiler_params=pltpu.CompilerParams(vmem_limit_bytes=40 << 20),
        name="rows",
    )(
        *[pltpu.with_memory_space_constraint(x, pltpu.HBM) for x in (
            doc_ids.reshape(1, length), assigned.reshape(1, slots), ln_gain.reshape(1, D), tokens,
            w_query, w_key, w_value)]
    )

    pair = pltpu.SemaphoreType.DMA((2,))
    new = pl.pallas_call(
        functools.partial(exchange_kernel, dp, mp),
        in_specs=[vmem] * 9 + [pl.BlockSpec(memory_space=pl.ANY)] * 2,
        out_specs=[vmem] * 4,
        out_shape=[
            shape(slots, width),
            shape(128, width),
            shape(cents, 128, dtype=BF16),
            shape(cents, width),
        ],
        scratch_shapes=[
            pltpu.SMEM((SEGS, 128), jnp.int32),
            pltpu.VMEM((SEGS, 1, width), F32),
            pltpu.VMEM((mp, slots, width), F32),
            pltpu.VMEM((mp, 8, width), F32),
            pltpu.VMEM((mp - 1, slots, width), F32),
            pltpu.VMEM((mp, 8, width), F32),
            pltpu.VMEM((dp, 1, 128), F32),
            pltpu.VMEM((dp, 1, 128), F32),
            pltpu.VMEM((8, 128), F32),
            pltpu.VMEM((mp - 1, 8, 128), F32),
            pltpu.VMEM((dp, 4, 128), F32),
            pltpu.VMEM((dp, 4, 128), F32),
            pltpu.VMEM((8, 128), F32),
            pltpu.VMEM((mp - 1, 8, 128), F32),
            pltpu.VMEM((width, D), BF16),
            pltpu.VMEM((cents, width), F32),
            pltpu.SemaphoreType.REGULAR,
            pltpu.SemaphoreType.DMA((2,)),
            pltpu.SemaphoreType.DMA,
            pair, pair, pair, pair, pair, pair,
        ],
        compiler_params=pltpu.CompilerParams(
            collective_id=0, has_side_effects=True, vmem_limit_bytes=24 << 20
        ),
        name="exchange",
    )(*held, cluster_mass.reshape(1, cents),
        *[pltpu.with_memory_space_constraint(x, pltpu.HBM) for x in (w_out, centroids)])

    anywhere = pl.BlockSpec(memory_space=pl.ANY)
    return pl.pallas_call(
        write_kernel,
        in_specs=[vmem] * 4,
        out_specs=[anywhere] * 2,
        out_shape=[shape(slots, width), shape(cents, width)],
        scratch_shapes=[pltpu.VMEM((cents, width), F32), pltpu.SemaphoreType.DMA((5,))],
        compiler_params=pltpu.CompilerParams(vmem_limit_bytes=16 << 20),
        name="write",
    )(*new)


def solution(mesh):
    placed = (
        P("dp", None),
        P("dp"),
        P(),
        P(None, "mp"),
        P(None, "mp"),
        P(None, "mp"),
        P("mp", None),
        P("dp", "mp"),
        P("dp"),
        P("dp"),
    )
    return jax.shard_map(
        shards,
        mesh=mesh,
        in_specs=placed,
        out_specs=(P("dp", "mp"), P("dp", "mp")),
        check_vma=False,
    )
```
